32 devices in a mesh: obj: 4 (over y, core), scan: 8 (over z, x).
Axes of the slice: x: 2, y: 2, z: 4, core: 2. Of those that a mesh axis runs over, the one named last changes fastest.
Arguments:
- object_slab: float32 [2, 2, 1536, 4096], P(None, None, 'obj', 'scan'), may hold values from -4 to 4
- probe_mode_stack: float32 [6, 2, 256, 256], replicated, may hold values from -2 to 2
- offsets: int32 [96, 2], P(('obj', 'scan')), may hold values from 0 to 3840, as said below
- measured: float32 [96, 256, 256], P(('obj', 'scan')), may hold values from 0.05 to 3
- counts: int32 [32], P(('obj', 'scan')), may hold values from 1 to 3, as said below
Outputs:
- new_object: float32 [2, 2, 1536, 4096], P(None, None, 'obj', 'scan')
- new_probe: float32 [6, 2, 256, 256], replicated
The draws below stay inside these ranges and needn't reach their ends.
Inputs may be any that keep to these rules, and one draw needn't show every extreme that they name: `offsets`: rows 3 d to 3 d + 2 belong to device d (devices in the order obj, then scan). Each row gives the object row and column of a patch's top-left pixel; that pixel lies in the device's own tile of 384 x 512 pixels, and the whole 256 x 256 patch lies inside the object. Device d uses its first counts[d] position slots; the others are ignored.
All inputs are finite; a program needn't handle non-finite values.
Results may differ from the reference program's by a relative error of at most 0.008.
The reference program's roundings to bfloat16 on the way count: a program that leaves them out, or rounds other values in their place, can miss the bound.
Values sent between devices are 32-bit elements; how exact they have to be, the bound alone decides.
A program may use at most 128 MiB of HBM per device.

```python
import math
import jax
import jax.numpy as jnp
from jax import lax

P_SIZE = 256
M = 6
SL = 2
TH = 384
TW = 512
CAP = 3
OH = 1536
OW = 4096
POSITIONS = 96
DEVICES = 32


def draw_offsets(key, part):
    row_ids = jnp.arange(CAP * DEVICES, dtype=jnp.int32)
    device = row_ids // CAP
    tiles_across = OW // TW
    tile_row = device // tiles_across
    tile_col = device % tiles_across
    lowest_row = tile_row * TH
    highest_row = jnp.minimum(lowest_row + TH, OH - P_SIZE + 1)
    lowest_col = tile_col * TW
    highest_col = jnp.minimum(lowest_col + TW, OW - P_SIZE + 1)
    key_rows, key_cols = jax.random.split(key)
    row_value = jax.random.randint(key_rows, row_ids.shape, lowest_row, highest_row)
    col_value = jax.random.randint(key_cols, row_ids.shape, lowest_col, highest_col)
    last_slot = CAP * (DEVICES - 1)
    row_value = row_value.at[0].set(0).at[last_slot].set(OH - P_SIZE)
    col_value = col_value.at[0].set(0).at[last_slot].set(OW - P_SIZE)
    return jnp.stack([row_value, col_value], axis=1).astype(jnp.int32)


def draw_counts(key, part):
    key_ticket, key_chosen = jax.random.split(key)
    ticket = jax.random.randint(key_ticket, (DEVICES,), 0, 20)
    used_slots = jnp.where(ticket < 12, 1, jnp.where(ticket < 15, 2, CAP))
    used_slots = jnp.minimum(used_slots, CAP)
    chosen = jax.random.randint(key_chosen, (), 0, DEVICES)
    used_slots = used_slots.at[chosen].set(CAP)
    return used_slots.astype(jnp.int32)


def level_of(key, shape, cuts, smallest, top_value):
    def one(axis_at, shards_of):
        steps = jax.random.uniform(jax.random.fold_in(jax.random.fold_in(key, 6), axis_at), (shards_of,), jnp.float32, smallest / len(cuts), top_value / len(cuts))
        return jnp.repeat(jnp.exp(steps), shape[axis_at] // shards_of).reshape((-1,) + (1,) * (len(shape) - axis_at - 1))

    level = one(*cuts[0])
    for cut in cuts[1:]:
        level = level * one(*cut)
    return level


def bell_draw(stream_key, dims, scale, most, cuts=(), kind=jnp.bfloat16):
    level = level_of(stream_key, dims, cuts, -0.22, 0.18) if cuts else 1.0
    array = jax.random.normal(stream_key, dims, jnp.float32) * scale * level
    return jnp.minimum(jnp.maximum(array, -most), most).astype(kind)


def setup_inputs(seed: int = 0) -> dict:
    seeds = jax.random.split(jax.random.key(seed), 6)
    return {
        "object_slab": bell_draw(seeds[0], (SL, 2, OH, OW), 0.7, 4.0, ((2, 4), (3, 8)), jnp.float32),
        "probe_mode_stack": bell_draw(seeds[1], (M, 2, P_SIZE, P_SIZE), 0.3, 2.0, (), jnp.float32),
        "offsets": draw_offsets(jax.random.fold_in(seeds[5], 71), 0),
        "measured": jnp.clip(jnp.exp(math.log(3.0) - 4.0943445 * jax.random.uniform(seeds[3], (POSITIONS, P_SIZE, P_SIZE), jnp.float32) ** level_of(seeds[3], (POSITIONS, P_SIZE, P_SIZE), ((0, 32),), -0.2, 0.2)), 0.05, 3.0),
        "counts": draw_counts(jax.random.fold_in(seeds[5], 71), 0),
    }


chirp_scale = 24.0
probe_step = 0.15

def dft_table(pattern, sign_factor):
    indices = jnp.arange(pattern, dtype=jnp.int32)
    phases = indices[:, None] * indices[None, :] % pattern
    angles = phases.astype(jnp.float32) * (2.0 * math.pi / pattern)
    normalizer = 1.0 / math.sqrt(pattern)
    real_part = jnp.cos(angles) * normalizer
    imag_part = sign_factor * jnp.sin(angles) * normalizer
    row_real = jnp.stack([real_part, -imag_part], axis=1)
    row_imag = jnp.stack([imag_part, real_part], axis=1)
    return jnp.stack([row_real, row_imag], axis=0).astype(jnp.bfloat16)

def propagator(pattern):
    indices = jnp.arange(pattern, dtype=jnp.int32)
    freqs = ((indices + pattern // 2) % pattern - pattern // 2).astype(jnp.float32) / pattern
    phases = -math.pi * chirp_scale * (freqs[:, None] ** 2 + freqs[None, :] ** 2)
    return jnp.stack([jnp.cos(phases), jnp.sin(phases)], axis=0)

def transform(field_in, tables):
    half_done = jnp.einsum('dkcy,mcyx->mdkx', tables.astype(jnp.float32), field_in.astype(jnp.float32))
    half_done = half_done.astype(jnp.bfloat16)
    return jnp.einsum('mcyx,dkcx->mdyk', half_done.astype(jnp.float32), tables.astype(jnp.float32))

def complex_times(left_arr, right_arr):
    left_real, left_imag = (left_arr[..., 0, :, :], left_arr[..., 1, :, :])
    right_real, right_imag = (right_arr[..., 0, :, :], right_arr[..., 1, :, :])
    return jnp.stack([left_real * right_real - left_imag * right_imag, left_real * right_imag + left_imag * right_real], axis=-3)

def conjugate(values):
    return jnp.stack([values[..., 0, :, :], -values[..., 1, :, :]], axis=-3)

def position_updates(object_window, probe_mode_stack, measured_pattern, propagate_forward, propagate_backward, fresnel_kernel):
    layers = object_window.shape[0]
    wavefield = probe_mode_stack
    inputs = []
    exit_wave = wavefield
    for layer_index in range(layers):
        inputs.append(wavefield)
        exit_wave = complex_times(object_window[layer_index], wavefield)
        if layer_index < layers - 1:
            spectrum = transform(exit_wave.astype(jnp.bfloat16), propagate_forward)
            wavefield = transform(complex_times(fresnel_kernel, spectrum).astype(jnp.bfloat16), propagate_backward)
    detector_wavefront = transform(exit_wave.astype(jnp.bfloat16), propagate_forward)
    modal_intensity = lax.optimization_barrier(jnp.sum(detector_wavefront[:, 0] ** 2 + detector_wavefront[:, 1] ** 2, axis=0))
    amplitude_residual = ((modal_intensity - measured_pattern)[None, None] * detector_wavefront).astype(jnp.bfloat16)
    gradient = transform(amplitude_residual, propagate_backward)
    pieces = [None] * layers
    for layer_index in reversed(range(layers)):
        if layer_index < layers - 1:
            spectrum = transform(gradient.astype(jnp.bfloat16), propagate_forward)
            gradient = transform(complex_times(conjugate(fresnel_kernel), spectrum).astype(jnp.bfloat16), propagate_backward)
        pieces[layer_index] = lax.optimization_barrier(jnp.sum(complex_times(conjugate(inputs[layer_index]), gradient), axis=0))
        gradient = complex_times(conjugate(object_window[layer_index]), gradient)
    return (jnp.stack(pieces, axis=0), gradient)

def reference(object_slab, probe_mode_stack, offsets, measured, counts):
    layers = object_slab.shape[0]
    propagate_forward = dft_table(P_SIZE, -1.0)
    propagate_backward = dft_table(P_SIZE, 1.0)
    fresnel_kernel = propagator(P_SIZE)
    lamp_power = lax.optimization_barrier(jnp.sum(probe_mode_stack[:, 0] ** 2 + probe_mode_stack[:, 1] ** 2, axis=0))
    row_ids = jnp.arange(POSITIONS, dtype=jnp.int32)
    is_used = row_ids % CAP < counts[row_ids // CAP]
    zero_index = jnp.int32(0)

    def visit_slot(state_now, current_entry):
        scan_offset, measured_pattern, visited_marker = current_entry

        def active(inner_state):
            grad_object, illumination, grad_probe = inner_state
            corner_at = (zero_index, zero_index, scan_offset[0].astype(jnp.int32), scan_offset[1].astype(jnp.int32))
            object_window = lax.dynamic_slice(object_slab, corner_at, (layers, 2, P_SIZE, P_SIZE))
            object_update, probe_update = position_updates(object_window, probe_mode_stack, measured_pattern, propagate_forward, propagate_backward, fresnel_kernel)
            previous = lax.dynamic_slice(grad_object, corner_at, (layers, 2, P_SIZE, P_SIZE))
            grad_object = lax.dynamic_update_slice(grad_object, previous + object_update, corner_at)
            light_at = (scan_offset[0].astype(jnp.int32), scan_offset[1].astype(jnp.int32))
            previous_light = lax.dynamic_slice(illumination, light_at, (P_SIZE, P_SIZE))
            illumination = lax.dynamic_update_slice(illumination, previous_light + lamp_power, light_at)
            return (grad_object, illumination, grad_probe + probe_update)
        return (lax.cond(visited_marker, active, lambda inner_state: inner_state, state_now), None)
    start_state = (jnp.zeros(object_slab.shape, jnp.float32), jnp.zeros(object_slab.shape[2:], jnp.float32), jnp.zeros(probe_mode_stack.shape, jnp.float32))
    final_state, _ = lax.scan(visit_slot, start_state, (offsets, measured, is_used))
    grad_object, illumination, grad_probe = final_state
    new_object = object_slab - grad_object / (illumination + 1.0)
    grad_scale = jnp.sqrt(jnp.mean(grad_probe * grad_probe) + 1e-06)
    new_probe = probe_mode_stack - probe_step * grad_probe / grad_scale
    return (new_object, new_probe)
```

```python
import functools
import math

import jax
import jax.numpy as jnp
import numpy as np
from jax import lax
from jax.experimental import pallas as pl
from jax.experimental.pallas import tpu as pltpu
from jax.sharding import PartitionSpec as P

chirp_scale = 24.0
probe_step = 0.15
lanes = 128
sublanes = 8
vmem_bytes = 56 * 1024 * 1024


def from_behind(array, axis, by):
    count = lax.axis_size(axis)
    pairs = [(i, i + by) for i in range(count) if 0 <= i + by < count]
    return lax.ppermute(array, axis, pairs)


def dft_parts(pattern):
    indices = np.arange(pattern)
    angles = (indices[:, None] * indices[None, :] % pattern) * (2.0 * math.pi / pattern)
    parts = (np.cos(angles) / math.sqrt(pattern), np.sin(angles) / math.sqrt(pattern))
    return [part.astype(np.float32).astype(jnp.bfloat16).astype(np.float64) for part in parts]


def block_matrix(real_part, imag_part):
    upper = np.concatenate([real_part, -imag_part], axis=1)
    lower = np.concatenate([imag_part, real_part], axis=1)
    return jnp.asarray(np.concatenate([upper, lower], axis=0).astype(np.float32), jnp.bfloat16)


def tables(pattern):
    cos, sin = dft_parts(pattern)
    indices = np.arange(pattern)
    freqs = ((indices + pattern // 2) % pattern - pattern // 2) / pattern
    chirp = np.exp(-1j * math.pi * chirp_scale * freqs**2)
    hop = (cos + 1j * sin) @ (chirp[:, None] * (cos - 1j * sin))
    return (
        block_matrix(cos, -sin), block_matrix(cos, sin),
        block_matrix(hop.real, hop.imag), block_matrix(hop.real, -hop.imag),
    )


def aligned(row, col):
    row_base = pl.multiple_of(row // sublanes * sublanes, sublanes)
    col_base = pl.multiple_of(col // lanes * lanes, lanes)
    return row_base, col_base, row - row_base, col - col_base


def pad(array):
    array = jnp.concatenate([array, jnp.zeros((array.shape[0], lanes), jnp.float32)], axis=1)
    return jnp.concatenate([array, jnp.zeros((sublanes, array.shape[1]), jnp.float32)], axis=0)


def roll_down(array, rows, cols):
    return pltpu.roll(pltpu.roll(array, cols, 1), rows, 0)


def transform(real_part, imag_part, left, right):
    pattern = real_part.shape[0]
    stacked = jnp.concatenate([real_part.astype(jnp.bfloat16), imag_part.astype(jnp.bfloat16)], axis=0)
    half = jnp.dot(left, stacked, preferred_element_type=jnp.float32).astype(jnp.bfloat16)
    half = jnp.concatenate([half[:pattern], half[pattern:]], axis=1)
    full = jnp.dot(half, right, preferred_element_type=jnp.float32)
    return full[:, :pattern], full[:, pattern:]


def slots_kernel(
    corners, used, tile, right, lower, corner, probe, measured, table_f, table_b, hop_f, hop_b,
    grad_tile, grad_right, grad_lower, grad_corner, grad_probe,
    ext, grad, window, waves, far, back, intensity, term, sems_in, sems_out,
):
    modes, _, pattern, _ = probe.shape
    layers = tile.shape[0]
    height, width = tile.shape[2], tile.shape[3]
    wide = pattern + lanes
    tall = pattern + sublanes

    def spots(buffer):
        return (
            buffer.at[:, :, pl.ds(0, height), pl.ds(0, width)],
            buffer.at[:, :, pl.ds(0, height), pl.ds(width, pattern)],
            buffer.at[:, :, pl.ds(height, pattern), pl.ds(0, width)],
            buffer.at[:, :, pl.ds(height, pattern), pl.ds(width, pattern)],
        )

    loads = [
        pltpu.make_async_copy(source, spot, sems_in.at[k])
        for k, (source, spot) in enumerate(zip((tile, right, lower, corner), spots(ext)))
    ]
    for load in loads:
        load.start()
    grad[...] = jnp.zeros_like(grad)
    grad_probe[...] = jnp.zeros_like(grad_probe)
    for load in loads:
        load.wait()

    @pl.loop(0, used[0])
    def _(slot):
        row = corners[slot, 0]
        col = corners[slot, 1]
        row_base, col_base, row_shift, col_shift = aligned(row, col)
        row_back = jnp.where(row_shift == 0, 0, tall - row_shift)
        col_back = jnp.where(col_shift == 0, 0, wide - col_shift)
        for layer in range(layers):
            for part in range(2):
                block = ext[layer, part, pl.ds(row_base, tall), pl.ds(col_base, wide)]
                window[layer, part] = roll_down(block, row_back, col_back)[:pattern, :pattern]
        intensity[...] = jnp.zeros_like(intensity)
        term[...] = jnp.zeros_like(term)

        for layer in range(layers):

            @pl.loop(0, modes, unroll=3)
            def _(mode, layer=layer):
                last = layer == layers - 1
                if layer == 0:
                    wr, wi = probe[mode, 0], probe[mode, 1]
                else:
                    wr, wi = waves[layer - 1, mode, 0], waves[layer - 1, mode, 1]
                o_r, o_i = window[layer, 0], window[layer, 1]
                tables = (table_f, table_b) if last else (hop_f, hop_b)
                fr, fi = transform(o_r * wr - o_i * wi, o_r * wi + o_i * wr, tables[0][...], tables[1][...])
                if last:
                    far[mode, 0] = fr
                    far[mode, 1] = fi
                    intensity[...] += fr * fr + fi * fi
                else:
                    waves[layer, mode, 0] = fr
                    waves[layer, mode, 1] = fi

        intensity[...] = intensity[...] - measured[slot]

        for layer in reversed(range(layers)):

            @pl.loop(0, modes, unroll=3)
            def _(mode, layer=layer):
                if layer == layers - 1:
                    gain = intensity[...]
                    gr, gi = transform(gain * far[mode, 0], gain * far[mode, 1], table_b[...], table_f[...])
                else:
                    gr, gi = transform(back[mode, 0], back[mode, 1], hop_b[...], hop_f[...])
                if layer == 0:
                    wr, wi = probe[mode, 0], probe[mode, 1]
                else:
                    wr, wi = waves[layer - 1, mode, 0], waves[layer - 1, mode, 1]
                term[layer, 0] += wr * gr + wi * gi
                term[layer, 1] += wr * gi - wi * gr
                o_r, o_i = window[layer, 0], window[layer, 1]
                gr, gi = o_r * gr + o_i * gi, o_r * gi - o_i * gr
                if layer == 0:
                    grad_probe[mode, 0] += gr
                    grad_probe[mode, 1] += gi
                else:
                    back[mode, 0] = gr.astype(jnp.bfloat16)
                    back[mode, 1] = gi.astype(jnp.bfloat16)

        for layer in range(layers):
            for part in range(2):
                at = (layer, part, pl.ds(row_base, tall), pl.ds(col_base, wide))
                grad[at] = grad[at] + roll_down(pad(term[layer, part]), row_shift, col_shift)

    saves = [
        pltpu.make_async_copy(spot, target, sems_out.at[k])
        for k, (spot, target) in enumerate(
            zip(spots(grad), (grad_tile, grad_right, grad_lower, grad_corner))
        )
    ]
    for save in saves:
        save.start()
    for save in saves:
        save.wait()


def run_slots(corners, used, tile, right, lower, corner, probe, measured, table_f, table_b, hop_f, hop_b):
    layers, _, height, width = tile.shape
    modes, _, pattern, _ = probe.shape
    smem = pl.BlockSpec(memory_space=pltpu.SMEM)
    vmem = pl.BlockSpec(memory_space=pltpu.VMEM)
    anyw = pl.BlockSpec(memory_space=pl.ANY)
    f32 = jnp.float32
    ext_shape = (layers, 2, height + pattern, width + pattern)
    return pl.pallas_call(
        slots_kernel,
        out_shape=(
            jax.ShapeDtypeStruct(tile.shape, f32),
            jax.ShapeDtypeStruct(right.shape, f32),
            jax.ShapeDtypeStruct(lower.shape, f32),
            jax.ShapeDtypeStruct(corner.shape, f32),
            jax.ShapeDtypeStruct(probe.shape, f32),
        ),
        in_specs=[smem, smem, anyw, anyw, anyw, anyw, vmem, vmem, vmem, vmem, vmem, vmem],
        out_specs=(anyw, anyw, anyw, anyw, vmem),
        scratch_shapes=[
            pltpu.VMEM(ext_shape, f32),
            pltpu.VMEM(ext_shape, f32),
            pltpu.VMEM((layers, 2, pattern, pattern), f32),
            pltpu.VMEM((layers - 1, modes, 2, pattern, pattern), f32),
            pltpu.VMEM((modes, 2, pattern, pattern), f32),
            pltpu.VMEM((modes, 2, pattern, pattern), jnp.bfloat16),
            pltpu.VMEM((pattern, pattern), f32),
            pltpu.VMEM((layers, 2, pattern, pattern), f32),
            pltpu.SemaphoreType.DMA((4,)),
            pltpu.SemaphoreType.DMA((4,)),
        ],
        compiler_params=pltpu.CompilerParams(vmem_limit_bytes=vmem_bytes),
        cost_estimate=pl.CostEstimate(flops=29_000_000_000, bytes_accessed=30_000_000, transcendentals=0),
    )(corners, used, tile, right, lower, corner, probe, measured, table_f, table_b, hop_f, hop_b)


def light_kernel(height, width, slots, info, probe, light, canvas, power):
    modes, _, pattern, _ = probe.shape
    total = jnp.zeros((pattern, pattern), jnp.float32)
    for mode in range(modes):
        total = total + (probe[mode, 0] * probe[mode, 0] + probe[mode, 1] * probe[mode, 1])
    power[...] = pad(total)
    canvas[...] = jnp.zeros_like(canvas)
    for block in range(4):
        base = block * (2 * slots + 1)

        @pl.loop(0, info[base + 2 * slots])
        def _(slot):
            row = info[base + 2 * slot] + height
            col = info[base + 2 * slot + 1] + width
            row_base, col_base, row_shift, col_shift = aligned(row, col)
            at = (pl.ds(row_base, pattern + sublanes), pl.ds(col_base, pattern + lanes))
            canvas[at] = canvas[at] + roll_down(power[...], row_shift, col_shift)

    light[...] = canvas[height : 2 * height, width : 2 * width] + 1.0


def run_light(height, width, slots, info, probe):
    pattern = probe.shape[-1]
    return pl.pallas_call(
        functools.partial(light_kernel, height, width, slots),
        out_shape=jax.ShapeDtypeStruct((height, width), jnp.float32),
        in_specs=[pl.BlockSpec(memory_space=pltpu.SMEM), pl.BlockSpec(memory_space=pltpu.VMEM)],
        out_specs=pl.BlockSpec(memory_space=pltpu.VMEM),
        scratch_shapes=[
            pltpu.VMEM((2 * height + pattern, 2 * width + pattern), jnp.float32),
            pltpu.VMEM((pattern + sublanes, pattern + lanes), jnp.float32),
        ],
        compiler_params=pltpu.CompilerParams(vmem_limit_bytes=24 * 1024 * 1024),
        cost_estimate=pl.CostEstimate(flops=10_000_000, bytes_accessed=12_000_000, transcendentals=0),
    )(info, probe)


def final_kernel(tile, grad, left, above, corner, light, out):
    pattern = left.shape[-1]
    grad[0, 0, :, :pattern] = grad[0, 0, :, :pattern] + left[0, 0]
    grad[0, 0, :pattern, :] = grad[0, 0, :pattern, :] + above[0, 0]
    grad[0, 0, :pattern, :pattern] = grad[0, 0, :pattern, :pattern] + corner[0, 0]
    out[0, 0] = tile[0, 0] - grad[0, 0] / light[...]


def run_final(tile, grad, left, above, corner, light):
    layers, parts, height, width = tile.shape
    spec = lambda array: pl.BlockSpec((1, 1) + array.shape[2:], lambda i, j: (i, j, 0, 0))
    return pl.pallas_call(
        final_kernel,
        grid=(layers, parts),
        out_shape=jax.ShapeDtypeStruct(tile.shape, jnp.float32),
        in_specs=[
            spec(tile), spec(grad), spec(left), spec(above), spec(corner),
            pl.BlockSpec(light.shape, lambda i, j: (0, 0)),
        ],
        out_specs=spec(tile),
        compiler_params=pltpu.CompilerParams(vmem_limit_bytes=24 * 1024 * 1024),
        cost_estimate=pl.CostEstimate(flops=4_000_000, bytes_accessed=14_000_000, transcendentals=0),
    )(tile, grad, left, above, corner, light)


def on_device(object_slab, probe_mode_stack, offsets, measured, counts):
    tile_height = object_slab.shape[2]
    tile_width = object_slab.shape[3]
    pattern = probe_mode_stack.shape[-1]
    slots = offsets.shape[0]
    table_f, table_b, hop_f, hop_b = tables(pattern)
    right_rim = from_behind(object_slab[:, :, :, :pattern], "scan", -1)
    lower_rim = from_behind(object_slab[:, :, :pattern, :], "obj", -1)
    corner_rim = from_behind(right_rim[:, :, :pattern, :], "obj", -1)
    base = jnp.stack([lax.axis_index("obj") * tile_height, lax.axis_index("scan") * tile_width])
    base = base.astype(jnp.int32)
    corners = offsets - base
    own_info = jnp.concatenate([offsets.reshape(-1), counts])
    left_info = from_behind(own_info, "scan", 1)
    row_info = jnp.concatenate([own_info, left_info])
    info = jnp.concatenate([row_info, from_behind(row_info, "obj", 1)])
    right_rim, lower_rim, corner_rim, corners, info = lax.optimization_barrier(
        (right_rim, lower_rim, corner_rim, corners, info)
    )
    shifts = jnp.tile(jnp.concatenate([jnp.tile(base, slots), jnp.zeros((1,), jnp.int32)]), 4)
    light = run_light(tile_height, tile_width, slots, info - shifts, probe_mode_stack)
    grad_tile, grad_right, grad_lower, grad_corner, grad_probe = run_slots(
        corners, counts, object_slab, right_rim, lower_rim, corner_rim, probe_mode_stack,
        measured, table_f, table_b, hop_f, hop_b,
    )
    summed = lax.psum(grad_probe, ("obj", "scan"))
    corner_half = from_behind(grad_corner, "obj", 1)
    from_above = from_behind(grad_lower, "obj", 1)
    from_left = from_behind(grad_right, "scan", 1)
    from_corner = from_behind(corner_half, "scan", 1)
    new_object = run_final(object_slab, grad_tile, from_left, from_above, from_corner, light)
    summed, new_object = lax.optimization_barrier((summed, new_object))
    grad_scale = jnp.sqrt(jnp.mean(summed * summed) + 1e-06)
    new_probe = probe_mode_stack - probe_step * summed / grad_scale
    return (new_object, new_probe)


def solution(mesh):
    in_specs = (
        P(None, None, "obj", "scan"),
        P(),
        P(("obj", "scan"), None),
        P(("obj", "scan"), None, None),
        P(("obj", "scan")),
    )
    out_specs = (P(None, None, "obj", "scan"), P())
    return jax.shard_map(
        on_device, mesh=mesh, in_specs=in_specs, out_specs=out_specs, check_vma=False
    )
```

```python
import functools
import math

import jax
import jax.numpy as jnp
import numpy as np
from jax import lax
from jax.experimental import pallas as pl
from jax.experimental.pallas import tpu as pltpu
from jax.sharding import PartitionSpec as P

chirp_scale = 24.0
probe_step = 0.15
lanes = 128
sublanes = 8
vmem_bytes = 56 * 1024 * 1024


def from_behind(array, axis, by):
    count = lax.axis_size(axis)
    pairs = [(i, i + by) for i in range(count) if 0 <= i + by < count]
    return lax.ppermute(array, axis, pairs)


def dft_parts(pattern):
    indices = np.arange(pattern)
    angles = (indices[:, None] * indices[None, :] % pattern) * (2.0 * math.pi / pattern)
    parts = (np.cos(angles) / math.sqrt(pattern), np.sin(angles) / math.sqrt(pattern))
    return [part.astype(np.float32).astype(jnp.bfloat16).astype(np.float64) for part in parts]


def block_matrix(real_part, imag_part):
    upper = np.concatenate([real_part, -imag_part], axis=1)
    lower = np.concatenate([imag_part, real_part], axis=1)
    return jnp.asarray(np.concatenate([upper, lower], axis=0).astype(np.float32), jnp.bfloat16)


def tables(pattern):
    cos, sin = dft_parts(pattern)
    indices = np.arange(pattern)
    freqs = ((indices + pattern // 2) % pattern - pattern // 2) / pattern
    chirp = np.exp(-1j * math.pi * chirp_scale * freqs**2)
    hop = (cos + 1j * sin) @ (chirp[:, None] * (cos - 1j * sin))
    return (
        block_matrix(cos, -sin), block_matrix(cos, sin),
        block_matrix(hop.real, hop.imag), block_matrix(hop.real, -hop.imag),
    )


def aligned(row, col):
    row_base = pl.multiple_of(row // sublanes * sublanes, sublanes)
    col_base = pl.multiple_of(col // lanes * lanes, lanes)
    return row_base, col_base, row - row_base, col - col_base


def pad(array):
    array = jnp.concatenate([array, jnp.zeros((array.shape[0], lanes), jnp.float32)], axis=1)
    return jnp.concatenate([array, jnp.zeros((sublanes, array.shape[1]), jnp.float32)], axis=0)


def roll_down(array, rows, cols):
    return pltpu.roll(pltpu.roll(array, cols, 1), rows, 0)


def transform(real_part, imag_part, left, right):
    pattern = real_part.shape[0]
    stacked = jnp.concatenate([real_part.astype(jnp.bfloat16), imag_part.astype(jnp.bfloat16)], axis=0)
    half = jnp.dot(left, stacked, preferred_element_type=jnp.float32).astype(jnp.bfloat16)
    half = jnp.concatenate([half[:pattern], half[pattern:]], axis=1)
    full = jnp.dot(half, right, preferred_element_type=jnp.float32)
    return full[:, :pattern], full[:, pattern:]


def slots_kernel(
    corners, used, tile, right, lower, corner, probe, measured, table_f, table_b, hop_f, hop_b,
    grad_tile, grad_right, grad_lower, grad_corner, grad_probe,
    ext, grad, window, waves, far, back, intensity, term, sems_in, sems_out,
):
    modes, _, pattern, _ = probe.shape
    layers = tile.shape[0]
    height, width = tile.shape[2], tile.shape[3]
    wide = pattern + lanes
    tall = pattern + sublanes

    def spots(buffer):
        return (
            buffer.at[:, :, pl.ds(0, height), pl.ds(0, width)],
            buffer.at[:, :, pl.ds(0, height), pl.ds(width, pattern)],
            buffer.at[:, :, pl.ds(height, pattern), pl.ds(0, width)],
            buffer.at[:, :, pl.ds(height, pattern), pl.ds(width, pattern)],
        )

    loads = [
        pltpu.make_async_copy(source, spot, sems_in.at[k])
        for k, (source, spot) in enumerate(zip((tile, right, lower, corner), spots(ext)))
    ]
    for load in loads:
        load.start()
    grad[...] = jnp.zeros_like(grad)
    grad_probe[...] = jnp.zeros_like(grad_probe)
    for load in loads:
        load.wait()

    @pl.loop(0, used[0])
    def _(slot):
        row = corners[slot, 0]
        col = corners[slot, 1]
        row_base, col_base, row_shift, col_shift = aligned(row, col)
        row_back = jnp.where(row_shift == 0, 0, tall - row_shift)
        col_back = jnp.where(col_shift == 0, 0, wide - col_shift)
        for layer in range(layers):
            for part in range(2):
                block = ext[layer, part, pl.ds(row_base, tall), pl.ds(col_base, wide)]
                window[layer, part] = roll_down(block, row_back, col_back)[:pattern, :pattern]
        intensity[...] = jnp.zeros_like(intensity)
        term[...] = jnp.zeros_like(term)

        for layer in range(layers):

            @pl.loop(0, modes, unroll=3)
            def _(mode, layer=layer):
                last = layer == layers - 1
                if layer == 0:
                    wr, wi = probe[mode, 0], probe[mode, 1]
                else:
                    wr, wi = waves[layer - 1, mode, 0], waves[layer - 1, mode, 1]
                o_r, o_i = window[layer, 0], window[layer, 1]
                tables = (table_f, table_b) if last else (hop_f, hop_b)
                fr, fi = transform(o_r * wr - o_i * wi, o_r * wi + o_i * wr, tables[0][...], tables[1][...])
                if last:
                    far[mode, 0] = fr
                    far[mode, 1] = fi
                    intensity[...] += fr * fr + fi * fi
                else:
                    waves[layer, mode, 0] = fr
                    waves[layer, mode, 1] = fi

        intensity[...] = intensity[...] - measured[slot]

        for layer in reversed(range(layers)):

            @pl.loop(0, modes, unroll=3)
            def _(mode, layer=layer):
                if layer == layers - 1:
                    gain = intensity[...]
                    gr, gi = transform(gain * far[mode, 0], gain * far[mode, 1], table_b[...], table_f[...])
                else:
                    gr, gi = transform(back[mode, 0], back[mode, 1], hop_b[...], hop_f[...])
                if layer == 0:
                    wr, wi = probe[mode, 0], probe[mode, 1]
                else:
                    wr, wi = waves[layer - 1, mode, 0], waves[layer - 1, mode, 1]
                term[layer, 0] += wr * gr + wi * gi
                term[layer, 1] += wr * gi - wi * gr
                o_r, o_i = window[layer, 0], window[layer, 1]
                gr, gi = o_r * gr + o_i * gi, o_r * gi - o_i * gr
                if layer == 0:
                    grad_probe[mode, 0] += gr
                    grad_probe[mode, 1] += gi
                else:
                    back[mode, 0] = gr.astype(jnp.bfloat16)
                    back[mode, 1] = gi.astype(jnp.bfloat16)

        for layer in range(layers):
            for part in range(2):
                at = (layer, part, pl.ds(row_base, tall), pl.ds(col_base, wide))
                grad[at] = grad[at] + roll_down(pad(term[layer, part]), row_shift, col_shift)

    saves = [
        pltpu.make_async_copy(spot, target, sems_out.at[k])
        for k, (spot, target) in enumerate(
            zip(spots(grad), (grad_tile, grad_right, grad_lower, grad_corner))
        )
    ]
    for save in saves:
        save.start()
    for save in saves:
        save.wait()


def run_slots(corners, used, tile, right, lower, corner, probe, measured, table_f, table_b, hop_f, hop_b):
    layers, _, height, width = tile.shape
    modes, _, pattern, _ = probe.shape
    smem = pl.BlockSpec(memory_space=pltpu.SMEM)
    vmem = pl.BlockSpec(memory_space=pltpu.VMEM)
    anyw = pl.BlockSpec(memory_space=pl.ANY)
    f32 = jnp.float32
    ext_shape = (layers, 2, height + pattern, width + pattern)
    return pl.pallas_call(
        slots_kernel,
        out_shape=(
            jax.ShapeDtypeStruct(tile.shape, f32),
            jax.ShapeDtypeStruct(right.shape, f32),
            jax.ShapeDtypeStruct(lower.shape, f32),
            jax.ShapeDtypeStruct(corner.shape, f32),
            jax.ShapeDtypeStruct(probe.shape, f32),
        ),
        in_specs=[smem, smem, anyw, anyw, anyw, anyw, vmem, vmem, vmem, vmem, vmem, vmem],
        out_specs=(anyw, anyw, anyw, anyw, vmem),
        scratch_shapes=[
            pltpu.VMEM(ext_shape, f32),
            pltpu.VMEM(ext_shape, f32),
            pltpu.VMEM((layers, 2, pattern, pattern), f32),
            pltpu.VMEM((layers - 1, modes, 2, pattern, pattern), f32),
            pltpu.VMEM((modes, 2, pattern, pattern), f32),
            pltpu.VMEM((modes, 2, pattern, pattern), jnp.bfloat16),
            pltpu.VMEM((pattern, pattern), f32),
            pltpu.VMEM((layers, 2, pattern, pattern), f32),
            pltpu.SemaphoreType.DMA((4,)),
            pltpu.SemaphoreType.DMA((4,)),
        ],
        compiler_params=pltpu.CompilerParams(vmem_limit_bytes=vmem_bytes),
        cost_estimate=pl.CostEstimate(flops=29_000_000_000, bytes_accessed=30_000_000, transcendentals=0),
    )(corners, used, tile, right, lower, corner, probe, measured, table_f, table_b, hop_f, hop_b)


MESH = pl.DeviceIdType.MESH


def place():
    return lax.axis_index("obj"), lax.axis_index("scan")


def greet(partners):
    barrier = pltpu.get_barrier_semaphore()
    for exists, device in partners:

        @pl.when(exists)
        def _(device=device):
            pl.semaphore_signal(barrier, inc=1, device_id=device, device_id_type=MESH)

    count = 0
    for exists, _ in partners:
        count = count + (1 if exists is True else jnp.where(exists, 1, 0))
    pl.semaphore_wait(barrier, count)


def neighbours(rows, cols):
    row, col = place()
    return {
        "up": (row > 0, (row - 1, col)),
        "down": (row < rows - 1, (row + 1, col)),
        "left": (col > 0, (row, col - 1)),
        "right": (col < cols - 1, (row, col + 1)),
    }


def rims_kernel(rows, cols, tile, right, lower, corner, sent, got):
    near = neighbours(rows, cols)
    greet(list(near.values()))
    layers, pattern = tile.shape[0], corner.shape[-1]
    height = tile.shape[2]
    has_up, up = near["up"]
    has_down, _ = near["down"]
    has_left, left = near["left"]
    has_right, _ = near["right"]

    def copy(source, target, k, device):
        return pltpu.make_async_remote_copy(
            src_ref=source, dst_ref=target, send_sem=sent.at[k], recv_sem=got.at[k],
            device_id=device, device_id_type=MESH,
        )

    top, rest = pl.ds(0, pattern), pl.ds(pattern, height - pattern)
    first = pl.ds(0, pattern)
    tops = [copy(tile.at[n, :, top, first], right.at[n, :, top], 4 * n, left) for n in range(layers)]
    rests = [copy(tile.at[n, :, rest, first], right.at[n, :, rest], 4 * n + 1, left) for n in range(layers)]
    lowers = [copy(tile.at[n, :, top], lower.at[n], 4 * n + 2, up) for n in range(layers)]
    corners = [copy(right.at[n, :, top], corner.at[n], 4 * n + 3, up) for n in range(layers)]
    for n in range(layers):

        @pl.when(has_left)
        def _(n=n):
            tops[n].start()

        @pl.when(has_up)
        def _(n=n):
            lowers[n].start()

        @pl.when(has_left)
        def _(n=n):
            rests[n].start()

    for n in range(layers):

        @pl.when(has_right)
        def _(n=n):
            tops[n].wait_recv()

            @pl.when(has_up)
            def _():
                corners[n].start()

    for n in range(layers):

        @pl.when(has_right)
        def _(n=n):
            rests[n].wait_recv()

            @pl.when(has_down)
            def _():
                corners[n].wait_recv()

            @pl.when(has_up)
            def _():
                corners[n].wait_send()

        @pl.when(has_down)
        def _(n=n):
            lowers[n].wait_recv()

        @pl.when(has_left)
        def _(n=n):
            tops[n].wait_send()
            rests[n].wait_send()

        @pl.when(has_up)
        def _(n=n):
            lowers[n].wait_send()


def run_rims(rows, cols, tile, pattern):
    layers, _, height, width = tile.shape
    anyw = pl.BlockSpec(memory_space=pl.ANY)
    f32 = jnp.float32
    return pl.pallas_call(
        functools.partial(rims_kernel, rows, cols),
        out_shape=(
            jax.ShapeDtypeStruct((layers, 2, height, pattern), f32),
            jax.ShapeDtypeStruct((layers, 2, pattern, width), f32),
            jax.ShapeDtypeStruct((layers, 2, pattern, pattern), f32),
        ),
        in_specs=[anyw],
        out_specs=(anyw,) * 3,
        scratch_shapes=[pltpu.SemaphoreType.DMA((4 * layers,)), pltpu.SemaphoreType.DMA((4 * layers,))],
        compiler_params=pltpu.CompilerParams(collective_id=0, has_side_effects=True),
        cost_estimate=pl.CostEstimate(flops=0, bytes_accessed=10_000_000, transcendentals=0),
    )(tile)


def digits(rows, cols):
    return {
        "core": ("obj", 1, 2),
        "y": ("obj", 2, rows // 2),
        "x": ("scan", 1, 2),
        "z": ("scan", 2, cols // 2),
    }


def member(digit, by):
    axis, stride, radix = digit
    row, col = place()
    at = row if axis == "obj" else col
    mine = at // stride % radix
    theirs = (mine + by) % radix
    there = at + (theirs - mine) * stride
    return mine, theirs, ((there, col) if axis == "obj" else (row, there))


def group(digit):
    return [(True, member(digit, by)[2]) for by in range(1, digit[2])]


streams = (
    (0, 0, 2, ("x", "y", "z")),
    (1, 0, 2, ("y", "x", "z")),
    (2, 0, 1, ("x", "z", "y")),
    (2, 1, 1, ("y", "z", "x")),
)


class Reduction:
    def __init__(self, rows, cols, grad, total, held, landed, core_in, sems):
        self.ways = digits(rows, cols)
        self.grad, self.total, self.held, self.landed, self.core_in = grad, total, held, landed, core_in
        self.sent, self.got = sems
        self.count = 0
        self.pending = []
        self.share = grad.shape[0] // 2
        self.state = [[0, grad.shape[1]] for _ in streams]
        self.waits = [[] for _ in streams]
        self.landing = [0 for _ in streams]

    def copy(self, source, target, device):
        k = self.count
        self.count += 1
        made = pltpu.make_async_remote_copy(
            src_ref=source, dst_ref=target, send_sem=self.sent.at[k], recv_sem=self.got.at[k],
            device_id=device, device_id_type=MESH,
        )
        made.start()
        self.pending.append(made)
        return made

    def core_send(self, k):
        mine, theirs, device = member(self.ways["core"], 1)
        self.core_waits = getattr(self, "core_waits", {})
        self.core_waits[k] = self.copy(self.grad.at[theirs * self.share + k], self.core_in.at[k], device)

    def core_add(self, k):
        mine, _, _ = member(self.ways["core"], 1)
        self.core_waits[k].wait_recv()
        self.held[k] = self.grad[mine * self.share + k] + self.core_in[k]

    def lanes_of(self, s):
        return pl.ds(streams[s][1] * lanes, streams[s][2] * lanes)

    def scatter_send(self, s, step):
        mode = streams[s][0]
        digit = self.ways[streams[s][3][step]]
        start, size = self.state[s]
        part = size // digit[2]
        self.waits[s] = []
        for by in range(1, digit[2]):
            _, theirs, device = member(digit, by)
            spot = self.landed.at[mode, pl.ds(self.landing[s], part), self.lanes_of(s)]
            source = self.held.at[mode, pl.ds(pl.multiple_of(start + theirs * part, sublanes), part), self.lanes_of(s)]
            self.waits[s].append((self.copy(source, spot, device), self.landing[s]))
            self.landing[s] += part

    def scatter_add(self, s, step):
        mode = streams[s][0]
        digit = self.ways[streams[s][3][step]]
        start, size = self.state[s]
        part = size // digit[2]
        if digit[2] > 1:
            mine, _, _ = member(digit, 1)
            start = start + mine * part
        self.state[s] = [start, part]
        span = pl.ds(pl.multiple_of(start, sublanes), part)
        value = self.held[mode, span, self.lanes_of(s)]
        for made, landing in self.waits[s]:
            made.wait_recv()
            value = value + self.landed[mode, pl.ds(landing, part), self.lanes_of(s)]
        if step == 2:
            own = member(self.ways["core"], 1)[0] * self.share + mode
            self.total[own, span, self.lanes_of(s)] = value
        else:
            self.held[mode, span, self.lanes_of(s)] = value

    def gather_send(self, s, step):
        mode = streams[s][0]
        digit = self.ways[streams[s][3][step]]
        start, size = self.state[s]
        own = member(self.ways["core"], 1)[0] * self.share + mode
        self.waits[s] = []
        for by in range(1, digit[2]):
            spot = self.total.at[own, pl.ds(pl.multiple_of(start, sublanes), size), self.lanes_of(s)]
            self.waits[s].append(self.copy(spot, spot, member(digit, by)[2]))

    def gather_wait(self, s, step):
        digit = self.ways[streams[s][3][step]]
        start, size = self.state[s]
        for made in self.waits[s]:
            made.wait_recv()
        if digit[2] > 1:
            start = start - member(digit, 1)[0] * size
        self.state[s] = [start, size * digit[2]]

    def core_share(self, s):
        mine, _, device = member(self.ways["core"], 1)
        spot = self.total.at[mine * self.share + streams[s][0], :, self.lanes_of(s)]
        self.waits[s] = [self.copy(spot, spot, device)]

    def run(self):
        every = range(len(streams))
        for k in range(self.share):
            self.core_add(k)
            for s in every:
                if streams[s][0] == k:
                    self.scatter_send(s, 0)
        for step in range(3):
            for s in every:
                self.scatter_add(s, step)
                if step < 2:
                    self.scatter_send(s, step + 1)
                else:
                    self.gather_send(s, 2)
        for step in (2, 1, 0):
            for s in every:
                self.gather_wait(s, step)
                if step:
                    self.gather_send(s, step - 1)
                else:
                    self.core_share(s)
        for s in every:
            for made in self.waits[s]:
                made.wait_recv()
        for made in self.pending:
            made.wait_send()


def share_kernel(
    rows, cols, right, lower, corner, grad, from_left, from_above, total,
    side, edge, held, landed, core_in, sems_in, sent, got, sent_halo, got_halo,
):
    near = neighbours(rows, cols)
    ways = digits(rows, cols)
    partners = list(near.values())
    for digit in ways.values():
        partners += group(digit)
    layers, pattern = right.shape[0], corner.shape[-1]
    height = right.shape[2]
    loads = [
        pltpu.make_async_copy(right, side, sems_in.at[0]),
    ]
    for load in loads:
        load.start()
    greet(partners)
    has_up, up = near["up"]
    has_down, down = near["down"]
    has_left, _ = near["left"]
    has_right, far_right = near["right"]

    def copy(source, target, k, device):
        return pltpu.make_async_remote_copy(
            src_ref=source, dst_ref=target, send_sem=sent_halo.at[k], recv_sem=got_halo.at[k],
            device_id=device, device_id_type=MESH,
        )

    top, rest = pl.ds(0, pattern), pl.ds(pattern, height - pattern)
    tops = [copy(side.at[n, :, top], from_left.at[n, :, top], 4 * n, far_right) for n in range(layers)]
    rests = [copy(side.at[n, :, rest], from_left.at[n, :, rest], 4 * n + 1, far_right) for n in range(layers)]
    lowers = [copy(lower.at[n], from_above.at[n], 4 * n + 2, down) for n in range(layers)]
    corners = [copy(corner.at[n], edge.at[n], 4 * n + 3, down) for n in range(layers)]
    reduction = Reduction(rows, cols, grad, total, held, landed, core_in, (sent, got))
    for k in range(reduction.share):
        reduction.core_send(k)

    @pl.when(has_down)
    def _():
        @pl.when(has_right)
        def _():
            for n in range(layers):
                corners[n].start()

        for n in range(layers):
            lowers[n].start()

    for load in loads:
        load.wait()

    @pl.when(has_right)
    def _():
        for n in range(layers):
            rests[n].start()
        for n in range(layers):

            @pl.when(has_up)
            def _(n=n):
                corners[n].wait_recv()
                side[n, :, :pattern] = side[n, :, :pattern] + edge[n]

            tops[n].start()

    reduction.run()

    @pl.when(has_right)
    def _():
        for n in range(layers):
            rests[n].wait_send()
            tops[n].wait_send()

            @pl.when(has_down)
            def _(n=n):
                corners[n].wait_send()

    @pl.when(has_down)
    def _():
        for n in range(layers):
            lowers[n].wait_send()

    @pl.when(has_left)
    def _():
        for n in range(layers):
            rests[n].wait_recv()
            tops[n].wait_recv()

    @pl.when(has_up)
    def _():
        for n in range(layers):
            lowers[n].wait_recv()


def run_share(rows, cols, right, lower, corner, grad):
    layers = right.shape[0]
    pattern = corner.shape[-1]
    modes = grad.shape[0]
    anyw = pl.BlockSpec(memory_space=pl.ANY)
    vmem = pl.BlockSpec(memory_space=pltpu.VMEM)
    f32 = jnp.float32
    half = (modes // 2, 2 * pattern, pattern)
    dma = pltpu.SemaphoreType.DMA
    count = modes // 2 + len(streams) * (2 * sum(way[2] - 1 for way in digits(rows, cols).values()) - 1)
    from_left, from_above, total = pl.pallas_call(
        functools.partial(share_kernel, rows, cols),
        out_shape=(
            jax.ShapeDtypeStruct(right.shape, f32),
            jax.ShapeDtypeStruct(lower.shape, f32),
            jax.ShapeDtypeStruct((modes, 2 * pattern, pattern), f32),
        ),
        in_specs=[anyw, anyw, anyw, vmem],
        out_specs=(anyw, anyw, vmem),
        scratch_shapes=[
            pltpu.VMEM(right.shape, f32),
            pltpu.VMEM(corner.shape, f32),
            pltpu.VMEM(half, f32), pltpu.VMEM(half, f32), pltpu.VMEM(half, f32),
            dma((1,)), dma((count,)), dma((count,)), dma((4 * layers,)), dma((4 * layers,)),
        ],
        compiler_params=pltpu.CompilerParams(
            collective_id=1, has_side_effects=True, vmem_limit_bytes=40 * 1024 * 1024
        ),
        cost_estimate=pl.CostEstimate(flops=0, bytes_accessed=30_000_000, transcendentals=0),
    )(right, lower, corner, grad.reshape(modes, 2 * pattern, pattern))
    return from_left, from_above, total.reshape(grad.shape)


def light_kernel(height, width, slots, info, probe, light, canvas, power):
    modes, _, pattern, _ = probe.shape
    total = jnp.zeros((pattern, pattern), jnp.float32)
    for mode in range(modes):
        total = total + (probe[mode, 0] * probe[mode, 0] + probe[mode, 1] * probe[mode, 1])
    power[...] = pad(total)
    canvas[...] = jnp.zeros_like(canvas)
    for block in range(4):
        base = block * (2 * slots + 1)

        @pl.loop(0, info[base + 2 * slots])
        def _(slot):
            row = info[base + 2 * slot] + height
            col = info[base + 2 * slot + 1] + width
            row_base, col_base, row_shift, col_shift = aligned(row, col)
            at = (pl.ds(row_base, pattern + sublanes), pl.ds(col_base, pattern + lanes))
            canvas[at] = canvas[at] + roll_down(power[...], row_shift, col_shift)

    light[...] = canvas[height : 2 * height, width : 2 * width] + 1.0


def run_light(height, width, slots, info, probe):
    pattern = probe.shape[-1]
    return pl.pallas_call(
        functools.partial(light_kernel, height, width, slots),
        out_shape=jax.ShapeDtypeStruct((height, width), jnp.float32),
        in_specs=[pl.BlockSpec(memory_space=pltpu.SMEM), pl.BlockSpec(memory_space=pltpu.VMEM)],
        out_specs=pl.BlockSpec(memory_space=pltpu.VMEM),
        scratch_shapes=[
            pltpu.VMEM((2 * height + pattern, 2 * width + pattern), jnp.float32),
            pltpu.VMEM((pattern + sublanes, pattern + lanes), jnp.float32),
        ],
        compiler_params=pltpu.CompilerParams(vmem_limit_bytes=24 * 1024 * 1024),
        cost_estimate=pl.CostEstimate(flops=10_000_000, bytes_accessed=12_000_000, transcendentals=0),
    )(info, probe)


def final_kernel(there, tile, grad, left, above, light, out):
    pattern = left.shape[-1]
    from_left = jnp.where(there[1] > 0, left[0, 0], 0.0)
    from_above = jnp.where(there[0] > 0, above[0, 0], 0.0)
    grad[0, 0, :, :pattern] = grad[0, 0, :, :pattern] + from_left
    grad[0, 0, :pattern, :] = grad[0, 0, :pattern, :] + from_above
    out[0, 0] = tile[0, 0] - grad[0, 0] / light[...]


def run_final(there, tile, grad, left, above, light):
    layers, parts, height, width = tile.shape
    spec = lambda array: pl.BlockSpec((1, 1) + array.shape[2:], lambda i, j: (i, j, 0, 0))
    return pl.pallas_call(
        final_kernel,
        grid=(layers, parts),
        out_shape=jax.ShapeDtypeStruct(tile.shape, jnp.float32),
        in_specs=[
            pl.BlockSpec(memory_space=pltpu.SMEM),
            spec(tile), spec(grad), spec(left), spec(above),
            pl.BlockSpec(light.shape, lambda i, j: (0, 0)),
        ],
        out_specs=spec(tile),
        compiler_params=pltpu.CompilerParams(vmem_limit_bytes=24 * 1024 * 1024),
        cost_estimate=pl.CostEstimate(flops=4_000_000, bytes_accessed=14_000_000, transcendentals=0),
    )(there, tile, grad, left, above, light)


def on_device(object_slab, probe_mode_stack, offsets, measured, counts):
    tile_height = object_slab.shape[2]
    tile_width = object_slab.shape[3]
    pattern = probe_mode_stack.shape[-1]
    slots = offsets.shape[0]
    table_f, table_b, hop_f, hop_b = tables(pattern)
    rows, cols = lax.axis_size("obj"), lax.axis_size("scan")
    right_rim, lower_rim, corner_rim = run_rims(rows, cols, object_slab, pattern)
    base = jnp.stack([lax.axis_index("obj") * tile_height, lax.axis_index("scan") * tile_width])
    base = base.astype(jnp.int32)
    corners = offsets - base
    own_info = jnp.concatenate([offsets.reshape(-1), counts])
    left_info = from_behind(own_info, "scan", 1)
    row_info = jnp.concatenate([own_info, left_info])
    info = jnp.concatenate([row_info, from_behind(row_info, "obj", 1)])
    right_rim, lower_rim, corner_rim, corners, info = lax.optimization_barrier(
        (right_rim, lower_rim, corner_rim, corners, info)
    )
    shifts = jnp.tile(jnp.concatenate([jnp.tile(base, slots), jnp.zeros((1,), jnp.int32)]), 4)
    light = run_light(tile_height, tile_width, slots, info - shifts, probe_mode_stack)
    grad_tile, grad_right, grad_lower, grad_corner, grad_probe = run_slots(
        corners, counts, object_slab, right_rim, lower_rim, corner_rim, probe_mode_stack,
        measured, table_f, table_b, hop_f, hop_b,
    )
    from_left, from_above, summed = run_share(rows, cols, grad_right, grad_lower, grad_corner, grad_probe)
    new_object = run_final(base, object_slab, grad_tile, from_left, from_above, light)
    grad_scale = jnp.sqrt(jnp.mean(summed * summed) + 1e-06)
    new_probe = probe_mode_stack - probe_step * summed / grad_scale
    return (new_object, new_probe)


def solution(mesh):
    in_specs = (
        P(None, None, "obj", "scan"),
        P(),
        P(("obj", "scan"), None),
        P(("obj", "scan"), None, None),
        P(("obj", "scan")),
    )
    out_specs = (P(None, None, "obj", "scan"), P())
    return jax.shard_map(
        on_device, mesh=mesh, in_specs=in_specs, out_specs=out_specs, check_vma=False
    )
```

```python
import functools
import math

import jax
import jax.numpy as jnp
import numpy as np
from jax import lax
from jax.experimental import pallas as pl
from jax.experimental.pallas import tpu as pltpu
from jax.sharding import PartitionSpec as P

chirp_scale = 24.0
probe_step = 0.15
lanes = 128
sublanes = 8


def dft_parts(pattern):
    indices = np.arange(pattern)
    angles = (indices[:, None] * indices[None, :] % pattern) * (2.0 * math.pi / pattern)
    parts = (np.cos(angles) / math.sqrt(pattern), np.sin(angles) / math.sqrt(pattern))
    return [part.astype(np.float32).astype(jnp.bfloat16).astype(np.float64) for part in parts]


def block_matrix(real_part, imag_part):
    upper = np.concatenate([real_part, -imag_part], axis=1)
    lower = np.concatenate([imag_part, real_part], axis=1)
    return jnp.asarray(np.concatenate([upper, lower], axis=0).astype(np.float32), jnp.bfloat16)


def tables(pattern):
    cos, sin = dft_parts(pattern)
    indices = np.arange(pattern)
    freqs = ((indices + pattern // 2) % pattern - pattern // 2) / pattern
    chirp = np.exp(-1j * math.pi * chirp_scale * freqs**2)
    hop = (cos + 1j * sin) @ (chirp[:, None] * (cos - 1j * sin))
    return (
        block_matrix(cos, -sin), block_matrix(cos, sin),
        block_matrix(hop.real, hop.imag), block_matrix(hop.real, -hop.imag),
    )


def aligned(row, col):
    row_base = pl.multiple_of(row // sublanes * sublanes, sublanes)
    col_base = pl.multiple_of(col // lanes * lanes, lanes)
    return row_base, col_base, row - row_base, col - col_base


def pad(array):
    array = jnp.concatenate([array, jnp.zeros((array.shape[0], lanes), jnp.float32)], axis=1)
    return jnp.concatenate([array, jnp.zeros((sublanes, array.shape[1]), jnp.float32)], axis=0)


def roll_down(array, rows, cols):
    return pltpu.roll(pltpu.roll(array, cols, 1), rows, 0)


def transform(real_part, imag_part, left, right):
    pattern = real_part.shape[0]
    stacked = jnp.concatenate([real_part.astype(jnp.bfloat16), imag_part.astype(jnp.bfloat16)], axis=0)
    half = jnp.dot(left, stacked, preferred_element_type=jnp.float32).astype(jnp.bfloat16)
    half = jnp.concatenate([half[:pattern], half[pattern:]], axis=1)
    full = jnp.dot(half, right, preferred_element_type=jnp.float32)
    return full[:, :pattern], full[:, pattern:]


MESH = pl.DeviceIdType.MESH


def place():
    return lax.axis_index("obj"), lax.axis_index("scan")


def greet(partners):
    barrier = pltpu.get_barrier_semaphore()
    for exists, device in partners:

        @pl.when(exists)
        def _(device=device):
            pl.semaphore_signal(barrier, inc=1, device_id=device, device_id_type=MESH)

    count = 0
    for exists, _ in partners:
        count = count + (1 if exists is True else jnp.where(exists, 1, 0))
    pl.semaphore_wait(barrier, count)


def neighbours(rows, cols):
    row, col = place()
    return {
        "up": (row > 0, (row - 1, col)),
        "down": (row < rows - 1, (row + 1, col)),
        "left": (col > 0, (row, col - 1)),
        "right": (col < cols - 1, (row, col + 1)),
    }


def digits(rows, cols):
    return {
        "core": ("obj", 1, 2),
        "y": ("obj", 2, rows // 2),
        "x": ("scan", 1, 2),
        "z": ("scan", 2, cols // 2),
    }


def member(digit, by):
    axis, stride, radix = digit
    row, col = place()
    at = row if axis == "obj" else col
    mine = at // stride % radix
    theirs = (mine + by) % radix
    there = at + (theirs - mine) * stride
    return mine, theirs, ((there, col) if axis == "obj" else (row, there))


def group(digit):
    return [(True, member(digit, by)[2]) for by in range(1, digit[2])]


streams = (
    (0, 0, 2, ("x", "y", "z")),
    (1, 0, 2, ("y", "x", "z")),
    (2, 0, 1, ("x", "z", "y")),
    (2, 1, 1, ("y", "z", "x")),
)


class Reduction:
    def __init__(self, rows, cols, grad, total, held, landed, core_in, sems):
        self.ways = digits(rows, cols)
        self.grad, self.total, self.held, self.landed, self.core_in = grad, total, held, landed, core_in
        self.sent, self.got = sems
        self.count = 0
        self.pending = []
        self.share = grad.shape[0] // 2
        self.state = [[0, grad.shape[1]] for _ in streams]
        self.waits = [[] for _ in streams]
        self.landing = [0 for _ in streams]

    def copy(self, source, target, device):
        k = self.count
        self.count += 1
        made = pltpu.make_async_remote_copy(
            src_ref=source, dst_ref=target, send_sem=self.sent.at[k], recv_sem=self.got.at[k],
            device_id=device, device_id_type=MESH,
        )
        made.start()
        self.pending.append(made)
        return made

    def core_send(self, k):
        mine, theirs, device = member(self.ways["core"], 1)
        self.core_waits = getattr(self, "core_waits", {})
        self.core_waits[k] = self.copy(self.grad.at[theirs * self.share + k], self.core_in.at[k], device)

    def core_add(self, k):
        mine, _, _ = member(self.ways["core"], 1)
        self.core_waits[k].wait_recv()
        self.held[k] = self.grad[mine * self.share + k] + self.core_in[k]

    def lanes_of(self, s):
        return pl.ds(streams[s][1] * lanes, streams[s][2] * lanes)

    def scatter_send(self, s, step):
        mode = streams[s][0]
        digit = self.ways[streams[s][3][step]]
        start, size = self.state[s]
        part = size // digit[2]
        self.waits[s] = []
        for by in range(1, digit[2]):
            _, theirs, device = member(digit, by)
            spot = self.landed.at[mode, pl.ds(self.landing[s], part), self.lanes_of(s)]
            source = self.held.at[mode, pl.ds(pl.multiple_of(start + theirs * part, sublanes), part), self.lanes_of(s)]
            self.waits[s].append((self.copy(source, spot, device), self.landing[s]))
            self.landing[s] += part

    def scatter_add(self, s, step):
        mode = streams[s][0]
        digit = self.ways[streams[s][3][step]]
        start, size = self.state[s]
        part = size // digit[2]
        if digit[2] > 1:
            mine, _, _ = member(digit, 1)
            start = start + mine * part
        self.state[s] = [start, part]
        span = pl.ds(pl.multiple_of(start, sublanes), part)
        value = self.held[mode, span, self.lanes_of(s)]
        for made, landing in self.waits[s]:
            made.wait_recv()
            value = value + self.landed[mode, pl.ds(landing, part), self.lanes_of(s)]
        if step == 2:
            own = member(self.ways["core"], 1)[0] * self.share + mode
            self.total[own, span, self.lanes_of(s)] = value
        else:
            self.held[mode, span, self.lanes_of(s)] = value

    def gather_send(self, s, step):
        mode = streams[s][0]
        digit = self.ways[streams[s][3][step]]
        start, size = self.state[s]
        own = member(self.ways["core"], 1)[0] * self.share + mode
        self.waits[s] = []
        for by in range(1, digit[2]):
            spot = self.total.at[own, pl.ds(pl.multiple_of(start, sublanes), size), self.lanes_of(s)]
            self.waits[s].append(self.copy(spot, spot, member(digit, by)[2]))

    def gather_wait(self, s, step):
        digit = self.ways[streams[s][3][step]]
        start, size = self.state[s]
        for made in self.waits[s]:
            made.wait_recv()
        if digit[2] > 1:
            start = start - member(digit, 1)[0] * size
        self.state[s] = [start, size * digit[2]]

    def core_share(self, s):
        mine, _, device = member(self.ways["core"], 1)
        spot = self.total.at[mine * self.share + streams[s][0], :, self.lanes_of(s)]
        self.waits[s] = [self.copy(spot, spot, device)]


def when(conditions, action):
    pl.when(functools.reduce(jnp.logical_and, conditions))(action)


def rims_kernel(rows, cols, tile, info, right, lower, corner, boxes, sent, got, sent_box, got_box, sem):
    near = neighbours(rows, cols)
    row, col = place()
    layers, pattern = tile.shape[0], corner.shape[-1]
    height = tile.shape[2]
    has_up, up = near["up"]
    has_down, down = near["down"]
    has_left, left = near["left"]
    has_right, far_right = near["right"]
    after = (jnp.logical_and(has_down, has_right), (row + 1, col + 1))
    before = (jnp.logical_and(has_up, has_left), (row - 1, col - 1))
    keep = pltpu.make_async_copy(info, boxes.at[0], sem.at[0])
    keep.start()
    greet(list(near.values()) + [after, before])

    def copy(source, target, k, device, sems=(sent, got)):
        return pltpu.make_async_remote_copy(
            src_ref=source, dst_ref=target, send_sem=sems[0].at[k], recv_sem=sems[1].at[k],
            device_id=device, device_id_type=MESH,
        )

    top, rest = pl.ds(0, pattern), pl.ds(pattern, height - pattern)
    first = pl.ds(0, pattern)
    each = range(layers)
    tops = [copy(tile.at[n, :, top, first], right.at[n, :, top], 4 * n, left) for n in each]
    rests = [copy(tile.at[n, :, rest, first], right.at[n, :, rest], 4 * n + 1, left) for n in each]
    lowers = [copy(tile.at[n, :, top], lower.at[n], 4 * n + 2, up) for n in each]
    corners = [copy(right.at[n, :, top], corner.at[n], 4 * n + 3, up) for n in each]
    tell = [
        (has_right, has_left, copy(info, boxes.at[1], 0, far_right, (sent_box, got_box))),
        (has_down, has_up, copy(info, boxes.at[2], 1, down, (sent_box, got_box))),
        (after[0], before[0], copy(info, boxes.at[3], 2, after[1], (sent_box, got_box))),
    ]
    for to, _, box in tell:
        when([to], box.start)
    for n in each:
        when([has_left], tops[n].start)
        when([has_up], lowers[n].start)
    for n in each:
        when([has_left], rests[n].start)
    keep.wait()
    for k, (to, there, box) in enumerate(tell):
        when([there], box.wait_recv)

        @pl.when(jnp.logical_not(there))
        def _(k=k):
            boxes[k + 1] = jnp.zeros(boxes.shape[1:], jnp.int32)

        when([to], box.wait_send)
    for n in each:
        when([has_right], tops[n].wait_recv)
        when([has_right, has_up], corners[n].start)
    for n in each:
        when([has_right], rests[n].wait_recv)
        when([has_right, has_down], corners[n].wait_recv)
        when([has_right, has_up], corners[n].wait_send)
        when([has_down], lowers[n].wait_recv)
        when([has_left], tops[n].wait_send)
        when([has_left], rests[n].wait_send)
        when([has_up], lowers[n].wait_send)


def run_rims(rows, cols, tile, info, pattern):
    layers, _, height, width = tile.shape
    anyw = pl.BlockSpec(memory_space=pl.ANY)
    vmem = pl.BlockSpec(memory_space=pltpu.VMEM)
    f32, dma = jnp.float32, pltpu.SemaphoreType.DMA
    return pl.pallas_call(
        functools.partial(rims_kernel, rows, cols),
        out_shape=(
            jax.ShapeDtypeStruct((layers, 2, height, pattern), f32),
            jax.ShapeDtypeStruct((layers, 2, pattern, width), f32),
            jax.ShapeDtypeStruct((layers, 2, pattern, pattern), f32),
            jax.ShapeDtypeStruct((4,) + info.shape, jnp.int32),
        ),
        in_specs=[anyw, vmem],
        out_specs=(anyw, anyw, anyw, vmem),
        scratch_shapes=[dma((4 * layers,)), dma((4 * layers,)), dma((3,)), dma((3,)), dma((1,))],
        compiler_params=pltpu.CompilerParams(collective_id=0, has_side_effects=True),
        cost_estimate=pl.CostEstimate(flops=0, bytes_accessed=10_000_000, transcendentals=0),
    )(tile, info)


def slots_kernel(
    rows, cols, boxes, offsets, used, tile, right, lower, corner, probe_in, measured_in, table_f_in, table_b_in, hop_f_in, hop_b_in,
    grad_tile, grad_right, grad_lower, grad_corner, grad, light,
    ext0, ext1, window, waves, far, back, term, canvas, probe, measured, table_f, table_b, hop_f, hop_b, intensity,
    sems_in, sems_out,
):
    bf16 = jnp.bfloat16
    modes, pattern = probe.shape[0], probe.shape[-1]
    slots = offsets.shape[0]
    height, width = tile.shape[2], tile.shape[3]
    wide, tall = pattern + lanes, pattern + sublanes
    exts = (ext0, ext1)
    row, col = place()
    first, second = pl.ds(0, pattern), pl.ds(pattern, pattern)

    def spots(n):
        return (
            exts[n].at[:, pl.ds(0, height), pl.ds(0, width)],
            exts[n].at[:, pl.ds(0, height), pl.ds(width, pattern)],
            exts[n].at[:, pl.ds(height, pattern), pl.ds(0, width)],
            exts[n].at[:, pl.ds(height, pattern), pl.ds(width, pattern)],
        )

    moves = [(probe_in, probe)]
    moves += [(array.at[0], spot) for array, spot in zip((tile, right, lower, corner), spots(0))]
    moves += [(hop_f_in, hop_f), (hop_b_in, hop_b)]
    moves += [(array.at[1], spot) for array, spot in zip((tile, right, lower, corner), spots(1))]
    moves += [(table_f_in, table_f), (table_b_in, table_b), (measured_in, measured)]
    loads = [pltpu.make_async_copy(a, b, sems_in.at[k]) for k, (a, b) in enumerate(moves)]
    for load in loads:
        load.start()

    canvas[...] = jnp.zeros_like(canvas)
    loads[0].wait()
    power = jnp.zeros((pattern, pattern), jnp.float32)
    for mode in range(modes):
        power = power + (probe[mode, 0] * probe[mode, 0] + probe[mode, 1] * probe[mode, 1])
    intensity[...] = power
    for block in range(4):

        @pl.loop(0, boxes[block, 0, 2 * slots])
        def _(slot, block=block):
            at_row = boxes[block, 0, 2 * slot] - row * height + height
            at_col = boxes[block, 0, 2 * slot + 1] - col * width + width
            row_base, col_base, row_shift, col_shift = aligned(at_row, at_col)
            at = (pl.ds(row_base, tall), pl.ds(col_base, wide))
            canvas[at] = canvas[at] + roll_down(pad(intensity[...]), row_shift, col_shift)

    light[...] = canvas[height : 2 * height, width : 2 * width] + 1.0

    def bases(slot):
        return aligned(offsets[slot, 0] - row * height, offsets[slot, 1] - col * width)

    def cut(n):
        @pl.loop(0, used[0])
        def _(slot):
            row_base, col_base, row_shift, col_shift = bases(slot)
            row_back = jnp.where(row_shift == 0, 0, tall - row_shift)
            col_back = jnp.where(col_shift == 0, 0, wide - col_shift)
            for part in range(2):
                block = exts[n][part, pl.ds(row_base, tall), pl.ds(col_base, wide)]
                window[slot, n, part] = roll_down(block, row_back, col_back)[:pattern, :pattern]

    def spread(n, slot):
        row_base, col_base, row_shift, col_shift = bases(slot)
        for part in range(2):
            at = (part, pl.ds(row_base, tall), pl.ds(col_base, wide))
            exts[n][at] = exts[n][at] + roll_down(pad(term[part]), row_shift, col_shift)

    def save(n):
        return [
            pltpu.make_async_copy(spot, target.at[n], sems_out.at[4 * n + k])
            for k, (spot, target) in enumerate(zip(spots(n), (grad_tile, grad_right, grad_lower, grad_corner)))
        ]

    for k in range(1, 7):
        loads[k].wait()
    cut(0)
    exts[0][...] = jnp.zeros_like(exts[0])

    @pl.loop(0, used[0])
    def _(slot):
        @pl.loop(0, modes, unroll=3)
        def _(mode):
            wr, wi = probe[mode, 0], probe[mode, 1]
            o_r, o_i = window[slot, 0, 0], window[slot, 0, 1]
            wr, wi = transform(o_r * wr - o_i * wi, o_r * wi + o_i * wr, hop_f[...], hop_b[...])
            waves[slot, mode, 0] = wr
            waves[slot, mode, 1] = wi

    for k in range(7, len(moves)):
        loads[k].wait()
    cut(1)
    exts[1][...] = jnp.zeros_like(exts[1])

    @pl.loop(0, used[0])
    def _(slot):
        intensity[...] = -measured[slot]
        term[...] = jnp.zeros_like(term)

        @pl.loop(0, modes, unroll=3)
        def _(mode):
            wr, wi = waves[slot, mode, 0], waves[slot, mode, 1]
            o_r, o_i = window[slot, 1, 0], window[slot, 1, 1]
            fr, fi = transform(o_r * wr - o_i * wi, o_r * wi + o_i * wr, table_f[...], table_b[...])
            far[mode, 0] = fr
            far[mode, 1] = fi
            intensity[...] += fr * fr + fi * fi

        @pl.loop(0, modes, unroll=3)
        def _(mode):
            gain = intensity[...]
            gr, gi = transform(gain * far[mode, 0], gain * far[mode, 1], table_b[...], table_f[...])
            wr, wi = waves[slot, mode, 0], waves[slot, mode, 1]
            term[0] += wr * gr + wi * gi
            term[1] += wr * gi - wi * gr
            o_r, o_i = window[slot, 1, 0], window[slot, 1, 1]
            back[slot, mode, 0] = (o_r * gr + o_i * gi).astype(bf16)
            back[slot, mode, 1] = (o_r * gi - o_i * gr).astype(bf16)

        spread(1, slot)

    saves = save(1)
    for one in saves:
        one.start()
    grad[...] = jnp.zeros_like(grad)

    @pl.loop(0, used[0])
    def _(slot):
        term[...] = jnp.zeros_like(term)

        @pl.loop(0, modes, unroll=3)
        def _(mode):
            gr, gi = transform(back[slot, mode, 0], back[slot, mode, 1], hop_b[...], hop_f[...])
            wr, wi = probe[mode, 0], probe[mode, 1]
            term[0] += wr * gr + wi * gi
            term[1] += wr * gi - wi * gr
            o_r, o_i = window[slot, 0, 0], window[slot, 0, 1]
            grad[mode, first] += o_r * gr + o_i * gi
            grad[mode, second] += o_r * gi - o_i * gr

        spread(0, slot)

    last = save(0)
    for one in last:
        one.start()
    for one in saves + last:
        one.wait()


def run_slots(rows, cols, boxes, offsets, used, tile, right, lower, corner, probe, measured, *matrices):
    layers, _, height, width = tile.shape
    modes, _, pattern, _ = probe.shape
    slots = offsets.shape[0]
    smem = pl.BlockSpec(memory_space=pltpu.SMEM)
    vmem = pl.BlockSpec(memory_space=pltpu.VMEM)
    anyw = pl.BlockSpec(memory_space=pl.ANY)
    f32, bf16 = jnp.float32, jnp.bfloat16
    space, dma = pltpu.VMEM, pltpu.SemaphoreType.DMA
    ext = (2, height + pattern, width + pattern)
    return pl.pallas_call(
        functools.partial(slots_kernel, rows, cols),
        out_shape=(
            jax.ShapeDtypeStruct(tile.shape, f32),
            jax.ShapeDtypeStruct(right.shape, f32),
            jax.ShapeDtypeStruct(lower.shape, f32),
            jax.ShapeDtypeStruct(corner.shape, f32),
            jax.ShapeDtypeStruct((modes, 2 * pattern, pattern), f32),
            jax.ShapeDtypeStruct((height, width), f32),
        ),
        in_specs=[smem, smem, smem] + [anyw] * 10,
        out_specs=(anyw, anyw, anyw, anyw, vmem, vmem),
        scratch_shapes=[
            space(ext, f32), space(ext, f32),
            space((slots, layers, 2, pattern, pattern), f32),
            space((slots, modes, 2, pattern, pattern), f32),
            space((modes, 2, pattern, pattern), f32),
            space((slots, modes, 2, pattern, pattern), bf16),
            space((2, pattern, pattern), f32),
            space((2 * height + pattern, 2 * width + pattern), f32),
            space(probe.shape, f32), space(measured.shape, f32),
            *[space((2 * pattern, 2 * pattern), bf16) for _ in range(4)],
            space((pattern, pattern), f32),
            dma((14,)), dma((8,)),
        ],
        compiler_params=pltpu.CompilerParams(vmem_limit_bytes=58 * 1024 * 1024),
        cost_estimate=pl.CostEstimate(flops=20_000_000_000, bytes_accessed=30_000_000, transcendentals=0),
    )(boxes, offsets, used, tile, right, lower, corner, probe, measured, *matrices)


def share_kernel(
    rows, cols, tile, right, lower, corner, grad_tile, grad, light, probe_in, new_object, total,
    side, inner, left_in, above_in, edge, held, landed, core_in, probe, sems_in, sent_halo, got_halo, sent, got,
):
    near = neighbours(rows, cols)
    ways = digits(rows, cols)
    partners = list(near.values())
    for digit in ways.values():
        partners += group(digit)
    layers, pattern = right.shape[0], corner.shape[-1]
    height, width = tile.shape[2], tile.shape[3]
    modes = grad.shape[0]
    each = range(layers)
    first, second = pl.ds(0, pattern), pl.ds(pattern, pattern)
    moves = [(right, side), (tile, new_object), (grad_tile, inner), (probe_in, probe)]
    loads = [pltpu.make_async_copy(a, b, sems_in.at[k]) for k, (a, b) in enumerate(moves)]
    for load in loads:
        load.start()
    greet(partners)
    has_up, up = near["up"]
    has_down, down = near["down"]
    has_left, _ = near["left"]
    has_right, far_right = near["right"]

    def copy(source, target, k, device):
        return pltpu.make_async_remote_copy(
            src_ref=source, dst_ref=target, send_sem=sent_halo.at[k], recv_sem=got_halo.at[k],
            device_id=device, device_id_type=MESH,
        )

    top, rest = pl.ds(0, pattern), pl.ds(pattern, height - pattern)
    tops = [copy(side.at[n, :, top], left_in.at[n, :, top], 4 * n, far_right) for n in each]
    rests = [copy(side.at[n, :, rest], left_in.at[n, :, rest], 4 * n + 1, far_right) for n in each]
    lowers = [copy(lower.at[n], above_in.at[n], 4 * n + 2, down) for n in each]
    corners = [copy(corner.at[n], edge.at[n], 4 * n + 3, down) for n in each]
    reduction = Reduction(rows, cols, grad, total, held, landed, core_in, (sent, got))

    def add_corner(n):
        @pl.when(jnp.logical_and(has_right, has_up))
        def _():
            corners[n].wait_recv()
            side[n, :, :pattern] = side[n, :, :pattern] + edge[n]

        when([has_right], tops[n].start)

    def finish(n):
        @pl.when(has_left)
        def _():
            rests[n].wait_recv()
            tops[n].wait_recv()

        @pl.when(jnp.logical_not(has_left))
        def _():
            left_in[n] = jnp.zeros(left_in.shape[1:], jnp.float32)

        when([has_up], lowers[n].wait_recv)

        @pl.when(jnp.logical_not(has_up))
        def _():
            above_in[n] = jnp.zeros(above_in.shape[1:], jnp.float32)

        inner[n, :, :, :pattern] += left_in[n]
        inner[n, :, :pattern, :] += above_in[n]
        for part in range(2):
            new_object[n, part] = new_object[n, part] - inner[n, part] / light[...]

    every = range(len(streams))
    for k in range(reduction.share):
        reduction.core_send(k)
    when([has_down, has_right], corners[0].start)
    when([has_down, has_right], corners[1].start)
    loads[0].wait()
    for k in range(reduction.share):
        reduction.core_add(k)
        for s in every:
            if streams[s][0] == k:
                reduction.scatter_send(s, 0)
    when([has_right], rests[0].start)
    when([has_right], rests[1].start)
    when([has_down], lowers[0].start)
    add_corner(0)
    add_corner(1)
    when([has_down], lowers[1].start)
    for step in range(3):
        for s in every:
            reduction.scatter_add(s, step)
            if step < 2:
                reduction.scatter_send(s, step + 1)
            else:
                reduction.gather_send(s, 2)
    for step in (2, 1, 0):
        for s in every:
            reduction.gather_wait(s, step)
            if step:
                reduction.gather_send(s, step - 1)
            else:
                reduction.core_share(s)
    loads[1].wait()
    loads[2].wait()
    finish(0)
    finish(1)
    for s in range(len(streams)):
        for made in reduction.waits[s]:
            made.wait_recv()
    for made in reduction.pending:
        made.wait_send()
    for n in each:
        when([has_right], rests[n].wait_send)
        when([has_right], tops[n].wait_send)
        when([has_down, has_right], corners[n].wait_send)
        when([has_down], lowers[n].wait_send)
    loads[3].wait()
    squares = jnp.zeros((pattern, pattern), jnp.float32)
    for mode in range(modes):
        squares = squares + (total[mode, first] * total[mode, first] + total[mode, second] * total[mode, second])
    count = modes * 2 * pattern * pattern
    scale = jnp.sqrt(jnp.broadcast_to(jnp.sum(squares), (pattern, pattern)) * (1.0 / count) + 1e-06)
    factor = probe_step / scale
    for mode in range(modes):
        total[mode, first] = probe[mode, 0] - factor * total[mode, first]
        total[mode, second] = probe[mode, 1] - factor * total[mode, second]


def run_share(rows, cols, tile, right, lower, corner, grad_tile, grad, light, probe):
    layers = right.shape[0]
    pattern = corner.shape[-1]
    modes = grad.shape[0]
    anyw = pl.BlockSpec(memory_space=pl.ANY)
    vmem = pl.BlockSpec(memory_space=pltpu.VMEM)
    f32, space, dma = jnp.float32, pltpu.VMEM, pltpu.SemaphoreType.DMA
    half = (modes // 2, 2 * pattern, pattern)
    count = modes // 2 + len(streams) * (2 * sum(way[2] - 1 for way in digits(rows, cols).values()) - 1)
    new_object, new_probe = pl.pallas_call(
        functools.partial(share_kernel, rows, cols),
        out_shape=(
            jax.ShapeDtypeStruct(tile.shape, f32),
            jax.ShapeDtypeStruct((modes, 2 * pattern, pattern), f32),
        ),
        in_specs=[anyw, anyw, anyw, anyw, anyw, vmem, vmem, anyw],
        out_specs=(vmem, vmem),
        scratch_shapes=[
            space(right.shape, f32), space(tile.shape, f32), space(right.shape, f32), space(lower.shape, f32),
            space(corner.shape, f32), space(half, f32), space(half, f32), space(half, f32), space(probe.shape, f32),
            dma((4,)), dma((4 * layers,)), dma((4 * layers,)), dma((count,)), dma((count,)),
        ],
        compiler_params=pltpu.CompilerParams(
            collective_id=1, has_side_effects=True, vmem_limit_bytes=40 * 1024 * 1024
        ),
        cost_estimate=pl.CostEstimate(flops=0, bytes_accessed=30_000_000, transcendentals=0),
    )(tile, right, lower, corner, grad_tile, grad, light, probe)
    return new_object, new_probe.reshape(probe.shape)


def on_device(object_slab, probe_mode_stack, offsets, measured, counts):
    pattern = probe_mode_stack.shape[-1]
    rows, cols = lax.axis_size("obj"), lax.axis_size("scan")
    info = jnp.concatenate([offsets.reshape(-1), counts])
    info = jnp.pad(info[None], ((0, sublanes - 1), (0, lanes - info.shape[0])))
    right, lower, corner, boxes = run_rims(rows, cols, object_slab, info, pattern)
    grad_tile, right, lower, corner, grad, light = run_slots(
        rows, cols, boxes, offsets, counts, object_slab, right, lower, corner, probe_mode_stack, measured, *tables(pattern)
    )
    return run_share(rows, cols, object_slab, right, lower, corner, grad_tile, grad, light, probe_mode_stack)


def solution(mesh):
    in_specs = (
        P(None, None, "obj", "scan"),
        P(),
        P(("obj", "scan"), None),
        P(("obj", "scan"), None, None),
        P(("obj", "scan")),
    )
    out_specs = (P(None, None, "obj", "scan"), P())
    return jax.shard_map(
        on_device, mesh=mesh, in_specs=in_specs, out_specs=out_specs, check_vma=False
    )
```

```python
import functools
import math

import jax
import jax.numpy as jnp
import numpy as np
from jax import lax
from jax.experimental import pallas as pl
from jax.experimental.pallas import tpu as pltpu
from jax.sharding import PartitionSpec as P

chirp_scale = 24.0
probe_step = 0.15
lanes = 128
sublanes = 8


def dft_parts(pattern):
    indices = np.arange(pattern)
    angles = (indices[:, None] * indices[None, :] % pattern) * (2.0 * math.pi / pattern)
    parts = (np.cos(angles) / math.sqrt(pattern), np.sin(angles) / math.sqrt(pattern))
    return [part.astype(np.float32).astype(jnp.bfloat16).astype(np.float64) for part in parts]


def block_matrix(real_part, imag_part):
    upper = np.concatenate([real_part, -imag_part], axis=1)
    lower = np.concatenate([imag_part, real_part], axis=1)
    return jnp.asarray(np.concatenate([upper, lower], axis=0).astype(np.float32), jnp.bfloat16)


def tables(pattern):
    cos, sin = dft_parts(pattern)
    indices = np.arange(pattern)
    freqs = ((indices + pattern // 2) % pattern - pattern // 2) / pattern
    chirp = np.exp(-1j * math.pi * chirp_scale * freqs**2)
    hop = (cos + 1j * sin) @ (chirp[:, None] * (cos - 1j * sin))
    return (
        block_matrix(cos, -sin), block_matrix(cos, sin),
        block_matrix(hop.real, hop.imag), block_matrix(hop.real, -hop.imag),
    )


def aligned(row, col):
    row_base = pl.multiple_of(row // sublanes * sublanes, sublanes)
    col_base = pl.multiple_of(col // lanes * lanes, lanes)
    return row_base, col_base, row - row_base, col - col_base


def pad(array):
    array = jnp.concatenate([array, jnp.zeros((array.shape[0], lanes), jnp.float32)], axis=1)
    return jnp.concatenate([array, jnp.zeros((sublanes, array.shape[1]), jnp.float32)], axis=0)


def roll_down(array, rows, cols):
    return pltpu.roll(pltpu.roll(array, cols, 1), rows, 0)


def transform(real_part, imag_part, left, right):
    pattern = real_part.shape[0]
    stacked = jnp.concatenate([real_part.astype(jnp.bfloat16), imag_part.astype(jnp.bfloat16)], axis=0)
    half = jnp.dot(left, stacked, preferred_element_type=jnp.float32).astype(jnp.bfloat16)
    half = jnp.concatenate([half[:pattern], half[pattern:]], axis=1)
    full = jnp.dot(half, right, preferred_element_type=jnp.float32)
    return full[:, :pattern], full[:, pattern:]


MESH = pl.DeviceIdType.MESH


def place():
    return lax.axis_index("obj"), lax.axis_index("scan")


def greet(partners):
    barrier = pltpu.get_barrier_semaphore()
    for exists, device in partners:

        @pl.when(exists)
        def _(device=device):
            pl.semaphore_signal(barrier, inc=1, device_id=device, device_id_type=MESH)

    count = 0
    for exists, _ in partners:
        count = count + (1 if exists is True else jnp.where(exists, 1, 0))
    pl.semaphore_wait(barrier, count)


def neighbours(rows, cols):
    row, col = place()
    return {
        "up": (row > 0, (row - 1, col)),
        "down": (row < rows - 1, (row + 1, col)),
        "left": (col > 0, (row, col - 1)),
        "right": (col < cols - 1, (row, col + 1)),
    }


def digits(rows, cols):
    return {
        "core": ("obj", 1, 2),
        "y": ("obj", 2, rows // 2),
        "x": ("scan", 1, 2),
        "z": ("scan", 2, cols // 2),
    }


def member(digit, by):
    axis, stride, radix = digit
    row, col = place()
    at = row if axis == "obj" else col
    mine = at // stride % radix
    theirs = (mine + by) % radix
    there = at + (theirs - mine) * stride
    return mine, theirs, ((there, col) if axis == "obj" else (row, there))


def group(digit):
    return [(True, member(digit, by)[2]) for by in range(1, digit[2])]


streams = (
    (0, 0, 2, ("x", "y", "z")),
    (1, 0, 2, ("y", "x", "z")),
    (2, 0, 1, ("x", "z", "y")),
    (2, 1, 1, ("y", "z", "x")),
)


class Reduction:
    def __init__(self, rows, cols, grad, total, held, landed, core_in, sems):
        self.ways = digits(rows, cols)
        self.grad, self.total, self.held, self.landed, self.core_in = grad, total, held, landed, core_in
        self.sent, self.got = sems
        self.count = 0
        self.pending = []
        self.share = grad.shape[0] // 2
        self.state = [[0, grad.shape[1]] for _ in streams]
        self.waits = [[] for _ in streams]
        self.landing = [0 for _ in streams]

    def copy(self, source, target, device):
        k = self.count
        self.count += 1
        made = pltpu.make_async_remote_copy(
            src_ref=source, dst_ref=target, send_sem=self.sent.at[k], recv_sem=self.got.at[k],
            device_id=device, device_id_type=MESH,
        )
        made.start()
        self.pending.append(made)
        return made

    def core_send(self, k):
        mine, theirs, device = member(self.ways["core"], 1)
        self.core_waits = getattr(self, "core_waits", {})
        self.core_waits[k] = self.copy(self.grad.at[theirs * self.share + k], self.core_in.at[k], device)

    def core_add(self, k):
        mine, _, _ = member(self.ways["core"], 1)
        self.core_waits[k].wait_recv()
        self.held[k] = self.grad[mine * self.share + k] + self.core_in[k]

    def lanes_of(self, s):
        return pl.ds(streams[s][1] * lanes, streams[s][2] * lanes)

    def scatter_send(self, s, step):
        mode = streams[s][0]
        digit = self.ways[streams[s][3][step]]
        start, size = self.state[s]
        part = size // digit[2]
        self.waits[s] = []
        for by in range(1, digit[2]):
            _, theirs, device = member(digit, by)
            spot = self.landed.at[mode, pl.ds(self.landing[s], part), self.lanes_of(s)]
            source = self.held.at[mode, pl.ds(pl.multiple_of(start + theirs * part, sublanes), part), self.lanes_of(s)]
            self.waits[s].append((self.copy(source, spot, device), self.landing[s]))
            self.landing[s] += part

    def scatter_add(self, s, step):
        mode = streams[s][0]
        digit = self.ways[streams[s][3][step]]
        start, size = self.state[s]
        part = size // digit[2]
        if digit[2] > 1:
            mine, _, _ = member(digit, 1)
            start = start + mine * part
        self.state[s] = [start, part]
        span = pl.ds(pl.multiple_of(start, sublanes), part)
        value = self.held[mode, span, self.lanes_of(s)]
        for made, landing in self.waits[s]:
            made.wait_recv()
            value = value + self.landed[mode, pl.ds(landing, part), self.lanes_of(s)]
        if step == 2:
            own = member(self.ways["core"], 1)[0] * self.share + mode
            self.total[own, span, self.lanes_of(s)] = value
        else:
            self.held[mode, span, self.lanes_of(s)] = value

    def gather_send(self, s, step):
        mode = streams[s][0]
        digit = self.ways[streams[s][3][step]]
        start, size = self.state[s]
        own = member(self.ways["core"], 1)[0] * self.share + mode
        self.waits[s] = []
        for by in range(1, digit[2]):
            spot = self.total.at[own, pl.ds(pl.multiple_of(start, sublanes), size), self.lanes_of(s)]
            self.waits[s].append(self.copy(spot, spot, member(digit, by)[2]))

    def gather_wait(self, s, step):
        digit = self.ways[streams[s][3][step]]
        start, size = self.state[s]
        for made in self.waits[s]:
            made.wait_recv()
        if digit[2] > 1:
            start = start - member(digit, 1)[0] * size
        self.state[s] = [start, size * digit[2]]

    def core_share(self, s):
        mine, _, device = member(self.ways["core"], 1)
        spot = self.total.at[mine * self.share + streams[s][0], :, self.lanes_of(s)]
        self.waits[s] = [self.copy(spot, spot, device)]


def when(conditions, action):
    pl.when(functools.reduce(jnp.logical_and, conditions))(action)


def rims_kernel(rows, cols, tile, info, right, lower, corner, boxes, sent, got, sent_box, got_box, sem):
    near = neighbours(rows, cols)
    row, col = place()
    layers, pattern = tile.shape[0], corner.shape[-1]
    height = tile.shape[2]
    has_up, up = near["up"]
    has_down, down = near["down"]
    has_left, left = near["left"]
    has_right, far_right = near["right"]
    after = (jnp.logical_and(has_down, has_right), (row + 1, col + 1))
    before = (jnp.logical_and(has_up, has_left), (row - 1, col - 1))
    keep = pltpu.make_async_copy(info, boxes.at[0], sem.at[0])
    keep.start()
    greet(list(near.values()) + [after, before])

    def copy(source, target, k, device, sems=(sent, got)):
        return pltpu.make_async_remote_copy(
            src_ref=source, dst_ref=target, send_sem=sems[0].at[k], recv_sem=sems[1].at[k],
            device_id=device, device_id_type=MESH,
        )

    top, rest = pl.ds(0, pattern), pl.ds(pattern, height - pattern)
    first = pl.ds(0, pattern)
    each = range(layers)
    tops = [copy(tile.at[n, :, top, first], right.at[n, :, top], 4 * n, left) for n in each]
    rests = [copy(tile.at[n, :, rest, first], right.at[n, :, rest], 4 * n + 1, left) for n in each]
    lowers = [copy(tile.at[n, :, top], lower.at[n], 4 * n + 2, up) for n in each]
    corners = [copy(right.at[n, :, top], corner.at[n], 4 * n + 3, up) for n in each]
    tell = [
        (has_right, has_left, copy(info, boxes.at[1], 0, far_right, (sent_box, got_box))),
        (has_down, has_up, copy(info, boxes.at[2], 1, down, (sent_box, got_box))),
        (after[0], before[0], copy(info, boxes.at[3], 2, after[1], (sent_box, got_box))),
    ]
    for to, _, box in tell:
        when([to], box.start)
    for n in each:
        when([has_left], tops[n].start)
        when([has_up], lowers[n].start)
    for n in each:
        when([has_left], rests[n].start)
    keep.wait()
    for k, (to, there, box) in enumerate(tell):
        when([there], box.wait_recv)

        @pl.when(jnp.logical_not(there))
        def _(k=k):
            boxes[k + 1] = jnp.zeros(boxes.shape[1:], jnp.int32)

        when([to], box.wait_send)
    for n in each:
        when([has_right], tops[n].wait_recv)
        when([has_right, has_up], corners[n].start)
    for n in each:
        when([has_right], rests[n].wait_recv)
        when([has_right, has_down], corners[n].wait_recv)
        when([has_right, has_up], corners[n].wait_send)
        when([has_down], lowers[n].wait_recv)
        when([has_left], tops[n].wait_send)
        when([has_left], rests[n].wait_send)
        when([has_up], lowers[n].wait_send)


def run_rims(rows, cols, tile, info, pattern):
    layers, _, height, width = tile.shape
    anyw = pl.BlockSpec(memory_space=pl.ANY)
    vmem = pl.BlockSpec(memory_space=pltpu.VMEM)
    f32, dma = jnp.float32, pltpu.SemaphoreType.DMA
    return pl.pallas_call(
        functools.partial(rims_kernel, rows, cols),
        out_shape=(
            jax.ShapeDtypeStruct((layers, 2, height, pattern), f32),
            jax.ShapeDtypeStruct((layers, 2, pattern, width), f32),
            jax.ShapeDtypeStruct((layers, 2, pattern, pattern), f32),
            jax.ShapeDtypeStruct((4,) + info.shape, jnp.int32),
        ),
        in_specs=[anyw, vmem],
        out_specs=(anyw, anyw, anyw, vmem),
        scratch_shapes=[dma((4 * layers,)), dma((4 * layers,)), dma((3,)), dma((3,)), dma((1,))],
        compiler_params=pltpu.CompilerParams(collective_id=0, has_side_effects=True),
        cost_estimate=pl.CostEstimate(flops=0, bytes_accessed=10_000_000, transcendentals=0),
    )(tile, info)


def slots_kernel(
    rows, cols, boxes, offsets, used, tile, right, lower, corner, probe_in, measured_in, table_f_in, table_b_in, hop_f_in, hop_b_in,
    grad_tile, grad_right, grad_lower, grad_corner, grad, light,
    ext0, ext1, window, waves, far, back, term, canvas, probe, measured, table_f, table_b, hop_f, hop_b, intensity,
    sems_in, sems_out,
):
    bf16 = jnp.bfloat16
    modes, pattern = probe.shape[0], probe.shape[-1]
    slots = offsets.shape[0]
    height, width = tile.shape[2], tile.shape[3]
    wide, tall = pattern + lanes, pattern + sublanes
    exts = (ext0, ext1)
    row, col = place()
    first, second = pl.ds(0, pattern), pl.ds(pattern, pattern)

    def spots(n):
        return (
            exts[n].at[:, pl.ds(0, height), pl.ds(0, width)],
            exts[n].at[:, pl.ds(0, height), pl.ds(width, pattern)],
            exts[n].at[:, pl.ds(height, pattern), pl.ds(0, width)],
            exts[n].at[:, pl.ds(height, pattern), pl.ds(width, pattern)],
        )

    moves = [(probe_in, probe)]
    moves += [(array.at[0], spot) for array, spot in zip((tile, right, lower, corner), spots(0))]
    moves += [(hop_f_in, hop_f), (hop_b_in, hop_b)]
    moves += [(array.at[1], spot) for array, spot in zip((tile, right, lower, corner), spots(1))]
    moves += [(table_f_in, table_f), (table_b_in, table_b), (measured_in, measured)]
    loads = [pltpu.make_async_copy(a, b, sems_in.at[k]) for k, (a, b) in enumerate(moves)]
    for load in loads:
        load.start()

    canvas[...] = jnp.zeros_like(canvas)
    loads[0].wait()
    power = jnp.zeros((pattern, pattern), jnp.float32)
    for mode in range(modes):
        power = power + (probe[mode, 0] * probe[mode, 0] + probe[mode, 1] * probe[mode, 1])
    intensity[...] = power
    for block in range(4):

        @pl.loop(0, boxes[block, 0, 2 * slots])
        def _(slot, block=block):
            at_row = boxes[block, 0, 2 * slot] - row * height + height
            at_col = boxes[block, 0, 2 * slot + 1] - col * width + width
            row_base, col_base, row_shift, col_shift = aligned(at_row, at_col)
            at = (pl.ds(row_base, tall), pl.ds(col_base, wide))
            canvas[at] = canvas[at] + roll_down(pad(intensity[...]), row_shift, col_shift)

    light[...] = canvas[height : 2 * height, width : 2 * width] + 1.0

    def bases(slot):
        return aligned(offsets[slot, 0] - row * height, offsets[slot, 1] - col * width)

    def cut(n):
        @pl.loop(0, used[0])
        def _(slot):
            row_base, col_base, row_shift, col_shift = bases(slot)
            row_back = jnp.where(row_shift == 0, 0, tall - row_shift)
            col_back = jnp.where(col_shift == 0, 0, wide - col_shift)
            for part in range(2):
                block = exts[n][part, pl.ds(row_base, tall), pl.ds(col_base, wide)]
                window[slot, n, part] = roll_down(block, row_back, col_back)[:pattern, :pattern]

    def spread(n, slot):
        row_base, col_base, row_shift, col_shift = bases(slot)
        for part in range(2):
            at = (part, pl.ds(row_base, tall), pl.ds(col_base, wide))
            exts[n][at] = exts[n][at] + roll_down(pad(term[part]), row_shift, col_shift)

    def save(n):
        return [
            pltpu.make_async_copy(spot, target.at[n], sems_out.at[4 * n + k])
            for k, (spot, target) in enumerate(zip(spots(n), (grad_tile, grad_right, grad_lower, grad_corner)))
        ]

    for k in range(1, 7):
        loads[k].wait()
    cut(0)
    exts[0][...] = jnp.zeros_like(exts[0])

    @pl.loop(0, used[0])
    def _(slot):
        @pl.loop(0, modes, unroll=3)
        def _(mode):
            wr, wi = probe[mode, 0], probe[mode, 1]
            o_r, o_i = window[slot, 0, 0], window[slot, 0, 1]
            wr, wi = transform(o_r * wr - o_i * wi, o_r * wi + o_i * wr, hop_f[...], hop_b[...])
            waves[slot, mode, 0] = wr
            waves[slot, mode, 1] = wi

    for k in range(7, len(moves)):
        loads[k].wait()
    cut(1)
    exts[1][...] = jnp.zeros_like(exts[1])

    @pl.loop(0, used[0])
    def _(slot):
        intensity[...] = -measured[slot]
        term[...] = jnp.zeros_like(term)

        @pl.loop(0, modes, unroll=3)
        def _(mode):
            wr, wi = waves[slot, mode, 0], waves[slot, mode, 1]
            o_r, o_i = window[slot, 1, 0], window[slot, 1, 1]
            fr, fi = transform(o_r * wr - o_i * wi, o_r * wi + o_i * wr, table_f[...], table_b[...])
            far[mode, 0] = fr
            far[mode, 1] = fi
            intensity[...] += fr * fr + fi * fi

        @pl.loop(0, modes, unroll=3)
        def _(mode):
            gain = intensity[...]
            gr, gi = transform(gain * far[mode, 0], gain * far[mode, 1], table_b[...], table_f[...])
            wr, wi = waves[slot, mode, 0], waves[slot, mode, 1]
            term[0] += wr * gr + wi * gi
            term[1] += wr * gi - wi * gr
            o_r, o_i = window[slot, 1, 0], window[slot, 1, 1]
            back[slot, mode, 0] = (o_r * gr + o_i * gi).astype(bf16)
            back[slot, mode, 1] = (o_r * gi - o_i * gr).astype(bf16)

        spread(1, slot)

    saves = save(1)
    for one in saves:
        one.start()
    grad[...] = jnp.zeros_like(grad)

    @pl.loop(0, used[0])
    def _(slot):
        term[...] = jnp.zeros_like(term)

        @pl.loop(0, modes, unroll=3)
        def _(mode):
            gr, gi = transform(back[slot, mode, 0], back[slot, mode, 1], hop_b[...], hop_f[...])
            wr, wi = probe[mode, 0], probe[mode, 1]
            term[0] += wr * gr + wi * gi
            term[1] += wr * gi - wi * gr
            o_r, o_i = window[slot, 0, 0], window[slot, 0, 1]
            grad[mode, first] += o_r * gr + o_i * gi
            grad[mode, second] += o_r * gi - o_i * gr

        spread(0, slot)

    last = save(0)
    for one in last:
        one.start()
    for one in saves + last:
        one.wait()


def run_slots(rows, cols, boxes, offsets, used, tile, right, lower, corner, probe, measured, *matrices):
    layers, _, height, width = tile.shape
    modes, _, pattern, _ = probe.shape
    slots = offsets.shape[0]
    smem = pl.BlockSpec(memory_space=pltpu.SMEM)
    vmem = pl.BlockSpec(memory_space=pltpu.VMEM)
    anyw = pl.BlockSpec(memory_space=pl.ANY)
    f32, bf16 = jnp.float32, jnp.bfloat16
    space, dma = pltpu.VMEM, pltpu.SemaphoreType.DMA
    ext = (2, height + pattern, width + pattern)
    return pl.pallas_call(
        functools.partial(slots_kernel, rows, cols),
        out_shape=(
            jax.ShapeDtypeStruct(tile.shape, f32),
            jax.ShapeDtypeStruct(right.shape, f32),
            jax.ShapeDtypeStruct(lower.shape, f32),
            jax.ShapeDtypeStruct(corner.shape, f32),
            jax.ShapeDtypeStruct((modes, 2 * pattern, pattern), f32),
            jax.ShapeDtypeStruct((height, width), f32),
        ),
        in_specs=[smem, smem, smem] + [anyw] * 10,
        out_specs=(anyw, anyw, anyw, anyw, vmem, vmem),
        scratch_shapes=[
            space(ext, f32), space(ext, f32),
            space((slots, layers, 2, pattern, pattern), f32),
            space((slots, modes, 2, pattern, pattern), f32),
            space((modes, 2, pattern, pattern), f32),
            space((slots, modes, 2, pattern, pattern), bf16),
            space((2, pattern, pattern), f32),
            space((2 * height + pattern, 2 * width + pattern), f32),
            space(probe.shape, f32), space(measured.shape, f32),
            *[space((2 * pattern, 2 * pattern), bf16) for _ in range(4)],
            space((pattern, pattern), f32),
            dma((14,)), dma((8,)),
        ],
        compiler_params=pltpu.CompilerParams(vmem_limit_bytes=58 * 1024 * 1024),
        cost_estimate=pl.CostEstimate(flops=20_000_000_000, bytes_accessed=30_000_000, transcendentals=0),
    )(boxes, offsets, used, tile, right, lower, corner, probe, measured, *matrices)


def share_kernel(
    rows, cols, tile, right, lower, corner, grad_tile, grad, light, probe_in, new_object, total,
    side, inner, left_in, above_in, edge, held, landed, core_in, probe, sems_in, sent_halo, got_halo, sent, got,
):
    near = neighbours(rows, cols)
    ways = digits(rows, cols)
    partners = list(near.values())
    for digit in ways.values():
        partners += group(digit)
    layers, pattern = right.shape[0], corner.shape[-1]
    height, width = tile.shape[2], tile.shape[3]
    modes = grad.shape[0]
    each = range(layers)
    first, second = pl.ds(0, pattern), pl.ds(pattern, pattern)
    moves = [(right, side), (tile, new_object), (grad_tile, inner), (probe_in, probe)]
    loads = [pltpu.make_async_copy(a, b, sems_in.at[k]) for k, (a, b) in enumerate(moves)]
    for load in loads:
        load.start()
    greet(partners)
    has_up, up = near["up"]
    has_down, down = near["down"]
    has_left, _ = near["left"]
    has_right, far_right = near["right"]

    def copy(source, target, k, device):
        return pltpu.make_async_remote_copy(
            src_ref=source, dst_ref=target, send_sem=sent_halo.at[k], recv_sem=got_halo.at[k],
            device_id=device, device_id_type=MESH,
        )

    top, rest = pl.ds(0, pattern), pl.ds(pattern, height - pattern)
    tops = [copy(side.at[n, :, top], left_in.at[n, :, top], 4 * n, far_right) for n in each]
    rests = [copy(side.at[n, :, rest], left_in.at[n, :, rest], 4 * n + 1, far_right) for n in each]
    lowers = [copy(lower.at[n], above_in.at[n], 4 * n + 2, down) for n in each]
    corners = [copy(corner.at[n], edge.at[n], 4 * n + 3, down) for n in each]
    reduction = Reduction(rows, cols, grad, total, held, landed, core_in, (sent, got))

    def add_corner(n):
        @pl.when(jnp.logical_and(has_right, has_up))
        def _():
            corners[n].wait_recv()
            side[n, :, :pattern] = side[n, :, :pattern] + edge[n]

        when([has_right], tops[n].start)

    def finish(n):
        @pl.when(has_left)
        def _():
            rests[n].wait_recv()
            tops[n].wait_recv()

        @pl.when(jnp.logical_not(has_left))
        def _():
            left_in[n] = jnp.zeros(left_in.shape[1:], jnp.float32)

        when([has_up], lowers[n].wait_recv)

        @pl.when(jnp.logical_not(has_up))
        def _():
            above_in[n] = jnp.zeros(above_in.shape[1:], jnp.float32)

        inner[n, :, :, :pattern] += left_in[n]
        inner[n, :, :pattern, :] += above_in[n]
        for part in range(2):
            new_object[n, part] = new_object[n, part] - inner[n, part] / light[...]

    every = range(len(streams))
    for k in range(reduction.share):
        reduction.core_send(k)
    when([has_down, has_right], corners[0].start)
    loads[0].wait()
    when([has_right], rests[0].start)
    for k in range(reduction.share):
        reduction.core_add(k)
        for s in every:
            if streams[s][0] == k:
                reduction.scatter_send(s, 0)
    when([has_down, has_right], corners[1].start)
    when([has_right], rests[1].start)
    for s in every:
        reduction.scatter_add(s, 0)
        reduction.scatter_send(s, 1)
    add_corner(0)
    when([has_down], lowers[0].start)
    for s in every:
        reduction.scatter_add(s, 1)
        reduction.scatter_send(s, 2)
    for s in every:
        reduction.scatter_add(s, 2)
        reduction.gather_send(s, 2)
    add_corner(1)
    when([has_down], lowers[1].start)
    for s in every:
        reduction.gather_wait(s, 2)
        reduction.gather_send(s, 1)
    loads[1].wait()
    loads[2].wait()
    for s in every:
        reduction.gather_wait(s, 1)
        reduction.gather_send(s, 0)
    finish(0)
    for s in every:
        reduction.gather_wait(s, 0)
        reduction.core_share(s)
    finish(1)
    for s in range(len(streams)):
        for made in reduction.waits[s]:
            made.wait_recv()
    for made in reduction.pending:
        made.wait_send()
    for n in each:
        when([has_right], rests[n].wait_send)
        when([has_right], tops[n].wait_send)
        when([has_down, has_right], corners[n].wait_send)
        when([has_down], lowers[n].wait_send)
    loads[3].wait()
    squares = jnp.zeros((pattern, pattern), jnp.float32)
    for mode in range(modes):
        squares = squares + (total[mode, first] * total[mode, first] + total[mode, second] * total[mode, second])
    count = modes * 2 * pattern * pattern
    scale = jnp.sqrt(jnp.broadcast_to(jnp.sum(squares), (pattern, pattern)) * (1.0 / count) + 1e-06)
    factor = probe_step / scale
    for mode in range(modes):
        total[mode, first] = probe[mode, 0] - factor * total[mode, first]
        total[mode, second] = probe[mode, 1] - factor * total[mode, second]


def run_share(rows, cols, tile, right, lower, corner, grad_tile, grad, light, probe):
    layers = right.shape[0]
    pattern = corner.shape[-1]
    modes = grad.shape[0]
    anyw = pl.BlockSpec(memory_space=pl.ANY)
    vmem = pl.BlockSpec(memory_space=pltpu.VMEM)
    f32, space, dma = jnp.float32, pltpu.VMEM, pltpu.SemaphoreType.DMA
    half = (modes // 2, 2 * pattern, pattern)
    count = modes // 2 + len(streams) * (2 * sum(way[2] - 1 for way in digits(rows, cols).values()) - 1)
    new_object, new_probe = pl.pallas_call(
        functools.partial(share_kernel, rows, cols),
        out_shape=(
            jax.ShapeDtypeStruct(tile.shape, f32),
            jax.ShapeDtypeStruct((modes, 2 * pattern, pattern), f32),
        ),
        in_specs=[anyw, anyw, anyw, anyw, anyw, vmem, vmem, anyw],
        out_specs=(vmem, vmem),
        scratch_shapes=[
            space(right.shape, f32), space(tile.shape, f32), space(right.shape, f32), space(lower.shape, f32),
            space(corner.shape, f32), space(half, f32), space(half, f32), space(half, f32), space(probe.shape, f32),
            dma((4,)), dma((4 * layers,)), dma((4 * layers,)), dma((count,)), dma((count,)),
        ],
        compiler_params=pltpu.CompilerParams(
            collective_id=1, has_side_effects=True, vmem_limit_bytes=60 * 1024 * 1024
        ),
        cost_estimate=pl.CostEstimate(flops=0, bytes_accessed=30_000_000, transcendentals=0),
    )(tile, right, lower, corner, grad_tile, grad, light, probe)
    return new_object, new_probe.reshape(probe.shape)


def on_device(object_slab, probe_mode_stack, offsets, measured, counts):
    pattern = probe_mode_stack.shape[-1]
    rows, cols = lax.axis_size("obj"), lax.axis_size("scan")
    info = jnp.concatenate([offsets.reshape(-1), counts])
    info = jnp.pad(info[None], ((0, sublanes - 1), (0, lanes - info.shape[0])))
    right, lower, corner, boxes = run_rims(rows, cols, object_slab, info, pattern)
    grad_tile, right, lower, corner, grad, light = run_slots(
        rows, cols, boxes, offsets, counts, object_slab, right, lower, corner, probe_mode_stack, measured, *tables(pattern)
    )
    return run_share(rows, cols, object_slab, right, lower, corner, grad_tile, grad, light, probe_mode_stack)


def solution(mesh):
    in_specs = (
        P(None, None, "obj", "scan"),
        P(),
        P(("obj", "scan"), None),
        P(("obj", "scan"), None, None),
        P(("obj", "scan")),
    )
    out_specs = (P(None, None, "obj", "scan"), P())
    return jax.shard_map(
        on_device, mesh=mesh, in_specs=in_specs, out_specs=out_specs, check_vma=False
    )
```

```python
import functools
import math

import jax
import jax.numpy as jnp
import numpy as np
from jax import lax
from jax.experimental import pallas as pl
from jax.experimental.pallas import tpu as pltpu
from jax.sharding import PartitionSpec as P

chirp_scale = 24.0
probe_step = 0.15
lanes = 128
sublanes = 8


def dft_parts(pattern):
    indices = np.arange(pattern)
    angles = (indices[:, None] * indices[None, :] % pattern) * (2.0 * math.pi / pattern)
    parts = (np.cos(angles) / math.sqrt(pattern), np.sin(angles) / math.sqrt(pattern))
    return [part.astype(np.float32).astype(jnp.bfloat16).astype(np.float64) for part in parts]


def block_matrix(real_part, imag_part):
    upper = np.concatenate([real_part, -imag_part], axis=1)
    lower = np.concatenate([imag_part, real_part], axis=1)
    return jnp.asarray(np.concatenate([upper, lower], axis=0).astype(np.float32), jnp.bfloat16)


def tables(pattern):
    cos, sin = dft_parts(pattern)
    indices = np.arange(pattern)
    freqs = ((indices + pattern // 2) % pattern - pattern // 2) / pattern
    chirp = np.exp(-1j * math.pi * chirp_scale * freqs**2)
    hop = (cos + 1j * sin) @ (chirp[:, None] * (cos - 1j * sin))
    return (
        block_matrix(cos, -sin), block_matrix(cos, sin),
        block_matrix(hop.real, hop.imag), block_matrix(hop.real, -hop.imag),
    )


def aligned(row, col):
    row_base = pl.multiple_of(row // sublanes * sublanes, sublanes)
    col_base = pl.multiple_of(col // lanes * lanes, lanes)
    return row_base, col_base, row - row_base, col - col_base


def pad(array):
    array = jnp.concatenate([array, jnp.zeros((array.shape[0], lanes), jnp.float32)], axis=1)
    return jnp.concatenate([array, jnp.zeros((sublanes, array.shape[1]), jnp.float32)], axis=0)


def roll_down(array, rows, cols):
    return pltpu.roll(pltpu.roll(array, cols, 1), rows, 0)


def transform(real_part, imag_part, left, right):
    pattern = real_part.shape[0]
    stacked = jnp.concatenate([real_part.astype(jnp.bfloat16), imag_part.astype(jnp.bfloat16)], axis=0)
    half = jnp.dot(left, stacked, preferred_element_type=jnp.float32).astype(jnp.bfloat16)
    half = jnp.concatenate([half[:pattern], half[pattern:]], axis=1)
    full = jnp.dot(half, right, preferred_element_type=jnp.float32)
    return full[:, :pattern], full[:, pattern:]


MESH = pl.DeviceIdType.MESH


def place():
    return lax.axis_index("obj"), lax.axis_index("scan")


def greet(partners):
    barrier = pltpu.get_barrier_semaphore()
    for exists, device in partners:

        @pl.when(exists)
        def _(device=device):
            pl.semaphore_signal(barrier, inc=1, device_id=device, device_id_type=MESH)

    count = 0
    for exists, _ in partners:
        count = count + (1 if exists is True else jnp.where(exists, 1, 0))
    pl.semaphore_wait(barrier, count)


def neighbours(rows, cols):
    row, col = place()
    return {
        "up": (row > 0, (row - 1, col)),
        "down": (row < rows - 1, (row + 1, col)),
        "left": (col > 0, (row, col - 1)),
        "right": (col < cols - 1, (row, col + 1)),
    }


def digits(rows, cols):
    return {
        "core": ("obj", 1, 2),
        "y": ("obj", 2, rows // 2),
        "x": ("scan", 1, 2),
        "z": ("scan", 2, cols // 2),
    }


def member(digit, by):
    axis, stride, radix = digit
    row, col = place()
    at = row if axis == "obj" else col
    mine = at // stride % radix
    theirs = (mine + by) % radix
    there = at + (theirs - mine) * stride
    return mine, theirs, ((there, col) if axis == "obj" else (row, there))


def group(digit):
    return [(True, member(digit, by)[2]) for by in range(1, digit[2])]


streams = (
    (0, 0, 2, ("x", "y", "z")),
    (1, 0, 2, ("y", "x", "z")),
    (2, 0, 1, ("x", "z", "y")),
    (2, 1, 1, ("y", "z", "x")),
)


class Reduction:
    def __init__(self, rows, cols, grad, total, held, landed, core_in, sems):
        self.ways = digits(rows, cols)
        self.grad, self.total, self.held, self.landed, self.core_in = grad, total, held, landed, core_in
        self.sent, self.got = sems
        self.count = 0
        self.pending = []
        self.share = grad.shape[0] // 2
        self.state = [[0, grad.shape[1]] for _ in streams]
        self.waits = [[] for _ in streams]
        self.landing = [0 for _ in streams]

    def copy(self, source, target, device):
        k = self.count
        self.count += 1
        made = pltpu.make_async_remote_copy(
            src_ref=source, dst_ref=target, send_sem=self.sent.at[k], recv_sem=self.got.at[k],
            device_id=device, device_id_type=MESH,
        )
        made.start()
        self.pending.append(made)
        return made

    def core_send(self, k):
        mine, theirs, device = member(self.ways["core"], 1)
        self.core_waits = getattr(self, "core_waits", {})
        self.core_waits[k] = self.copy(self.grad.at[theirs * self.share + k], self.core_in.at[k], device)

    def core_add(self, k):
        mine, _, _ = member(self.ways["core"], 1)
        self.core_waits[k].wait_recv()
        self.held[k] = self.grad[mine * self.share + k] + self.core_in[k]

    def lanes_of(self, s):
        return pl.ds(streams[s][1] * lanes, streams[s][2] * lanes)

    def scatter_send(self, s, step):
        mode = streams[s][0]
        digit = self.ways[streams[s][3][step]]
        start, size = self.state[s]
        part = size // digit[2]
        self.waits[s] = []
        for by in range(1, digit[2]):
            _, theirs, device = member(digit, by)
            spot = self.landed.at[mode, pl.ds(self.landing[s], part), self.lanes_of(s)]
            source = self.held.at[mode, pl.ds(pl.multiple_of(start + theirs * part, sublanes), part), self.lanes_of(s)]
            self.waits[s].append((self.copy(source, spot, device), self.landing[s]))
            self.landing[s] += part

    def scatter_add(self, s, step):
        mode = streams[s][0]
        digit = self.ways[streams[s][3][step]]
        start, size = self.state[s]
        part = size // digit[2]
        if digit[2] > 1:
            mine, _, _ = member(digit, 1)
            start = start + mine * part
        self.state[s] = [start, part]
        span = pl.ds(pl.multiple_of(start, sublanes), part)
        value = self.held[mode, span, self.lanes_of(s)]
        for made, landing in self.waits[s]:
            made.wait_recv()
            value = value + self.landed[mode, pl.ds(landing, part), self.lanes_of(s)]
        if step == 2:
            own = member(self.ways["core"], 1)[0] * self.share + mode
            self.total[own, span, self.lanes_of(s)] = value
        else:
            self.held[mode, span, self.lanes_of(s)] = value

    def gather_send(self, s, step):
        mode = streams[s][0]
        digit = self.ways[streams[s][3][step]]
        start, size = self.state[s]
        own = member(self.ways["core"], 1)[0] * self.share + mode
        self.waits[s] = []
        for by in range(1, digit[2]):
            spot = self.total.at[own, pl.ds(pl.multiple_of(start, sublanes), size), self.lanes_of(s)]
            self.waits[s].append(self.copy(spot, spot, member(digit, by)[2]))

    def gather_wait(self, s, step):
        digit = self.ways[streams[s][3][step]]
        start, size = self.state[s]
        for made in self.waits[s]:
            made.wait_recv()
        if digit[2] > 1:
            start = start - member(digit, 1)[0] * size
        self.state[s] = [start, size * digit[2]]

    def core_share(self, s):
        mine, _, device = member(self.ways["core"], 1)
        spot = self.total.at[mine * self.share + streams[s][0], :, self.lanes_of(s)]
        self.waits[s] = [self.copy(spot, spot, device)]


def when(conditions, action):
    pl.when(functools.reduce(jnp.logical_and, conditions))(action)


def rims_kernel(rows, cols, tile, info, right, lower, corner, boxes, sent, got, sent_box, got_box, sem):
    near = neighbours(rows, cols)
    row, col = place()
    layers, pattern = tile.shape[0], corner.shape[-1]
    height = tile.shape[2]
    has_up, up = near["up"]
    has_down, down = near["down"]
    has_left, left = near["left"]
    has_right, far_right = near["right"]
    after = (jnp.logical_and(has_down, has_right), (row + 1, col + 1))
    before = (jnp.logical_and(has_up, has_left), (row - 1, col - 1))
    keep = pltpu.make_async_copy(info, boxes.at[0], sem.at[0])
    keep.start()
    greet(list(near.values()) + [after, before])

    def copy(source, target, k, device, sems=(sent, got)):
        return pltpu.make_async_remote_copy(
            src_ref=source, dst_ref=target, send_sem=sems[0].at[k], recv_sem=sems[1].at[k],
            device_id=device, device_id_type=MESH,
        )

    top, rest = pl.ds(0, pattern), pl.ds(pattern, height - pattern)
    first = pl.ds(0, pattern)
    each = range(layers)
    tops = [copy(tile.at[n, :, top, first], right.at[n, :, top], 4 * n, left) for n in each]
    rests = [copy(tile.at[n, :, rest, first], right.at[n, :, rest], 4 * n + 1, left) for n in each]
    lowers = [copy(tile.at[n, :, top], lower.at[n], 4 * n + 2, up) for n in each]
    corners = [copy(right.at[n, :, top], corner.at[n], 4 * n + 3, up) for n in each]
    tell = [
        (has_right, has_left, copy(info, boxes.at[1], 0, far_right, (sent_box, got_box))),
        (has_down, has_up, copy(info, boxes.at[2], 1, down, (sent_box, got_box))),
        (after[0], before[0], copy(info, boxes.at[3], 2, after[1], (sent_box, got_box))),
    ]
    for to, _, box in tell:
        when([to], box.start)
    for n in each:
        when([has_left], tops[n].start)
        when([has_up], lowers[n].start)
    for n in each:
        when([has_left], rests[n].start)
    keep.wait()
    for k, (to, there, box) in enumerate(tell):
        when([there], box.wait_recv)

        @pl.when(jnp.logical_not(there))
        def _(k=k):
            boxes[k + 1] = jnp.zeros(boxes.shape[1:], jnp.int32)

        when([to], box.wait_send)
    for n in each:
        when([has_right], tops[n].wait_recv)
        when([has_right, has_up], corners[n].start)
    for n in each:
        when([has_right], rests[n].wait_recv)
        when([has_right, has_down], corners[n].wait_recv)
        when([has_right, has_up], corners[n].wait_send)
        when([has_down], lowers[n].wait_recv)
        when([has_left], tops[n].wait_send)
        when([has_left], rests[n].wait_send)
        when([has_up], lowers[n].wait_send)


def run_rims(rows, cols, tile, info, pattern):
    layers, _, height, width = tile.shape
    anyw = pl.BlockSpec(memory_space=pl.ANY)
    vmem = pl.BlockSpec(memory_space=pltpu.VMEM)
    f32, dma = jnp.float32, pltpu.SemaphoreType.DMA
    return pl.pallas_call(
        functools.partial(rims_kernel, rows, cols),
        out_shape=(
            jax.ShapeDtypeStruct((layers, 2, height, pattern), f32),
            jax.ShapeDtypeStruct((layers, 2, pattern, width), f32),
            jax.ShapeDtypeStruct((layers, 2, pattern, pattern), f32),
            jax.ShapeDtypeStruct((4,) + info.shape, jnp.int32),
        ),
        in_specs=[anyw, vmem],
        out_specs=(anyw, anyw, anyw, vmem),
        scratch_shapes=[dma((4 * layers,)), dma((4 * layers,)), dma((3,)), dma((3,)), dma((1,))],
        compiler_params=pltpu.CompilerParams(collective_id=0, has_side_effects=True),
        cost_estimate=pl.CostEstimate(flops=0, bytes_accessed=10_000_000, transcendentals=0),
    )(tile, info)


def each_mode(modes):
    def run(body):
        for mode in range(modes):
            body(mode)

    return run


def slots_kernel(
    rows, cols, boxes, offsets, used, tile, right, lower, corner, probe_in, measured_in, table_f_in, table_b_in, hop_f_in, hop_b_in,
    grad_tile, grad_right, grad_lower, grad_corner, grad, light,
    ext0, ext1, window, waves, far, back, term, canvas, probe, measured, table_f, table_b, hop_f, hop_b, intensity,
    sems_in, sems_out,
):
    bf16 = jnp.bfloat16
    modes, pattern = probe.shape[0], probe.shape[-1]
    slots = offsets.shape[0]
    height, width = tile.shape[2], tile.shape[3]
    wide, tall = pattern + lanes, pattern + sublanes
    exts = (ext0, ext1)
    row, col = place()
    first, second = pl.ds(0, pattern), pl.ds(pattern, pattern)

    def spots(n):
        return (
            exts[n].at[:, pl.ds(0, height), pl.ds(0, width)],
            exts[n].at[:, pl.ds(0, height), pl.ds(width, pattern)],
            exts[n].at[:, pl.ds(height, pattern), pl.ds(0, width)],
            exts[n].at[:, pl.ds(height, pattern), pl.ds(width, pattern)],
        )

    moves = [(probe_in, probe)]
    moves += [(array.at[0], spot) for array, spot in zip((tile, right, lower, corner), spots(0))]
    moves += [(hop_f_in, hop_f), (hop_b_in, hop_b)]
    moves += [(array.at[1], spot) for array, spot in zip((tile, right, lower, corner), spots(1))]
    moves += [(table_f_in, table_f), (table_b_in, table_b), (measured_in, measured)]
    loads = [pltpu.make_async_copy(a, b, sems_in.at[k]) for k, (a, b) in enumerate(moves)]
    for load in loads:
        load.start()

    canvas[...] = jnp.zeros_like(canvas)
    loads[0].wait()
    power = jnp.zeros((pattern, pattern), jnp.float32)
    for mode in range(modes):
        power = power + (probe[mode, 0] * probe[mode, 0] + probe[mode, 1] * probe[mode, 1])
    intensity[...] = power
    for block in range(4):

        @pl.loop(0, boxes[block, 0, 2 * slots])
        def _(slot, block=block):
            at_row = boxes[block, 0, 2 * slot] - row * height + height
            at_col = boxes[block, 0, 2 * slot + 1] - col * width + width
            row_base, col_base, row_shift, col_shift = aligned(at_row, at_col)
            at = (pl.ds(row_base, tall), pl.ds(col_base, wide))
            canvas[at] = canvas[at] + roll_down(pad(intensity[...]), row_shift, col_shift)

    light[...] = canvas[height : 2 * height, width : 2 * width] + 1.0

    def bases(slot):
        return aligned(offsets[slot, 0] - row * height, offsets[slot, 1] - col * width)

    def cut(n):
        @pl.loop(0, used[0])
        def _(slot):
            row_base, col_base, row_shift, col_shift = bases(slot)
            row_back = jnp.where(row_shift == 0, 0, tall - row_shift)
            col_back = jnp.where(col_shift == 0, 0, wide - col_shift)
            for part in range(2):
                block = exts[n][part, pl.ds(row_base, tall), pl.ds(col_base, wide)]
                window[slot, n, part] = roll_down(block, row_back, col_back)[:pattern, :pattern]

    def spread(n, slot):
        row_base, col_base, row_shift, col_shift = bases(slot)
        for part in range(2):
            at = (part, pl.ds(row_base, tall), pl.ds(col_base, wide))
            exts[n][at] = exts[n][at] + roll_down(pad(term[part]), row_shift, col_shift)

    def save(n):
        return [
            pltpu.make_async_copy(spot, target.at[n], sems_out.at[4 * n + k])
            for k, (spot, target) in enumerate(zip(spots(n), (grad_tile, grad_right, grad_lower, grad_corner)))
        ]

    for k in range(1, 7):
        loads[k].wait()
    cut(0)
    exts[0][...] = jnp.zeros_like(exts[0])

    @pl.loop(0, used[0])
    def _(slot):
        @each_mode(modes)
        def _(mode):
            wr, wi = probe[mode, 0], probe[mode, 1]
            o_r, o_i = window[slot, 0, 0], window[slot, 0, 1]
            wr, wi = transform(o_r * wr - o_i * wi, o_r * wi + o_i * wr, hop_f[...], hop_b[...])
            waves[slot, mode, 0] = wr
            waves[slot, mode, 1] = wi

    for k in range(7, len(moves)):
        loads[k].wait()
    cut(1)
    exts[1][...] = jnp.zeros_like(exts[1])

    @pl.loop(0, used[0])
    def _(slot):
        intensity[...] = -measured[slot]
        term[...] = jnp.zeros_like(term)

        @each_mode(modes)
        def _(mode):
            wr, wi = waves[slot, mode, 0], waves[slot, mode, 1]
            o_r, o_i = window[slot, 1, 0], window[slot, 1, 1]
            fr, fi = transform(o_r * wr - o_i * wi, o_r * wi + o_i * wr, table_f[...], table_b[...])
            far[mode, 0] = fr
            far[mode, 1] = fi
            intensity[...] += fr * fr + fi * fi

        @each_mode(modes)
        def _(mode):
            gain = intensity[...]
            gr, gi = transform(gain * far[mode, 0], gain * far[mode, 1], table_b[...], table_f[...])
            wr, wi = waves[slot, mode, 0], waves[slot, mode, 1]
            term[0] += wr * gr + wi * gi
            term[1] += wr * gi - wi * gr
            o_r, o_i = window[slot, 1, 0], window[slot, 1, 1]
            back[slot, mode, 0] = (o_r * gr + o_i * gi).astype(bf16)
            back[slot, mode, 1] = (o_r * gi - o_i * gr).astype(bf16)

        spread(1, slot)

    saves = save(1)
    for one in saves:
        one.start()
    grad[...] = jnp.zeros_like(grad)

    @pl.loop(0, used[0])
    def _(slot):
        term[...] = jnp.zeros_like(term)

        @each_mode(modes)
        def _(mode):
            gr, gi = transform(back[slot, mode, 0], back[slot, mode, 1], hop_b[...], hop_f[...])
            wr, wi = probe[mode, 0], probe[mode, 1]
            term[0] += wr * gr + wi * gi
            term[1] += wr * gi - wi * gr
            o_r, o_i = window[slot, 0, 0], window[slot, 0, 1]
            grad[mode, first] += o_r * gr + o_i * gi
            grad[mode, second] += o_r * gi - o_i * gr

        spread(0, slot)

    last = save(0)
    for one in last:
        one.start()
    for one in saves + last:
        one.wait()


def run_slots(rows, cols, boxes, offsets, used, tile, right, lower, corner, probe, measured, *matrices):
    layers, _, height, width = tile.shape
    modes, _, pattern, _ = probe.shape
    slots = offsets.shape[0]
    smem = pl.BlockSpec(memory_space=pltpu.SMEM)
    vmem = pl.BlockSpec(memory_space=pltpu.VMEM)
    anyw = pl.BlockSpec(memory_space=pl.ANY)
    f32, bf16 = jnp.float32, jnp.bfloat16
    space, dma = pltpu.VMEM, pltpu.SemaphoreType.DMA
    ext = (2, height + pattern, width + pattern)
    return pl.pallas_call(
        functools.partial(slots_kernel, rows, cols),
        out_shape=(
            jax.ShapeDtypeStruct(tile.shape, f32),
            jax.ShapeDtypeStruct(right.shape, f32),
            jax.ShapeDtypeStruct(lower.shape, f32),
            jax.ShapeDtypeStruct(corner.shape, f32),
            jax.ShapeDtypeStruct((modes, 2 * pattern, pattern), f32),
            jax.ShapeDtypeStruct((height, width), f32),
        ),
        in_specs=[smem, smem, smem] + [anyw] * 10,
        out_specs=(anyw, anyw, anyw, anyw, vmem, vmem),
        scratch_shapes=[
            space(ext, f32), space(ext, f32),
            space((slots, layers, 2, pattern, pattern), f32),
            space((slots, modes, 2, pattern, pattern), f32),
            space((modes, 2, pattern, pattern), f32),
            space((slots, modes, 2, pattern, pattern), bf16),
            space((2, pattern, pattern), f32),
            space((2 * height + pattern, 2 * width + pattern), f32),
            space(probe.shape, f32), space(measured.shape, f32),
            *[space((2 * pattern, 2 * pattern), bf16) for _ in range(4)],
            space((pattern, pattern), f32),
            dma((14,)), dma((8,)),
        ],
        compiler_params=pltpu.CompilerParams(vmem_limit_bytes=58 * 1024 * 1024),
        cost_estimate=pl.CostEstimate(flops=20_000_000_000, bytes_accessed=30_000_000, transcendentals=0),
    )(boxes, offsets, used, tile, right, lower, corner, probe, measured, *matrices)


def share_kernel(
    rows, cols, tile, right, lower, corner, grad_tile, grad, light, probe_in, new_object, total,
    side, inner, left_in, above_in, edge, held, landed, core_in, probe, sems_in, sent_halo, got_halo, sent, got,
):
    near = neighbours(rows, cols)
    ways = digits(rows, cols)
    partners = list(near.values())
    for digit in ways.values():
        partners += group(digit)
    layers, pattern = right.shape[0], corner.shape[-1]
    height, width = tile.shape[2], tile.shape[3]
    modes = grad.shape[0]
    each = range(layers)
    first, second = pl.ds(0, pattern), pl.ds(pattern, pattern)
    moves = [(right, side), (tile, new_object), (grad_tile, inner), (probe_in, probe)]
    loads = [pltpu.make_async_copy(a, b, sems_in.at[k]) for k, (a, b) in enumerate(moves)]
    for load in loads:
        load.start()
    greet(partners)
    has_up, up = near["up"]
    has_down, down = near["down"]
    has_left, _ = near["left"]
    has_right, far_right = near["right"]

    def copy(source, target, k, device):
        return pltpu.make_async_remote_copy(
            src_ref=source, dst_ref=target, send_sem=sent_halo.at[k], recv_sem=got_halo.at[k],
            device_id=device, device_id_type=MESH,
        )

    top, rest = pl.ds(0, pattern), pl.ds(pattern, height - pattern)
    tops = [[copy(side.at[n, p, top], left_in.at[n, p, top], 6 * n + p, far_right) for p in (0, 1)] for n in each]
    rests = [copy(side.at[n, :, rest], left_in.at[n, :, rest], 6 * n + 2, far_right) for n in each]
    lowers = [[copy(lower.at[n, p], above_in.at[n, p], 6 * n + 3 + p, down) for p in (0, 1)] for n in each]
    corners = [copy(corner.at[n], edge.at[n], 6 * n + 5, down) for n in each]
    reduction = Reduction(rows, cols, grad, total, held, landed, core_in, (sent, got))

    def add_corner(n):
        @pl.when(jnp.logical_and(has_right, has_up))
        def _():
            corners[n].wait_recv()
            side[n, :, :pattern] = side[n, :, :pattern] + edge[n]

    def release(n, part):
        when([has_right], tops[n][part].start)
        when([has_down], lowers[n][part].start)

    def finish(n):
        @pl.when(has_left)
        def _():
            rests[n].wait_recv()
            tops[n][0].wait_recv()
            tops[n][1].wait_recv()

        @pl.when(jnp.logical_not(has_left))
        def _():
            left_in[n] = jnp.zeros(left_in.shape[1:], jnp.float32)

        @pl.when(has_up)
        def _():
            lowers[n][0].wait_recv()
            lowers[n][1].wait_recv()

        @pl.when(jnp.logical_not(has_up))
        def _():
            above_in[n] = jnp.zeros(above_in.shape[1:], jnp.float32)

        inner[n, :, :, :pattern] += left_in[n]
        inner[n, :, :pattern, :] += above_in[n]
        for part in range(2):
            new_object[n, part] = new_object[n, part] - inner[n, part] / light[...]

    every = range(len(streams))
    for k in range(reduction.share):
        reduction.core_send(k)
    when([has_down, has_right], corners[0].start)
    loads[0].wait()
    when([has_right], rests[0].start)
    for k in range(reduction.share):
        reduction.core_add(k)
        for s in every:
            if streams[s][0] == k:
                reduction.scatter_send(s, 0)
    when([has_down, has_right], corners[1].start)
    when([has_right], rests[1].start)
    for s in every:
        reduction.scatter_add(s, 0)
        reduction.scatter_send(s, 1)
    add_corner(0)
    release(0, 0)
    for s in every:
        reduction.scatter_add(s, 1)
        reduction.scatter_send(s, 2)
    release(0, 1)
    for s in every:
        reduction.scatter_add(s, 2)
        reduction.gather_send(s, 2)
    add_corner(1)
    release(1, 0)
    for s in every:
        reduction.gather_wait(s, 2)
        reduction.gather_send(s, 1)
    release(1, 1)
    loads[1].wait()
    loads[2].wait()
    for s in every:
        reduction.gather_wait(s, 1)
        reduction.gather_send(s, 0)
    finish(0)
    for s in every:
        reduction.gather_wait(s, 0)
        reduction.core_share(s)
    finish(1)
    for s in range(len(streams)):
        for made in reduction.waits[s]:
            made.wait_recv()
    for made in reduction.pending:
        made.wait_send()
    for n in each:
        when([has_right], rests[n].wait_send)
        when([has_down, has_right], corners[n].wait_send)
        for part in (0, 1):
            when([has_right], tops[n][part].wait_send)
            when([has_down], lowers[n][part].wait_send)
    loads[3].wait()
    squares = jnp.zeros((pattern, pattern), jnp.float32)
    for mode in range(modes):
        squares = squares + (total[mode, first] * total[mode, first] + total[mode, second] * total[mode, second])
    count = modes * 2 * pattern * pattern
    scale = jnp.sqrt(jnp.broadcast_to(jnp.sum(squares), (pattern, pattern)) * (1.0 / count) + 1e-06)
    factor = probe_step / scale
    for mode in range(modes):
        total[mode, first] = probe[mode, 0] - factor * total[mode, first]
        total[mode, second] = probe[mode, 1] - factor * total[mode, second]


def run_share(rows, cols, tile, right, lower, corner, grad_tile, grad, light, probe):
    layers = right.shape[0]
    pattern = corner.shape[-1]
    modes = grad.shape[0]
    anyw = pl.BlockSpec(memory_space=pl.ANY)
    vmem = pl.BlockSpec(memory_space=pltpu.VMEM)
    f32, space, dma = jnp.float32, pltpu.VMEM, pltpu.SemaphoreType.DMA
    half = (modes // 2, 2 * pattern, pattern)
    count = modes // 2 + len(streams) * (2 * sum(way[2] - 1 for way in digits(rows, cols).values()) - 1)
    new_object, new_probe = pl.pallas_call(
        functools.partial(share_kernel, rows, cols),
        out_shape=(
            jax.ShapeDtypeStruct(tile.shape, f32),
            jax.ShapeDtypeStruct((modes, 2 * pattern, pattern), f32),
        ),
        in_specs=[anyw, anyw, anyw, anyw, anyw, vmem, vmem, anyw],
        out_specs=(vmem, vmem),
        scratch_shapes=[
            space(right.shape, f32), space(tile.shape, f32), space(right.shape, f32), space(lower.shape, f32),
            space(corner.shape, f32), space(half, f32), space(half, f32), space(half, f32), space(probe.shape, f32),
            dma((4,)), dma((6 * layers,)), dma((6 * layers,)), dma((count,)), dma((count,)),
        ],
        compiler_params=pltpu.CompilerParams(
            collective_id=1, has_side_effects=True, vmem_limit_bytes=60 * 1024 * 1024
        ),
        cost_estimate=pl.CostEstimate(flops=0, bytes_accessed=30_000_000, transcendentals=0),
    )(tile, right, lower, corner, grad_tile, grad, light, probe)
    return new_object, new_probe.reshape(probe.shape)


def on_device(object_slab, probe_mode_stack, offsets, measured, counts):
    pattern = probe_mode_stack.shape[-1]
    rows, cols = lax.axis_size("obj"), lax.axis_size("scan")
    info = jnp.concatenate([offsets.reshape(-1), counts])
    info = jnp.pad(info[None], ((0, sublanes - 1), (0, lanes - info.shape[0])))
    right, lower, corner, boxes = run_rims(rows, cols, object_slab, info, pattern)
    grad_tile, right, lower, corner, grad, light = run_slots(
        rows, cols, boxes, offsets, counts, object_slab, right, lower, corner, probe_mode_stack, measured, *tables(pattern)
    )
    return run_share(rows, cols, object_slab, right, lower, corner, grad_tile, grad, light, probe_mode_stack)


def solution(mesh):
    in_specs = (
        P(None, None, "obj", "scan"),
        P(),
        P(("obj", "scan"), None),
        P(("obj", "scan"), None, None),
        P(("obj", "scan")),
    )
    out_specs = (P(None, None, "obj", "scan"), P())
    return jax.shard_map(
        on_device, mesh=mesh, in_specs=in_specs, out_specs=out_specs, check_vma=False
    )
```

```python
import functools
import math

import jax
import jax.numpy as jnp
import numpy as np
from jax import lax
from jax.experimental import pallas as pl
from jax.experimental.pallas import tpu as pltpu
from jax.sharding import PartitionSpec as P

chirp_scale = 24.0
probe_step = 0.15
lanes = 128
sublanes = 8


def dft_parts(pattern):
    indices = np.arange(pattern)
    angles = (indices[:, None] * indices[None, :] % pattern) * (2.0 * math.pi / pattern)
    parts = (np.cos(angles) / math.sqrt(pattern), np.sin(angles) / math.sqrt(pattern))
    return [part.astype(np.float32).astype(jnp.bfloat16).astype(np.float64) for part in parts]


def block_matrix(real_part, imag_part):
    upper = np.concatenate([real_part, -imag_part], axis=1)
    lower = np.concatenate([imag_part, real_part], axis=1)
    return jnp.asarray(np.concatenate([upper, lower], axis=0).astype(np.float32), jnp.bfloat16)


def tables(pattern):
    cos, sin = dft_parts(pattern)
    indices = np.arange(pattern)
    freqs = ((indices + pattern // 2) % pattern - pattern // 2) / pattern
    chirp = np.exp(-1j * math.pi * chirp_scale * freqs**2)
    hop = (cos + 1j * sin) @ (chirp[:, None] * (cos - 1j * sin))
    return (
        block_matrix(cos, -sin), block_matrix(cos, sin),
        block_matrix(hop.real, hop.imag), block_matrix(hop.real, -hop.imag),
    )


def aligned(row, col):
    row_base = pl.multiple_of(row // sublanes * sublanes, sublanes)
    col_base = pl.multiple_of(col // lanes * lanes, lanes)
    return row_base, col_base, row - row_base, col - col_base


def pad(array):
    array = jnp.concatenate([array, jnp.zeros((array.shape[0], lanes), jnp.float32)], axis=1)
    return jnp.concatenate([array, jnp.zeros((sublanes, array.shape[1]), jnp.float32)], axis=0)


def roll_down(array, rows, cols):
    return pltpu.roll(pltpu.roll(array, cols, 1), rows, 0)


def transform(real_part, imag_part, left, right):
    pattern = real_part.shape[0]
    stacked = jnp.concatenate([real_part.astype(jnp.bfloat16), imag_part.astype(jnp.bfloat16)], axis=0)
    half = jnp.dot(left, stacked, preferred_element_type=jnp.float32).astype(jnp.bfloat16)
    half = jnp.concatenate([half[:pattern], half[pattern:]], axis=1)
    full = jnp.dot(half, right, preferred_element_type=jnp.float32)
    return full[:, :pattern], full[:, pattern:]


MESH = pl.DeviceIdType.MESH


def place():
    return lax.axis_index("obj"), lax.axis_index("scan")


def greet(partners):
    barrier = pltpu.get_barrier_semaphore()
    for exists, device in partners:

        @pl.when(exists)
        def _(device=device):
            pl.semaphore_signal(barrier, inc=1, device_id=device, device_id_type=MESH)

    count = 0
    for exists, _ in partners:
        count = count + (1 if exists is True else jnp.where(exists, 1, 0))
    pl.semaphore_wait(barrier, count)


def neighbours(rows, cols):
    row, col = place()
    return {
        "up": (row > 0, (row - 1, col)),
        "down": (row < rows - 1, (row + 1, col)),
        "left": (col > 0, (row, col - 1)),
        "right": (col < cols - 1, (row, col + 1)),
    }


def digits(rows, cols):
    return {
        "core": ("obj", 1, 2),
        "y": ("obj", 2, rows // 2),
        "x": ("scan", 1, 2),
        "z": ("scan", 2, cols // 2),
    }


def member(digit, by):
    axis, stride, radix = digit
    row, col = place()
    at = row if axis == "obj" else col
    mine = at // stride % radix
    theirs = (mine + by) % radix
    there = at + (theirs - mine) * stride
    return mine, theirs, ((there, col) if axis == "obj" else (row, there))


def group(digit):
    return [(True, member(digit, by)[2]) for by in range(1, digit[2])]


streams = (
    (0, 0, 2, ("x", "y", "z")),
    (1, 0, 2, ("y", "x", "z")),
    (2, 0, 1, ("x", "z", "y")),
    (2, 1, 1, ("y", "z", "x")),
)


class Reduction:
    def __init__(self, rows, cols, grad, total, held, landed, core_in, sems):
        self.ways = digits(rows, cols)
        self.grad, self.total, self.held, self.landed, self.core_in = grad, total, held, landed, core_in
        self.sent, self.got = sems
        self.count = 0
        self.pending = []
        self.share = grad.shape[0] // 2
        self.state = [[0, grad.shape[1]] for _ in streams]
        self.waits = [[] for _ in streams]
        self.landing = [0 for _ in streams]

    def copy(self, source, target, device):
        k = self.count
        self.count += 1
        made = pltpu.make_async_remote_copy(
            src_ref=source, dst_ref=target, send_sem=self.sent.at[k], recv_sem=self.got.at[k],
            device_id=device, device_id_type=MESH,
        )
        made.start()
        self.pending.append(made)
        return made

    def core_send(self, k):
        mine, theirs, device = member(self.ways["core"], 1)
        self.core_waits = getattr(self, "core_waits", {})
        self.core_waits[k] = self.copy(self.grad.at[theirs * self.share + k], self.core_in.at[k], device)

    def core_add(self, k):
        mine, _, _ = member(self.ways["core"], 1)
        self.core_waits[k].wait_recv()
        self.held[k] = self.grad[mine * self.share + k] + self.core_in[k]

    def lanes_of(self, s):
        return pl.ds(streams[s][1] * lanes, streams[s][2] * lanes)

    def scatter_send(self, s, step):
        mode = streams[s][0]
        digit = self.ways[streams[s][3][step]]
        start, size = self.state[s]
        part = size // digit[2]
        self.waits[s] = []
        for by in range(1, digit[2]):
            _, theirs, device = member(digit, by)
            spot = self.landed.at[mode, pl.ds(self.landing[s], part), self.lanes_of(s)]
            source = self.held.at[mode, pl.ds(pl.multiple_of(start + theirs * part, sublanes), part), self.lanes_of(s)]
            self.waits[s].append((self.copy(source, spot, device), self.landing[s]))
            self.landing[s] += part

    def scatter_add(self, s, step):
        mode = streams[s][0]
        digit = self.ways[streams[s][3][step]]
        start, size = self.state[s]
        part = size // digit[2]
        if digit[2] > 1:
            mine, _, _ = member(digit, 1)
            start = start + mine * part
        self.state[s] = [start, part]
        span = pl.ds(pl.multiple_of(start, sublanes), part)
        value = self.held[mode, span, self.lanes_of(s)]
        for made, landing in self.waits[s]:
            made.wait_recv()
            value = value + self.landed[mode, pl.ds(landing, part), self.lanes_of(s)]
        if step == 2:
            own = member(self.ways["core"], 1)[0] * self.share + mode
            self.total[own, span, self.lanes_of(s)] = value
        else:
            self.held[mode, span, self.lanes_of(s)] = value

    def gather_send(self, s, step):
        mode = streams[s][0]
        digit = self.ways[streams[s][3][step]]
        start, size = self.state[s]
        own = member(self.ways["core"], 1)[0] * self.share + mode
        self.waits[s] = []
        for by in range(1, digit[2]):
            spot = self.total.at[own, pl.ds(pl.multiple_of(start, sublanes), size), self.lanes_of(s)]
            self.waits[s].append(self.copy(spot, spot, member(digit, by)[2]))

    def gather_wait(self, s, step):
        digit = self.ways[streams[s][3][step]]
        start, size = self.state[s]
        for made in self.waits[s]:
            made.wait_recv()
        if digit[2] > 1:
            start = start - member(digit, 1)[0] * size
        self.state[s] = [start, size * digit[2]]

    def core_share(self, s):
        mine, _, device = member(self.ways["core"], 1)
        spot = self.total.at[mine * self.share + streams[s][0], :, self.lanes_of(s)]
        self.waits[s] = [self.copy(spot, spot, device)]


def when(conditions, action):
    pl.when(functools.reduce(jnp.logical_and, conditions))(action)


def rims_kernel(rows, cols, tile, info, right, lower, corner, boxes, sent, got, sent_box, got_box, sem):
    near = neighbours(rows, cols)
    row, col = place()
    layers, pattern = tile.shape[0], corner.shape[-1]
    height = tile.shape[2]
    has_up, up = near["up"]
    has_down, down = near["down"]
    has_left, left = near["left"]
    has_right, far_right = near["right"]
    after = (jnp.logical_and(has_down, has_right), (row + 1, col + 1))
    before = (jnp.logical_and(has_up, has_left), (row - 1, col - 1))
    keep = pltpu.make_async_copy(info, boxes.at[0], sem.at[0])
    keep.start()
    greet(list(near.values()) + [after, before])

    def copy(source, target, k, device, sems=(sent, got)):
        return pltpu.make_async_remote_copy(
            src_ref=source, dst_ref=target, send_sem=sems[0].at[k], recv_sem=sems[1].at[k],
            device_id=device, device_id_type=MESH,
        )

    top, rest = pl.ds(0, pattern), pl.ds(pattern, height - pattern)
    first = pl.ds(0, pattern)
    each = range(layers)
    tops = [copy(tile.at[n, :, top, first], right.at[n, :, top], 4 * n, left) for n in each]
    rests = [copy(tile.at[n, :, rest, first], right.at[n, :, rest], 4 * n + 1, left) for n in each]
    lowers = [copy(tile.at[n, :, top], lower.at[n], 4 * n + 2, up) for n in each]
    corners = [copy(right.at[n, :, top], corner.at[n], 4 * n + 3, up) for n in each]
    tell = [
        (has_right, has_left, copy(info, boxes.at[1], 0, far_right, (sent_box, got_box))),
        (has_down, has_up, copy(info, boxes.at[2], 1, down, (sent_box, got_box))),
        (after[0], before[0], copy(info, boxes.at[3], 2, after[1], (sent_box, got_box))),
    ]
    for to, _, box in tell:
        when([to], box.start)
    for n in each:
        when([has_left], tops[n].start)
        when([has_up], lowers[n].start)
    for n in each:
        when([has_left], rests[n].start)
    keep.wait()
    for k, (to, there, box) in enumerate(tell):
        when([there], box.wait_recv)

        @pl.when(jnp.logical_not(there))
        def _(k=k):
            boxes[k + 1] = jnp.zeros(boxes.shape[1:], jnp.int32)

        when([to], box.wait_send)
    for n in each:
        when([has_right], tops[n].wait_recv)
        when([has_right, has_up], corners[n].start)
    for n in each:
        when([has_right], rests[n].wait_recv)
        when([has_right, has_down], corners[n].wait_recv)
        when([has_right, has_up], corners[n].wait_send)
        when([has_down], lowers[n].wait_recv)
        when([has_left], tops[n].wait_send)
        when([has_left], rests[n].wait_send)
        when([has_up], lowers[n].wait_send)


def run_rims(rows, cols, tile, info, pattern):
    layers, _, height, width = tile.shape
    anyw = pl.BlockSpec(memory_space=pl.ANY)
    vmem = pl.BlockSpec(memory_space=pltpu.VMEM)
    f32, dma = jnp.float32, pltpu.SemaphoreType.DMA
    return pl.pallas_call(
        functools.partial(rims_kernel, rows, cols),
        out_shape=(
            jax.ShapeDtypeStruct((layers, 2, height, pattern), f32),
            jax.ShapeDtypeStruct((layers, 2, pattern, width), f32),
            jax.ShapeDtypeStruct((layers, 2, pattern, pattern), f32),
            jax.ShapeDtypeStruct((4,) + info.shape, jnp.int32),
        ),
        in_specs=[anyw, vmem],
        out_specs=(anyw, anyw, anyw, vmem),
        scratch_shapes=[dma((4 * layers,)), dma((4 * layers,)), dma((3,)), dma((3,)), dma((1,))],
        compiler_params=pltpu.CompilerParams(collective_id=0, has_side_effects=True),
        cost_estimate=pl.CostEstimate(flops=0, bytes_accessed=10_000_000, transcendentals=0),
    )(tile, info)


def each_mode(modes):
    def run(body):
        for mode in range(modes):
            body(mode)

    return run


def slots_kernel(
    rows, cols, boxes, offsets, used, tile, right, lower, corner, probe_in, measured_in, table_f_in, table_b_in, hop_f_in, hop_b_in,
    grad_tile, grad_right, grad_lower, grad_corner, grad_out, light_out,
    grad, light, ext0, ext1, window, waves, far, back, term, canvas, probe, measured, table_f, table_b, hop_f, hop_b, intensity,
    sems_in, sems_out,
):
    bf16 = jnp.bfloat16
    modes, pattern = probe.shape[0], probe.shape[-1]
    slots = offsets.shape[0]
    height, width = tile.shape[2], tile.shape[3]
    wide, tall = pattern + lanes, pattern + sublanes
    exts = (ext0, ext1)
    row, col = place()
    first, second = pl.ds(0, pattern), pl.ds(pattern, pattern)

    def spots(n):
        return (
            exts[n].at[:, pl.ds(0, height), pl.ds(0, width)],
            exts[n].at[:, pl.ds(0, height), pl.ds(width, pattern)],
            exts[n].at[:, pl.ds(height, pattern), pl.ds(0, width)],
            exts[n].at[:, pl.ds(height, pattern), pl.ds(width, pattern)],
        )

    moves = [(probe_in, probe)]
    moves += [(array.at[0], spot) for array, spot in zip((tile, right, lower, corner), spots(0))]
    moves += [(hop_f_in, hop_f), (hop_b_in, hop_b)]
    moves += [(array.at[1], spot) for array, spot in zip((tile, right, lower, corner), spots(1))]
    moves += [(table_f_in, table_f), (table_b_in, table_b), (measured_in, measured)]
    loads = [pltpu.make_async_copy(a, b, sems_in.at[k]) for k, (a, b) in enumerate(moves)]
    for load in loads:
        load.start()

    canvas[...] = jnp.zeros_like(canvas)
    loads[0].wait()
    power = jnp.zeros((pattern, pattern), jnp.float32)
    for mode in range(modes):
        power = power + (probe[mode, 0] * probe[mode, 0] + probe[mode, 1] * probe[mode, 1])
    intensity[...] = power
    for block in range(4):

        @pl.loop(0, boxes[block, 0, 2 * slots])
        def _(slot, block=block):
            at_row = boxes[block, 0, 2 * slot] - row * height + height
            at_col = boxes[block, 0, 2 * slot + 1] - col * width + width
            row_base, col_base, row_shift, col_shift = aligned(at_row, at_col)
            at = (pl.ds(row_base, tall), pl.ds(col_base, wide))
            canvas[at] = canvas[at] + roll_down(pad(intensity[...]), row_shift, col_shift)

    light[...] = canvas[height : 2 * height, width : 2 * width] + 1.0
    light_save = pltpu.make_async_copy(light, light_out, sems_out.at[8])
    light_save.start()

    def bases(slot):
        return aligned(offsets[slot, 0] - row * height, offsets[slot, 1] - col * width)

    def cut(n):
        @pl.loop(0, used[0])
        def _(slot):
            row_base, col_base, row_shift, col_shift = bases(slot)
            row_back = jnp.where(row_shift == 0, 0, tall - row_shift)
            col_back = jnp.where(col_shift == 0, 0, wide - col_shift)
            for part in range(2):
                block = exts[n][part, pl.ds(row_base, tall), pl.ds(col_base, wide)]
                window[slot, n, part] = roll_down(block, row_back, col_back)[:pattern, :pattern]

    def spread(n, slot):
        row_base, col_base, row_shift, col_shift = bases(slot)
        for part in range(2):
            at = (part, pl.ds(row_base, tall), pl.ds(col_base, wide))
            exts[n][at] = exts[n][at] + roll_down(pad(term[slot, part]), row_shift, col_shift)

    def save(n):
        return [
            pltpu.make_async_copy(spot, target.at[n], sems_out.at[4 * n + k])
            for k, (spot, target) in enumerate(zip(spots(n), (grad_tile, grad_right, grad_lower, grad_corner)))
        ]

    for k in range(1, 7):
        loads[k].wait()
    cut(0)
    exts[0][...] = jnp.zeros_like(exts[0])

    @pl.loop(0, used[0])
    def _(slot):
        @each_mode(modes)
        def _(mode):
            wr, wi = probe[mode, 0], probe[mode, 1]
            o_r, o_i = window[slot, 0, 0], window[slot, 0, 1]
            wr, wi = transform(o_r * wr - o_i * wi, o_r * wi + o_i * wr, hop_f[...], hop_b[...])
            waves[slot, mode, 0] = wr
            waves[slot, mode, 1] = wi

    for k in range(7, len(moves)):
        loads[k].wait()
    cut(1)
    exts[1][...] = jnp.zeros_like(exts[1])

    @pl.loop(0, used[0])
    def _(slot):
        intensity[...] = -measured[slot]
        term[slot] = jnp.zeros(term.shape[1:], jnp.float32)

        @each_mode(modes)
        def _(mode):
            wr, wi = waves[slot, mode, 0], waves[slot, mode, 1]
            o_r, o_i = window[slot, 1, 0], window[slot, 1, 1]
            fr, fi = transform(o_r * wr - o_i * wi, o_r * wi + o_i * wr, table_f[...], table_b[...])
            far[mode, 0] = fr
            far[mode, 1] = fi
            intensity[...] += fr * fr + fi * fi

        @each_mode(modes)
        def _(mode):
            gain = intensity[...]
            gr, gi = transform(gain * far[mode, 0], gain * far[mode, 1], table_b[...], table_f[...])
            wr, wi = waves[slot, mode, 0], waves[slot, mode, 1]
            term[slot, 0] += wr * gr + wi * gi
            term[slot, 1] += wr * gi - wi * gr
            o_r, o_i = window[slot, 1, 0], window[slot, 1, 1]
            back[slot, mode, 0] = (o_r * gr + o_i * gi).astype(bf16)
            back[slot, mode, 1] = (o_r * gi - o_i * gr).astype(bf16)

        spread(1, slot)

    saves = save(1)
    for one in saves:
        one.start()
    grad[...] = jnp.zeros_like(grad)

    @pl.loop(0, used[0])
    def _(slot):
        term[slot] = jnp.zeros(term.shape[1:], jnp.float32)

        @each_mode(modes)
        def _(mode):
            gr, gi = transform(back[slot, mode, 0], back[slot, mode, 1], hop_b[...], hop_f[...])
            wr, wi = probe[mode, 0], probe[mode, 1]
            term[slot, 0] += wr * gr + wi * gi
            term[slot, 1] += wr * gi - wi * gr
            o_r, o_i = window[slot, 0, 0], window[slot, 0, 1]
            grad[mode, first] += o_r * gr + o_i * gi
            grad[mode, second] += o_r * gi - o_i * gr

    grad_save = pltpu.make_async_copy(grad, grad_out, sems_out.at[9])
    grad_save.start()

    @pl.loop(0, used[0])
    def _(slot):
        spread(0, slot)

    last = save(0)
    for one in last:
        one.start()
    for one in saves + last + [light_save, grad_save]:
        one.wait()


def run_slots(rows, cols, boxes, offsets, used, tile, right, lower, corner, probe, measured, *matrices):
    layers, _, height, width = tile.shape
    modes, _, pattern, _ = probe.shape
    slots = offsets.shape[0]
    smem = pl.BlockSpec(memory_space=pltpu.SMEM)
    vmem = pl.BlockSpec(memory_space=pltpu.VMEM)
    anyw = pl.BlockSpec(memory_space=pl.ANY)
    f32, bf16 = jnp.float32, jnp.bfloat16
    space, dma = pltpu.VMEM, pltpu.SemaphoreType.DMA
    ext = (2, height + pattern, width + pattern)
    return pl.pallas_call(
        functools.partial(slots_kernel, rows, cols),
        out_shape=(
            jax.ShapeDtypeStruct(tile.shape, f32),
            jax.ShapeDtypeStruct(right.shape, f32),
            jax.ShapeDtypeStruct(lower.shape, f32),
            jax.ShapeDtypeStruct(corner.shape, f32),
            jax.ShapeDtypeStruct((modes, 2 * pattern, pattern), f32),
            jax.ShapeDtypeStruct((height, width), f32),
        ),
        in_specs=[smem, smem, smem] + [anyw] * 10,
        out_specs=(anyw,) * 6,
        scratch_shapes=[
            space((modes, 2 * pattern, pattern), f32), space((height, width), f32),
            space(ext, f32), space(ext, f32),
            space((slots, layers, 2, pattern, pattern), f32),
            space((slots, modes, 2, pattern, pattern), f32),
            space((modes, 2, pattern, pattern), f32),
            space((slots, modes, 2, pattern, pattern), bf16),
            space((slots, 2, pattern, pattern), f32),
            space((2 * height + pattern, 2 * width + pattern), f32),
            space(probe.shape, f32), space(measured.shape, f32),
            *[space((2 * pattern, 2 * pattern), bf16) for _ in range(4)],
            space((pattern, pattern), f32),
            dma((14,)), dma((10,)),
        ],
        compiler_params=pltpu.CompilerParams(vmem_limit_bytes=58 * 1024 * 1024),
        cost_estimate=pl.CostEstimate(flops=20_000_000_000, bytes_accessed=30_000_000, transcendentals=0),
    )(boxes, offsets, used, tile, right, lower, corner, probe, measured, *matrices)


def share_kernel(
    rows, cols, tile, right, lower, corner, grad_tile, grad, light, probe_in, new_object, new_probe,
    fresh, total, side, inner, left_in, above_in, edge, held, landed, core_in, probe, sems_in, sems_out, sent_halo, got_halo, sent, got,
):
    near = neighbours(rows, cols)
    ways = digits(rows, cols)
    partners = list(near.values())
    for digit in ways.values():
        partners += group(digit)
    layers, pattern = right.shape[0], corner.shape[-1]
    height, width = tile.shape[2], tile.shape[3]
    modes = grad.shape[0]
    each = range(layers)
    first, second = pl.ds(0, pattern), pl.ds(pattern, pattern)
    moves = [(right, side), (tile, fresh), (grad_tile, inner), (probe_in, probe)]
    loads = [pltpu.make_async_copy(a, b, sems_in.at[k]) for k, (a, b) in enumerate(moves)]
    for load in loads:
        load.start()
    greet(partners)
    has_up, up = near["up"]
    has_down, down = near["down"]
    has_left, _ = near["left"]
    has_right, far_right = near["right"]

    def copy(source, target, k, device):
        return pltpu.make_async_remote_copy(
            src_ref=source, dst_ref=target, send_sem=sent_halo.at[k], recv_sem=got_halo.at[k],
            device_id=device, device_id_type=MESH,
        )

    top, rest = pl.ds(0, pattern), pl.ds(pattern, height - pattern)
    tops = [[copy(side.at[n, p, top], left_in.at[n, p, top], 6 * n + p, far_right) for p in (0, 1)] for n in each]
    rests = [copy(side.at[n, :, rest], left_in.at[n, :, rest], 6 * n + 2, far_right) for n in each]
    lowers = [[copy(lower.at[n, p], above_in.at[n, p], 6 * n + 3 + p, down) for p in (0, 1)] for n in each]
    corners = [copy(corner.at[n], edge.at[n], 6 * n + 5, down) for n in each]
    leaves = [pltpu.make_async_copy(fresh.at[n], new_object.at[n], sems_out.at[n]) for n in each]
    outs = [pltpu.make_async_copy(total.at[m], new_probe.at[m], sems_out.at[layers + m]) for m in range(modes)]
    reduction = Reduction(rows, cols, grad, total, held, landed, core_in, (sent, got))

    def add_corner(n):
        @pl.when(jnp.logical_and(has_right, has_up))
        def _():
            corners[n].wait_recv()
            side[n, :, :pattern] = side[n, :, :pattern] + edge[n]

    def release(n, part):
        when([has_right], tops[n][part].start)
        when([has_down], lowers[n][part].start)

    def finish(n):
        @pl.when(has_left)
        def _():
            rests[n].wait_recv()
            tops[n][0].wait_recv()
            tops[n][1].wait_recv()

        @pl.when(jnp.logical_not(has_left))
        def _():
            left_in[n] = jnp.zeros(left_in.shape[1:], jnp.float32)

        @pl.when(has_up)
        def _():
            lowers[n][0].wait_recv()
            lowers[n][1].wait_recv()

        @pl.when(jnp.logical_not(has_up))
        def _():
            above_in[n] = jnp.zeros(above_in.shape[1:], jnp.float32)

        inner[n, :, :, :pattern] += left_in[n]
        inner[n, :, :pattern, :] += above_in[n]
        for part in range(2):
            fresh[n, part] = fresh[n, part] - inner[n, part] / light[...]
        leaves[n].start()

    every = range(len(streams))
    for k in range(reduction.share):
        reduction.core_send(k)
    when([has_down, has_right], corners[0].start)
    loads[0].wait()
    when([has_right], rests[0].start)
    for k in range(reduction.share):
        reduction.core_add(k)
        for s in every:
            if streams[s][0] == k:
                reduction.scatter_send(s, 0)
    when([has_down, has_right], corners[1].start)
    when([has_right], rests[1].start)
    for s in every:
        reduction.scatter_add(s, 0)
        reduction.scatter_send(s, 1)
    add_corner(0)
    release(0, 0)
    for s in every:
        reduction.scatter_add(s, 1)
        reduction.scatter_send(s, 2)
    release(0, 1)
    for s in every:
        reduction.scatter_add(s, 2)
        reduction.gather_send(s, 2)
    add_corner(1)
    release(1, 0)
    for s in every:
        reduction.gather_wait(s, 2)
        reduction.gather_send(s, 1)
    release(1, 1)
    loads[1].wait()
    loads[2].wait()
    for s in every:
        reduction.gather_wait(s, 1)
        reduction.gather_send(s, 0)
    finish(0)
    for s in every:
        reduction.gather_wait(s, 0)
        reduction.core_share(s)
    finish(1)
    mine, theirs, _ = member(ways["core"], 1)

    def squares_of(half):
        squares = jnp.zeros((pattern, pattern), jnp.float32)
        for m in range(reduction.share):
            mode = half * reduction.share + m
            squares = squares + (total[mode, first] * total[mode, first] + total[mode, second] * total[mode, second])
        return squares

    squares = squares_of(mine)
    for s in range(len(streams)):
        for made in reduction.waits[s]:
            made.wait_recv()
    squares = squares + squares_of(theirs)
    for made in reduction.pending:
        made.wait_send()
    loads[3].wait()
    count = modes * 2 * pattern * pattern
    scale = jnp.sqrt(jnp.broadcast_to(jnp.sum(squares), (pattern, pattern)) * (1.0 / count) + 1e-06)
    factor = probe_step / scale
    for mode in range(modes):
        total[mode, first] = probe[mode, 0] - factor * total[mode, first]
        total[mode, second] = probe[mode, 1] - factor * total[mode, second]
        outs[mode].start()
    for n in each:
        when([has_right], rests[n].wait_send)
        when([has_down, has_right], corners[n].wait_send)
        for part in (0, 1):
            when([has_right], tops[n][part].wait_send)
            when([has_down], lowers[n][part].wait_send)
    for one in leaves + outs:
        one.wait()


def run_share(rows, cols, tile, right, lower, corner, grad_tile, grad, light, probe):
    layers = right.shape[0]
    pattern = corner.shape[-1]
    modes = grad.shape[0]
    anyw = pl.BlockSpec(memory_space=pl.ANY)
    vmem = pl.BlockSpec(memory_space=pltpu.VMEM)
    f32, space, dma = jnp.float32, pltpu.VMEM, pltpu.SemaphoreType.DMA
    half = (modes // 2, 2 * pattern, pattern)
    count = modes // 2 + len(streams) * (2 * sum(way[2] - 1 for way in digits(rows, cols).values()) - 1)
    new_object, new_probe = pl.pallas_call(
        functools.partial(share_kernel, rows, cols),
        out_shape=(
            jax.ShapeDtypeStruct(tile.shape, f32),
            jax.ShapeDtypeStruct((modes, 2 * pattern, pattern), f32),
        ),
        in_specs=[anyw, anyw, anyw, anyw, anyw, vmem, vmem, anyw],
        out_specs=(anyw, anyw),
        scratch_shapes=[
            space(tile.shape, f32), space((modes, 2 * pattern, pattern), f32),
            space(right.shape, f32), space(tile.shape, f32), space(right.shape, f32), space(lower.shape, f32),
            space(corner.shape, f32), space(half, f32), space(half, f32), space(half, f32), space(probe.shape, f32),
            dma((4,)), dma((layers + modes,)), dma((6 * layers,)), dma((6 * layers,)), dma((count,)), dma((count,)),
        ],
        compiler_params=pltpu.CompilerParams(
            collective_id=1, has_side_effects=True, vmem_limit_bytes=60 * 1024 * 1024
        ),
        cost_estimate=pl.CostEstimate(flops=0, bytes_accessed=30_000_000, transcendentals=0),
    )(tile, right, lower, corner, grad_tile, grad, light, probe)
    return new_object, new_probe.reshape(probe.shape)


def on_device(object_slab, probe_mode_stack, offsets, measured, counts):
    pattern = probe_mode_stack.shape[-1]
    rows, cols = lax.axis_size("obj"), lax.axis_size("scan")
    info = jnp.concatenate([offsets.reshape(-1), counts])
    info = jnp.pad(info[None], ((0, sublanes - 1), (0, lanes - info.shape[0])))
    right, lower, corner, boxes = run_rims(rows, cols, object_slab, info, pattern)
    grad_tile, right, lower, corner, grad, light = run_slots(
        rows, cols, boxes, offsets, counts, object_slab, right, lower, corner, probe_mode_stack, measured, *tables(pattern)
    )
    return run_share(rows, cols, object_slab, right, lower, corner, grad_tile, grad, light, probe_mode_stack)


def solution(mesh):
    in_specs = (
        P(None, None, "obj", "scan"),
        P(),
        P(("obj", "scan"), None),
        P(("obj", "scan"), None, None),
        P(("obj", "scan")),
    )
    out_specs = (P(None, None, "obj", "scan"), P())
    return jax.shard_map(
        on_device, mesh=mesh, in_specs=in_specs, out_specs=out_specs, check_vma=False
    )
```

```python
import functools
import math

import jax
import jax.numpy as jnp
import numpy as np
from jax import lax
from jax.experimental import pallas as pl
from jax.experimental.pallas import tpu as pltpu
from jax.sharding import PartitionSpec as P

chirp_scale = 24.0
probe_step = 0.15
lanes = 128
sublanes = 8


def dft_parts(pattern):
    indices = np.arange(pattern)
    angles = (indices[:, None] * indices[None, :] % pattern) * (2.0 * math.pi / pattern)
    parts = (np.cos(angles) / math.sqrt(pattern), np.sin(angles) / math.sqrt(pattern))
    return [part.astype(np.float32).astype(jnp.bfloat16).astype(np.float64) for part in parts]


def block_matrix(real_part, imag_part):
    upper = np.concatenate([real_part, -imag_part], axis=1)
    lower = np.concatenate([imag_part, real_part], axis=1)
    return jnp.asarray(np.concatenate([upper, lower], axis=0).astype(np.float32), jnp.bfloat16)


def tables(pattern):
    cos, sin = dft_parts(pattern)
    indices = np.arange(pattern)
    freqs = ((indices + pattern // 2) % pattern - pattern // 2) / pattern
    chirp = np.exp(-1j * math.pi * chirp_scale * freqs**2)
    hop = (cos + 1j * sin) @ (chirp[:, None] * (cos - 1j * sin))
    return (
        block_matrix(cos, -sin), block_matrix(cos, sin),
        block_matrix(hop.real, hop.imag), block_matrix(hop.real, -hop.imag),
    )


def aligned(row, col):
    row_base = pl.multiple_of(row // sublanes * sublanes, sublanes)
    col_base = pl.multiple_of(col // lanes * lanes, lanes)
    return row_base, col_base, row - row_base, col - col_base


def pad(array):
    array = jnp.concatenate([array, jnp.zeros((array.shape[0], lanes), jnp.float32)], axis=1)
    return jnp.concatenate([array, jnp.zeros((sublanes, array.shape[1]), jnp.float32)], axis=0)


def roll_down(array, rows, cols):
    return pltpu.roll(pltpu.roll(array, cols, 1), rows, 0)


def transform(real_part, imag_part, left, right):
    pattern = real_part.shape[0]
    stacked = jnp.concatenate([real_part.astype(jnp.bfloat16), imag_part.astype(jnp.bfloat16)], axis=0)
    half = jnp.dot(left, stacked, preferred_element_type=jnp.float32).astype(jnp.bfloat16)
    half = jnp.concatenate([half[:pattern], half[pattern:]], axis=1)
    full = jnp.dot(half, right, preferred_element_type=jnp.float32)
    return full[:, :pattern], full[:, pattern:]


MESH = pl.DeviceIdType.MESH


def place():
    return lax.axis_index("obj"), lax.axis_index("scan")


def greet(partners):
    barrier = pltpu.get_barrier_semaphore()
    for exists, device in partners:

        @pl.when(exists)
        def _(device=device):
            pl.semaphore_signal(barrier, inc=1, device_id=device, device_id_type=MESH)

    count = 0
    for exists, _ in partners:
        count = count + (1 if exists is True else jnp.where(exists, 1, 0))
    pl.semaphore_wait(barrier, count)


def neighbours(rows, cols):
    row, col = place()
    return {
        "up": (row > 0, (row - 1, col)),
        "down": (row < rows - 1, (row + 1, col)),
        "left": (col > 0, (row, col - 1)),
        "right": (col < cols - 1, (row, col + 1)),
    }


def digits(rows, cols):
    return {
        "core": ("obj", 1, 2),
        "y": ("obj", 2, rows // 2),
        "x": ("scan", 1, 2),
        "z": ("scan", 2, cols // 2),
    }


def member(digit, by):
    axis, stride, radix = digit
    row, col = place()
    at = row if axis == "obj" else col
    mine = at // stride % radix
    theirs = (mine + by) % radix
    there = at + (theirs - mine) * stride
    return mine, theirs, ((there, col) if axis == "obj" else (row, there))


def group(digit):
    return [(True, member(digit, by)[2]) for by in range(1, digit[2])]


streams = (
    (0, 0, 1, ("z", "x", "y")),
    (0, 1, 1, ("y", "z", "x")),
    (1, 0, 2, ("x", "y", "z")),
    (2, 0, 2, ("y", "x", "z")),
)


class Reduction:
    def __init__(self, rows, cols, grad, total, held, landed, core_in, sems):
        self.ways = digits(rows, cols)
        self.grad, self.total, self.held, self.landed, self.core_in = grad, total, held, landed, core_in
        self.sent, self.got = sems
        self.count = 0
        self.pending = []
        self.share = grad.shape[0] // 2
        self.state = [[0, grad.shape[1]] for _ in streams]
        self.waits = [[] for _ in streams]
        self.landing = [0 for _ in streams]

    def copy(self, source, target, device):
        k = self.count
        self.count += 1
        made = pltpu.make_async_remote_copy(
            src_ref=source, dst_ref=target, send_sem=self.sent.at[k], recv_sem=self.got.at[k],
            device_id=device, device_id_type=MESH,
        )
        made.start()
        self.pending.append(made)
        return made

    def core_send(self, k):
        mine, theirs, device = member(self.ways["core"], 1)
        self.core_waits = getattr(self, "core_waits", {})
        self.core_waits[k] = self.copy(self.grad.at[theirs * self.share + k], self.core_in.at[k], device)

    def core_add(self, k):
        mine, _, _ = member(self.ways["core"], 1)
        self.core_waits[k].wait_recv()
        self.held[k] = self.grad[mine * self.share + k] + self.core_in[k]

    def lanes_of(self, s):
        return pl.ds(streams[s][1] * lanes, streams[s][2] * lanes)

    def scatter_send(self, s, step):
        mode = streams[s][0]
        digit = self.ways[streams[s][3][step]]
        start, size = self.state[s]
        part = size // digit[2]
        self.waits[s] = []
        for by in range(1, digit[2]):
            _, theirs, device = member(digit, by)
            spot = self.landed.at[mode, pl.ds(self.landing[s], part), self.lanes_of(s)]
            source = self.held.at[mode, pl.ds(pl.multiple_of(start + theirs * part, sublanes), part), self.lanes_of(s)]
            self.waits[s].append((self.copy(source, spot, device), self.landing[s]))
            self.landing[s] += part

    def scatter_add(self, s, step):
        mode = streams[s][0]
        digit = self.ways[streams[s][3][step]]
        start, size = self.state[s]
        part = size // digit[2]
        if digit[2] > 1:
            mine, _, _ = member(digit, 1)
            start = start + mine * part
        self.state[s] = [start, part]
        span = pl.ds(pl.multiple_of(start, sublanes), part)
        value = self.held[mode, span, self.lanes_of(s)]
        for made, landing in self.waits[s]:
            made.wait_recv()
            value = value + self.landed[mode, pl.ds(landing, part), self.lanes_of(s)]
        if step == 2:
            own = member(self.ways["core"], 1)[0] * self.share + mode
            self.total[own, span, self.lanes_of(s)] = value
        else:
            self.held[mode, span, self.lanes_of(s)] = value

    def gather_send(self, s, step):
        mode = streams[s][0]
        digit = self.ways[streams[s][3][step]]
        start, size = self.state[s]
        own = member(self.ways["core"], 1)[0] * self.share + mode
        self.waits[s] = []
        for by in range(1, digit[2]):
            spot = self.total.at[own, pl.ds(pl.multiple_of(start, sublanes), size), self.lanes_of(s)]
            self.waits[s].append(self.copy(spot, spot, member(digit, by)[2]))

    def gather_wait(self, s, step):
        digit = self.ways[streams[s][3][step]]
        start, size = self.state[s]
        for made in self.waits[s]:
            made.wait_recv()
        if digit[2] > 1:
            start = start - member(digit, 1)[0] * size
        self.state[s] = [start, size * digit[2]]

    def core_share(self, s):
        mine, _, device = member(self.ways["core"], 1)
        spot = self.total.at[mine * self.share + streams[s][0], :, self.lanes_of(s)]
        self.waits[s] = [self.copy(spot, spot, device)]


def when(conditions, action):
    pl.when(functools.reduce(jnp.logical_and, conditions))(action)


def rims_kernel(rows, cols, tile, info, right, lower, corner, boxes, sent, got, sent_box, got_box, sem):
    near = neighbours(rows, cols)
    row, col = place()
    layers, pattern = tile.shape[0], corner.shape[-1]
    height = tile.shape[2]
    has_up, up = near["up"]
    has_down, down = near["down"]
    has_left, left = near["left"]
    has_right, far_right = near["right"]
    after = (jnp.logical_and(has_down, has_right), (row + 1, col + 1))
    before = (jnp.logical_and(has_up, has_left), (row - 1, col - 1))
    keep = pltpu.make_async_copy(info, boxes.at[0], sem.at[0])
    keep.start()
    greet(list(near.values()) + [after, before])

    def copy(source, target, k, device, sems=(sent, got)):
        return pltpu.make_async_remote_copy(
            src_ref=source, dst_ref=target, send_sem=sems[0].at[k], recv_sem=sems[1].at[k],
            device_id=device, device_id_type=MESH,
        )

    top, rest = pl.ds(0, pattern), pl.ds(pattern, height - pattern)
    first = pl.ds(0, pattern)
    each = range(layers)
    tops = [copy(tile.at[n, :, top, first], right.at[n, :, top], 4 * n, left) for n in each]
    rests = [copy(tile.at[n, :, rest, first], right.at[n, :, rest], 4 * n + 1, left) for n in each]
    lowers = [copy(tile.at[n, :, top], lower.at[n], 4 * n + 2, up) for n in each]
    corners = [copy(right.at[n, :, top], corner.at[n], 4 * n + 3, up) for n in each]
    tell = [
        (has_right, has_left, copy(info, boxes.at[1], 0, far_right, (sent_box, got_box))),
        (has_down, has_up, copy(info, boxes.at[2], 1, down, (sent_box, got_box))),
        (after[0], before[0], copy(info, boxes.at[3], 2, after[1], (sent_box, got_box))),
    ]
    for to, _, box in tell:
        when([to], box.start)
    for n in each:
        when([has_left], tops[n].start)
        when([has_up], lowers[n].start)
    for n in each:
        when([has_left], rests[n].start)
    keep.wait()
    for k, (to, there, box) in enumerate(tell):
        when([there], box.wait_recv)

        @pl.when(jnp.logical_not(there))
        def _(k=k):
            boxes[k + 1] = jnp.zeros(boxes.shape[1:], jnp.int32)

        when([to], box.wait_send)
    for n in each:
        when([has_right], tops[n].wait_recv)
        when([has_right, has_up], corners[n].start)
    for n in each:
        when([has_right], rests[n].wait_recv)
        when([has_right, has_down], corners[n].wait_recv)
        when([has_right, has_up], corners[n].wait_send)
        when([has_down], lowers[n].wait_recv)
        when([has_left], tops[n].wait_send)
        when([has_left], rests[n].wait_send)
        when([has_up], lowers[n].wait_send)


def run_rims(rows, cols, tile, info, pattern):
    layers, _, height, width = tile.shape
    anyw = pl.BlockSpec(memory_space=pl.ANY)
    vmem = pl.BlockSpec(memory_space=pltpu.VMEM)
    f32, dma = jnp.float32, pltpu.SemaphoreType.DMA
    return pl.pallas_call(
        functools.partial(rims_kernel, rows, cols),
        out_shape=(
            jax.ShapeDtypeStruct((layers, 2, height, pattern), f32),
            jax.ShapeDtypeStruct((layers, 2, pattern, width), f32),
            jax.ShapeDtypeStruct((layers, 2, pattern, pattern), f32),
            jax.ShapeDtypeStruct((4,) + info.shape, jnp.int32),
        ),
        in_specs=[anyw, vmem],
        out_specs=(anyw, anyw, anyw, vmem),
        scratch_shapes=[dma((4 * layers,)), dma((4 * layers,)), dma((3,)), dma((3,)), dma((1,))],
        compiler_params=pltpu.CompilerParams(collective_id=0, has_side_effects=True),
        cost_estimate=pl.CostEstimate(flops=0, bytes_accessed=10_000_000, transcendentals=0),
    )(tile, info)


def each_mode(modes):
    def run(body):
        for mode in range(modes):
            body(mode)

    return run


def slots_kernel(
    rows, cols, boxes, offsets, used, tile, right, lower, corner, probe_in, measured_in, table_f_in, table_b_in, hop_f_in, hop_b_in,
    grad_tile, grad_right, grad_lower, grad_corner, grad_out, light_out,
    grad, light, ext0, ext1, window, waves, far, back, term, canvas, probe, measured, table_f, table_b, hop_f, hop_b, intensity,
    sems_in, sems_out,
):
    bf16 = jnp.bfloat16
    modes, pattern = probe.shape[0], probe.shape[-1]
    slots = offsets.shape[0]
    height, width = tile.shape[2], tile.shape[3]
    wide, tall = pattern + lanes, pattern + sublanes
    exts = (ext0, ext1)
    row, col = place()
    first, second = pl.ds(0, pattern), pl.ds(pattern, pattern)

    def spots(n):
        return (
            exts[n].at[:, pl.ds(0, height), pl.ds(0, width)],
            exts[n].at[:, pl.ds(0, height), pl.ds(width, pattern)],
            exts[n].at[:, pl.ds(height, pattern), pl.ds(0, width)],
            exts[n].at[:, pl.ds(height, pattern), pl.ds(width, pattern)],
        )

    moves = [(probe_in, probe)]
    moves += [(array.at[0], spot) for array, spot in zip((tile, right, lower, corner), spots(0))]
    moves += [(hop_f_in, hop_f), (hop_b_in, hop_b)]
    moves += [(array.at[1], spot) for array, spot in zip((tile, right, lower, corner), spots(1))]
    moves += [(table_f_in, table_f), (table_b_in, table_b), (measured_in, measured)]
    loads = [pltpu.make_async_copy(a, b, sems_in.at[k]) for k, (a, b) in enumerate(moves)]
    for load in loads:
        load.start()

    canvas[...] = jnp.zeros_like(canvas)
    loads[0].wait()
    power = jnp.zeros((pattern, pattern), jnp.float32)
    for mode in range(modes):
        power = power + (probe[mode, 0] * probe[mode, 0] + probe[mode, 1] * probe[mode, 1])
    intensity[...] = power
    for block in range(4):

        @pl.loop(0, boxes[block, 0, 2 * slots])
        def _(slot, block=block):
            at_row = boxes[block, 0, 2 * slot] - row * height + height
            at_col = boxes[block, 0, 2 * slot + 1] - col * width + width
            row_base, col_base, row_shift, col_shift = aligned(at_row, at_col)
            at = (pl.ds(row_base, tall), pl.ds(col_base, wide))
            canvas[at] = canvas[at] + roll_down(pad(intensity[...]), row_shift, col_shift)

    light[...] = canvas[height : 2 * height, width : 2 * width] + 1.0
    light_save = pltpu.make_async_copy(light, light_out, sems_out.at[8])
    light_save.start()

    def bases(slot):
        return aligned(offsets[slot, 0] - row * height, offsets[slot, 1] - col * width)

    def cut(n):
        @pl.loop(0, used[0])
        def _(slot):
            row_base, col_base, row_shift, col_shift = bases(slot)
            row_back = jnp.where(row_shift == 0, 0, tall - row_shift)
            col_back = jnp.where(col_shift == 0, 0, wide - col_shift)
            for part in range(2):
                block = exts[n][part, pl.ds(row_base, tall), pl.ds(col_base, wide)]
                window[slot, n, part] = roll_down(block, row_back, col_back)[:pattern, :pattern]

    def spread(n, slot):
        row_base, col_base, row_shift, col_shift = bases(slot)
        for part in range(2):
            at = (part, pl.ds(row_base, tall), pl.ds(col_base, wide))
            exts[n][at] = exts[n][at] + roll_down(pad(term[slot, part]), row_shift, col_shift)

    def save(n):
        return [
            pltpu.make_async_copy(spot, target.at[n], sems_out.at[4 * n + k])
            for k, (spot, target) in enumerate(zip(spots(n), (grad_tile, grad_right, grad_lower, grad_corner)))
        ]

    for k in range(1, 7):
        loads[k].wait()
    cut(0)
    exts[0][...] = jnp.zeros_like(exts[0])

    @pl.loop(0, used[0])
    def _(slot):
        @each_mode(modes)
        def _(mode):
            wr, wi = probe[mode, 0], probe[mode, 1]
            o_r, o_i = window[slot, 0, 0], window[slot, 0, 1]
            wr, wi = transform(o_r * wr - o_i * wi, o_r * wi + o_i * wr, hop_f[...], hop_b[...])
            waves[slot, mode, 0] = wr
            waves[slot, mode, 1] = wi

    for k in range(7, len(moves)):
        loads[k].wait()
    cut(1)
    exts[1][...] = jnp.zeros_like(exts[1])

    @pl.loop(0, used[0])
    def _(slot):
        intensity[...] = -measured[slot]
        term[slot] = jnp.zeros(term.shape[1:], jnp.float32)

        @each_mode(modes)
        def _(mode):
            wr, wi = waves[slot, mode, 0], waves[slot, mode, 1]
            o_r, o_i = window[slot, 1, 0], window[slot, 1, 1]
            fr, fi = transform(o_r * wr - o_i * wi, o_r * wi + o_i * wr, table_f[...], table_b[...])
            far[mode, 0] = fr
            far[mode, 1] = fi
            intensity[...] += fr * fr + fi * fi

        @each_mode(modes)
        def _(mode):
            gain = intensity[...]
            gr, gi = transform(gain * far[mode, 0], gain * far[mode, 1], table_b[...], table_f[...])
            wr, wi = waves[slot, mode, 0], waves[slot, mode, 1]
            term[slot, 0] += wr * gr + wi * gi
            term[slot, 1] += wr * gi - wi * gr
            o_r, o_i = window[slot, 1, 0], window[slot, 1, 1]
            back[slot, mode, 0] = (o_r * gr + o_i * gi).astype(bf16)
            back[slot, mode, 1] = (o_r * gi - o_i * gr).astype(bf16)

        spread(1, slot)

    saves = save(1)
    for one in saves:
        one.start()
    grad[...] = jnp.zeros_like(grad)

    @pl.loop(0, used[0])
    def _(slot):
        term[slot] = jnp.zeros(term.shape[1:], jnp.float32)

        @each_mode(modes)
        def _(mode):
            gr, gi = transform(back[slot, mode, 0], back[slot, mode, 1], hop_b[...], hop_f[...])
            wr, wi = probe[mode, 0], probe[mode, 1]
            term[slot, 0] += wr * gr + wi * gi
            term[slot, 1] += wr * gi - wi * gr
            o_r, o_i = window[slot, 0, 0], window[slot, 0, 1]
            grad[mode, first] += o_r * gr + o_i * gi
            grad[mode, second] += o_r * gi - o_i * gr

    grad_save = pltpu.make_async_copy(grad, grad_out, sems_out.at[9])
    grad_save.start()

    @pl.loop(0, used[0])
    def _(slot):
        spread(0, slot)

    last = save(0)
    for one in last:
        one.start()
    for one in saves + last + [light_save, grad_save]:
        one.wait()


def run_slots(rows, cols, boxes, offsets, used, tile, right, lower, corner, probe, measured, *matrices):
    layers, _, height, width = tile.shape
    modes, _, pattern, _ = probe.shape
    slots = offsets.shape[0]
    smem = pl.BlockSpec(memory_space=pltpu.SMEM)
    vmem = pl.BlockSpec(memory_space=pltpu.VMEM)
    anyw = pl.BlockSpec(memory_space=pl.ANY)
    f32, bf16 = jnp.float32, jnp.bfloat16
    space, dma = pltpu.VMEM, pltpu.SemaphoreType.DMA
    ext = (2, height + pattern, width + pattern)
    return pl.pallas_call(
        functools.partial(slots_kernel, rows, cols),
        out_shape=(
            jax.ShapeDtypeStruct(tile.shape, f32),
            jax.ShapeDtypeStruct(right.shape, f32),
            jax.ShapeDtypeStruct(lower.shape, f32),
            jax.ShapeDtypeStruct(corner.shape, f32),
            jax.ShapeDtypeStruct((modes, 2 * pattern, pattern), f32),
            jax.ShapeDtypeStruct((height, width), f32),
        ),
        in_specs=[smem, smem, smem] + [anyw] * 10,
        out_specs=(anyw,) * 6,
        scratch_shapes=[
            space((modes, 2 * pattern, pattern), f32), space((height, width), f32),
            space(ext, f32), space(ext, f32),
            space((slots, layers, 2, pattern, pattern), f32),
            space((slots, modes, 2, pattern, pattern), f32),
            space((modes, 2, pattern, pattern), f32),
            space((slots, modes, 2, pattern, pattern), bf16),
            space((slots, 2, pattern, pattern), f32),
            space((2 * height + pattern, 2 * width + pattern), f32),
            space(probe.shape, f32), space(measured.shape, f32),
            *[space((2 * pattern, 2 * pattern), bf16) for _ in range(4)],
            space((pattern, pattern), f32),
            dma((14,)), dma((10,)),
        ],
        compiler_params=pltpu.CompilerParams(vmem_limit_bytes=58 * 1024 * 1024),
        cost_estimate=pl.CostEstimate(flops=20_000_000_000, bytes_accessed=30_000_000, transcendentals=0),
    )(boxes, offsets, used, tile, right, lower, corner, probe, measured, *matrices)


def share_kernel(
    rows, cols, tile, right, lower, corner, grad_tile, grad, light, probe_in, new_object, new_probe,
    fresh, total, side, inner, left_in, above_in, edge, held, landed, core_in, probe, sems_in, sems_out, sent_halo, got_halo, sent, got,
):
    near = neighbours(rows, cols)
    ways = digits(rows, cols)
    partners = list(near.values())
    for digit in ways.values():
        partners += group(digit)
    layers, pattern = right.shape[0], corner.shape[-1]
    height, width = tile.shape[2], tile.shape[3]
    modes = grad.shape[0]
    each = range(layers)
    first, second = pl.ds(0, pattern), pl.ds(pattern, pattern)
    moves = [(right, side), (tile, fresh), (grad_tile, inner), (probe_in, probe)]
    loads = [pltpu.make_async_copy(a, b, sems_in.at[k]) for k, (a, b) in enumerate(moves)]
    for load in loads:
        load.start()
    greet(partners)
    has_up, up = near["up"]
    has_down, down = near["down"]
    has_left, _ = near["left"]
    has_right, far_right = near["right"]

    def copy(source, target, k, device):
        return pltpu.make_async_remote_copy(
            src_ref=source, dst_ref=target, send_sem=sent_halo.at[k], recv_sem=got_halo.at[k],
            device_id=device, device_id_type=MESH,
        )

    top, rest = pl.ds(0, pattern), pl.ds(pattern, height - pattern)
    tops = [[copy(side.at[n, p, top], left_in.at[n, p, top], 6 * n + p, far_right) for p in (0, 1)] for n in each]
    rests = [copy(side.at[n, :, rest], left_in.at[n, :, rest], 6 * n + 2, far_right) for n in each]
    lowers = [[copy(lower.at[n, p], above_in.at[n, p], 6 * n + 3 + p, down) for p in (0, 1)] for n in each]
    corners = [copy(corner.at[n], edge.at[n], 6 * n + 5, down) for n in each]
    leaves = [pltpu.make_async_copy(fresh.at[n], new_object.at[n], sems_out.at[n]) for n in each]
    outs = [pltpu.make_async_copy(total.at[m], new_probe.at[m], sems_out.at[layers + m]) for m in range(modes)]
    reduction = Reduction(rows, cols, grad, total, held, landed, core_in, (sent, got))

    def add_corner(n):
        @pl.when(jnp.logical_and(has_right, has_up))
        def _():
            corners[n].wait_recv()
            side[n, :, :pattern] = side[n, :, :pattern] + edge[n]

    def release(n, part):
        when([has_right], tops[n][part].start)
        when([has_down], lowers[n][part].start)

    def finish(n):
        @pl.when(has_left)
        def _():
            rests[n].wait_recv()
            tops[n][0].wait_recv()
            tops[n][1].wait_recv()

        @pl.when(jnp.logical_not(has_left))
        def _():
            left_in[n] = jnp.zeros(left_in.shape[1:], jnp.float32)

        @pl.when(has_up)
        def _():
            lowers[n][0].wait_recv()
            lowers[n][1].wait_recv()

        @pl.when(jnp.logical_not(has_up))
        def _():
            above_in[n] = jnp.zeros(above_in.shape[1:], jnp.float32)

        inner[n, :, :, :pattern] += left_in[n]
        inner[n, :, :pattern, :] += above_in[n]
        for part in range(2):
            fresh[n, part] = fresh[n, part] - inner[n, part] / light[...]
        leaves[n].start()

    every = range(len(streams))
    for k in range(reduction.share):
        reduction.core_send(k)
    when([has_down, has_right], corners[0].start)
    loads[0].wait()
    when([has_right], rests[0].start)
    for k in range(reduction.share):
        reduction.core_add(k)
        for s in every:
            if streams[s][0] == k:
                reduction.scatter_send(s, 0)
    when([has_down, has_right], corners[1].start)
    when([has_right], rests[1].start)
    for s in every:
        reduction.scatter_add(s, 0)
        reduction.scatter_send(s, 1)
    add_corner(0)
    release(0, 0)
    for s in every:
        reduction.scatter_add(s, 1)
        reduction.scatter_send(s, 2)
    for s in every:
        reduction.scatter_add(s, 2)
        reduction.gather_send(s, 2)
    release(0, 1)
    add_corner(1)
    for s in every:
        reduction.gather_wait(s, 2)
        reduction.gather_send(s, 1)
    release(1, 0)
    loads[1].wait()
    loads[2].wait()
    for s in every:
        reduction.gather_wait(s, 1)
        reduction.gather_send(s, 0)
    release(1, 1)
    finish(0)
    for s in every:
        reduction.gather_wait(s, 0)
        reduction.core_share(s)
    finish(1)
    mine, theirs, _ = member(ways["core"], 1)

    def squares_of(half):
        squares = jnp.zeros((pattern, pattern), jnp.float32)
        for m in range(reduction.share):
            mode = half * reduction.share + m
            squares = squares + (total[mode, first] * total[mode, first] + total[mode, second] * total[mode, second])
        return squares

    squares = squares_of(mine)
    for s in range(len(streams)):
        for made in reduction.waits[s]:
            made.wait_recv()
    squares = squares + squares_of(theirs)
    for made in reduction.pending:
        made.wait_send()
    loads[3].wait()
    count = modes * 2 * pattern * pattern
    scale = jnp.sqrt(jnp.broadcast_to(jnp.sum(squares), (pattern, pattern)) * (1.0 / count) + 1e-06)
    factor = probe_step / scale
    for mode in range(modes):
        total[mode, first] = probe[mode, 0] - factor * total[mode, first]
        total[mode, second] = probe[mode, 1] - factor * total[mode, second]
        outs[mode].start()
    for n in each:
        when([has_right], rests[n].wait_send)
        when([has_down, has_right], corners[n].wait_send)
        for part in (0, 1):
            when([has_right], tops[n][part].wait_send)
            when([has_down], lowers[n][part].wait_send)
    for one in leaves + outs:
        one.wait()


def run_share(rows, cols, tile, right, lower, corner, grad_tile, grad, light, probe):
    layers = right.shape[0]
    pattern = corner.shape[-1]
    modes = grad.shape[0]
    anyw = pl.BlockSpec(memory_space=pl.ANY)
    vmem = pl.BlockSpec(memory_space=pltpu.VMEM)
    f32, space, dma = jnp.float32, pltpu.VMEM, pltpu.SemaphoreType.DMA
    half = (modes // 2, 2 * pattern, pattern)
    count = modes // 2 + len(streams) * (2 * sum(way[2] - 1 for way in digits(rows, cols).values()) - 1)
    new_object, new_probe = pl.pallas_call(
        functools.partial(share_kernel, rows, cols),
        out_shape=(
            jax.ShapeDtypeStruct(tile.shape, f32),
            jax.ShapeDtypeStruct((modes, 2 * pattern, pattern), f32),
        ),
        in_specs=[anyw, anyw, anyw, anyw, anyw, vmem, vmem, anyw],
        out_specs=(anyw, anyw),
        scratch_shapes=[
            space(tile.shape, f32), space((modes, 2 * pattern, pattern), f32),
            space(right.shape, f32), space(tile.shape, f32), space(right.shape, f32), space(lower.shape, f32),
            space(corner.shape, f32), space(half, f32), space(half, f32), space(half, f32), space(probe.shape, f32),
            dma((4,)), dma((layers + modes,)), dma((6 * layers,)), dma((6 * layers,)), dma((count,)), dma((count,)),
        ],
        compiler_params=pltpu.CompilerParams(
            collective_id=1, has_side_effects=True, vmem_limit_bytes=60 * 1024 * 1024
        ),
        cost_estimate=pl.CostEstimate(flops=0, bytes_accessed=30_000_000, transcendentals=0),
    )(tile, right, lower, corner, grad_tile, grad, light, probe)
    return new_object, new_probe.reshape(probe.shape)


def on_device(object_slab, probe_mode_stack, offsets, measured, counts):
    pattern = probe_mode_stack.shape[-1]
    rows, cols = lax.axis_size("obj"), lax.axis_size("scan")
    info = jnp.concatenate([offsets.reshape(-1), counts])
    info = jnp.pad(info[None], ((0, sublanes - 1), (0, lanes - info.shape[0])))
    right, lower, corner, boxes = run_rims(rows, cols, object_slab, info, pattern)
    grad_tile, right, lower, corner, grad, light = run_slots(
        rows, cols, boxes, offsets, counts, object_slab, right, lower, corner, probe_mode_stack, measured, *tables(pattern)
    )
    return run_share(rows, cols, object_slab, right, lower, corner, grad_tile, grad, light, probe_mode_stack)


def solution(mesh):
    in_specs = (
        P(None, None, "obj", "scan"),
        P(),
        P(("obj", "scan"), None),
        P(("obj", "scan"), None, None),
        P(("obj", "scan")),
    )
    out_specs = (P(None, None, "obj", "scan"), P())
    return jax.shard_map(
        on_device, mesh=mesh, in_specs=in_specs, out_specs=out_specs, check_vma=False
    )
```

```python
import functools
import math

import jax
import jax.numpy as jnp
import numpy as np
from jax import lax
from jax.experimental import pallas as pl
from jax.experimental.pallas import tpu as pltpu
from jax.sharding import PartitionSpec as P

chirp_scale = 24.0
probe_step = 0.15
lanes = 128
sublanes = 8


def dft_parts(pattern):
    indices = np.arange(pattern)
    angles = (indices[:, None] * indices[None, :] % pattern) * (2.0 * math.pi / pattern)
    parts = (np.cos(angles) / math.sqrt(pattern), np.sin(angles) / math.sqrt(pattern))
    return [part.astype(np.float32).astype(jnp.bfloat16).astype(np.float64) for part in parts]


def block_matrix(real_part, imag_part):
    upper = np.concatenate([real_part, -imag_part], axis=1)
    lower = np.concatenate([imag_part, real_part], axis=1)
    return jnp.asarray(np.concatenate([upper, lower], axis=0).astype(np.float32), jnp.bfloat16)


def tables(pattern):
    cos, sin = dft_parts(pattern)
    indices = np.arange(pattern)
    freqs = ((indices + pattern // 2) % pattern - pattern // 2) / pattern
    chirp = np.exp(-1j * math.pi * chirp_scale * freqs**2)
    hop = (cos + 1j * sin) @ (chirp[:, None] * (cos - 1j * sin))
    return (
        block_matrix(cos, -sin), block_matrix(cos, sin),
        block_matrix(hop.real, hop.imag), block_matrix(hop.real, -hop.imag),
    )


def aligned(row, col):
    row_base = pl.multiple_of(row // sublanes * sublanes, sublanes)
    col_base = pl.multiple_of(col // lanes * lanes, lanes)
    return row_base, col_base, row - row_base, col - col_base


def pad(array):
    array = jnp.concatenate([array, jnp.zeros((array.shape[0], lanes), jnp.float32)], axis=1)
    return jnp.concatenate([array, jnp.zeros((sublanes, array.shape[1]), jnp.float32)], axis=0)


def roll_down(array, rows, cols):
    return pltpu.roll(pltpu.roll(array, cols, 1), rows, 0)


def transform(real_part, imag_part, left, right):
    pattern = real_part.shape[0]
    stacked = jnp.concatenate([real_part.astype(jnp.bfloat16), imag_part.astype(jnp.bfloat16)], axis=0)
    half = jnp.dot(left, stacked, preferred_element_type=jnp.float32).astype(jnp.bfloat16)
    half = jnp.concatenate([half[:pattern], half[pattern:]], axis=1)
    full = jnp.dot(half, right, preferred_element_type=jnp.float32)
    return full[:, :pattern], full[:, pattern:]


MESH = pl.DeviceIdType.MESH


def place():
    return lax.axis_index("obj"), lax.axis_index("scan")


def greet(partners):
    barrier = pltpu.get_barrier_semaphore()
    for exists, device in partners:

        @pl.when(exists)
        def _(device=device):
            pl.semaphore_signal(barrier, inc=1, device_id=device, device_id_type=MESH)

    count = 0
    for exists, _ in partners:
        count = count + (1 if exists is True else jnp.where(exists, 1, 0))
    pl.semaphore_wait(barrier, count)


def neighbours(rows, cols):
    row, col = place()
    return {
        "up": (row > 0, (row - 1, col)),
        "down": (row < rows - 1, (row + 1, col)),
        "left": (col > 0, (row, col - 1)),
        "right": (col < cols - 1, (row, col + 1)),
    }


def digits(rows, cols):
    return {
        "core": ("obj", 1, 2),
        "y": ("obj", 2, rows // 2),
        "x": ("scan", 1, 2),
        "z": ("scan", 2, cols // 2),
    }


def member(digit, by):
    axis, stride, radix = digit
    row, col = place()
    at = row if axis == "obj" else col
    mine = at // stride % radix
    theirs = (mine + by) % radix
    there = at + (theirs - mine) * stride
    return mine, theirs, ((there, col) if axis == "obj" else (row, there))


def group(digit):
    return [(True, member(digit, by)[2]) for by in range(1, digit[2])]


streams = (
    (0, 0, 1, ("z", "x", "y")),
    (0, 1, 1, ("y", "z", "x")),
    (1, 0, 2, ("x", "y", "z")),
    (2, 0, 2, ("y", "x", "z")),
)


class Reduction:
    def __init__(self, rows, cols, grad, total, held, landed, core_in, sems):
        self.ways = digits(rows, cols)
        self.grad, self.total, self.held, self.landed, self.core_in = grad, total, held, landed, core_in
        self.sent, self.got = sems
        self.count = 0
        self.pending = []
        self.share = grad.shape[0] // 2
        self.state = [[0, grad.shape[1]] for _ in streams]
        self.waits = [[] for _ in streams]
        self.landing = [0 for _ in streams]

    def copy(self, source, target, device):
        k = self.count
        self.count += 1
        made = pltpu.make_async_remote_copy(
            src_ref=source, dst_ref=target, send_sem=self.sent.at[k], recv_sem=self.got.at[k],
            device_id=device, device_id_type=MESH,
        )
        made.start()
        self.pending.append(made)
        return made

    def core_send(self, k):
        mine, theirs, device = member(self.ways["core"], 1)
        self.core_waits = getattr(self, "core_waits", {})
        self.core_waits[k] = self.copy(self.grad.at[theirs * self.share + k], self.core_in.at[k], device)

    def core_add(self, k):
        mine, _, _ = member(self.ways["core"], 1)
        self.core_waits[k].wait_recv()
        self.held[k] = self.grad[mine * self.share + k] + self.core_in[k]

    def lanes_of(self, s):
        return pl.ds(streams[s][1] * lanes, streams[s][2] * lanes)

    def scatter_send(self, s, step):
        mode = streams[s][0]
        digit = self.ways[streams[s][3][step]]
        start, size = self.state[s]
        part = size // digit[2]
        self.waits[s] = []
        for by in range(1, digit[2]):
            _, theirs, device = member(digit, by)
            spot = self.landed.at[mode, pl.ds(self.landing[s], part), self.lanes_of(s)]
            source = self.held.at[mode, pl.ds(pl.multiple_of(start + theirs * part, sublanes), part), self.lanes_of(s)]
            self.waits[s].append((self.copy(source, spot, device), self.landing[s]))
            self.landing[s] += part

    def scatter_add(self, s, step):
        mode = streams[s][0]
        digit = self.ways[streams[s][3][step]]
        start, size = self.state[s]
        part = size // digit[2]
        if digit[2] > 1:
            mine, _, _ = member(digit, 1)
            start = start + mine * part
        self.state[s] = [start, part]
        span = pl.ds(pl.multiple_of(start, sublanes), part)
        value = self.held[mode, span, self.lanes_of(s)]
        for made, landing in self.waits[s]:
            made.wait_recv()
            value = value + self.landed[mode, pl.ds(landing, part), self.lanes_of(s)]
        if step == 2:
            own = member(self.ways["core"], 1)[0] * self.share + mode
            self.total[own, span, self.lanes_of(s)] = value
        else:
            self.held[mode, span, self.lanes_of(s)] = value

    def gather_send(self, s, step):
        mode = streams[s][0]
        digit = self.ways[streams[s][3][step]]
        start, size = self.state[s]
        own = member(self.ways["core"], 1)[0] * self.share + mode
        self.waits[s] = []
        for by in range(1, digit[2]):
            spot = self.total.at[own, pl.ds(pl.multiple_of(start, sublanes), size), self.lanes_of(s)]
            self.waits[s].append(self.copy(spot, spot, member(digit, by)[2]))

    def gather_wait(self, s, step):
        digit = self.ways[streams[s][3][step]]
        start, size = self.state[s]
        for made in self.waits[s]:
            made.wait_recv()
        if digit[2] > 1:
            start = start - member(digit, 1)[0] * size
        self.state[s] = [start, size * digit[2]]

    def core_share(self, s):
        mine, _, device = member(self.ways["core"], 1)
        spot = self.total.at[mine * self.share + streams[s][0], :, self.lanes_of(s)]
        self.waits[s] = [self.copy(spot, spot, device)]


def when(conditions, action):
    pl.when(functools.reduce(jnp.logical_and, conditions))(action)


def rims_kernel(rows, cols, tile, info, right, lower, corner, boxes, sent, got, sent_box, got_box, sem):
    near = neighbours(rows, cols)
    row, col = place()
    layers, pattern = tile.shape[0], corner.shape[-1]
    height = tile.shape[2]
    has_up, up = near["up"]
    has_down, down = near["down"]
    has_left, left = near["left"]
    has_right, far_right = near["right"]
    after = (jnp.logical_and(has_down, has_right), (row + 1, col + 1))
    before = (jnp.logical_and(has_up, has_left), (row - 1, col - 1))
    keep = pltpu.make_async_copy(info, boxes.at[0], sem.at[0])
    keep.start()
    greet(list(near.values()) + [after, before])

    def copy(source, target, k, device, sems=(sent, got)):
        return pltpu.make_async_remote_copy(
            src_ref=source, dst_ref=target, send_sem=sems[0].at[k], recv_sem=sems[1].at[k],
            device_id=device, device_id_type=MESH,
        )

    top, rest = pl.ds(0, pattern), pl.ds(pattern, height - pattern)
    first = pl.ds(0, pattern)
    each = range(layers)
    tops = [copy(tile.at[n, :, top, first], right.at[n, :, top], 4 * n, left) for n in each]
    rests = [copy(tile.at[n, :, rest, first], right.at[n, :, rest], 4 * n + 1, left) for n in each]
    lowers = [copy(tile.at[n, :, top], lower.at[n], 4 * n + 2, up) for n in each]
    corners = [copy(right.at[n, :, top], corner.at[n], 4 * n + 3, up) for n in each]
    tell = [
        (has_right, has_left, copy(info, boxes.at[1], 0, far_right, (sent_box, got_box))),
        (has_down, has_up, copy(info, boxes.at[2], 1, down, (sent_box, got_box))),
        (after[0], before[0], copy(info, boxes.at[3], 2, after[1], (sent_box, got_box))),
    ]
    for to, _, box in tell:
        when([to], box.start)
    for n in each:
        when([has_left], tops[n].start)
        when([has_up], lowers[n].start)
    for n in each:
        when([has_left], rests[n].start)
    keep.wait()
    for k, (to, there, box) in enumerate(tell):
        when([there], box.wait_recv)

        @pl.when(jnp.logical_not(there))
        def _(k=k):
            boxes[k + 1] = jnp.zeros(boxes.shape[1:], jnp.int32)

        when([to], box.wait_send)
    for n in each:
        when([has_right], tops[n].wait_recv)
        when([has_right, has_up], corners[n].start)
    for n in each:
        when([has_right], rests[n].wait_recv)
        when([has_right, has_down], corners[n].wait_recv)
        when([has_right, has_up], corners[n].wait_send)
        when([has_down], lowers[n].wait_recv)
        when([has_left], tops[n].wait_send)
        when([has_left], rests[n].wait_send)
        when([has_up], lowers[n].wait_send)


def run_rims(rows, cols, tile, info, pattern):
    layers, _, height, width = tile.shape
    anyw = pl.BlockSpec(memory_space=pl.ANY)
    vmem = pl.BlockSpec(memory_space=pltpu.VMEM)
    f32, dma = jnp.float32, pltpu.SemaphoreType.DMA
    return pl.pallas_call(
        functools.partial(rims_kernel, rows, cols),
        out_shape=(
            jax.ShapeDtypeStruct((layers, 2, height, pattern), f32),
            jax.ShapeDtypeStruct((layers, 2, pattern, width), f32),
            jax.ShapeDtypeStruct((layers, 2, pattern, pattern), f32),
            jax.ShapeDtypeStruct((4,) + info.shape, jnp.int32),
        ),
        in_specs=[anyw, vmem],
        out_specs=(anyw, anyw, anyw, vmem),
        scratch_shapes=[dma((4 * layers,)), dma((4 * layers,)), dma((3,)), dma((3,)), dma((1,))],
        compiler_params=pltpu.CompilerParams(collective_id=0, has_side_effects=True),
        cost_estimate=pl.CostEstimate(flops=0, bytes_accessed=10_000_000, transcendentals=0),
    )(tile, info)


def each_mode(modes):
    def run(body):
        for mode in range(modes):
            body(mode)

    return run


def slots_kernel(
    rows, cols, boxes, offsets, used, tile, right, lower, corner, probe_in, measured_in, table_f_in, table_b_in, hop_f_in, hop_b_in,
    grad_tile, grad_right, grad_lower, grad_corner, grad_out, light_out,
    grad, light, ext0, ext1, window, waves, far, back, term, canvas, probe, measured, table_f, table_b, hop_f, hop_b, intensity,
    sems_in, sems_out,
):
    bf16 = jnp.bfloat16
    modes, pattern = probe.shape[0], probe.shape[-1]
    slots = offsets.shape[0]
    height, width = tile.shape[2], tile.shape[3]
    wide, tall = pattern + lanes, pattern + sublanes
    exts = (ext0, ext1)
    row, col = place()
    first, second = pl.ds(0, pattern), pl.ds(pattern, pattern)

    def spots(n):
        return (
            exts[n].at[:, pl.ds(0, height), pl.ds(0, width)],
            exts[n].at[:, pl.ds(0, height), pl.ds(width, pattern)],
            exts[n].at[:, pl.ds(height, pattern), pl.ds(0, width)],
            exts[n].at[:, pl.ds(height, pattern), pl.ds(width, pattern)],
        )

    moves = [(probe_in, probe)]
    moves += [(array.at[0], spot) for array, spot in zip((tile, right, lower, corner), spots(0))]
    moves += [(hop_f_in, hop_f), (hop_b_in, hop_b)]
    moves += [(array.at[1], spot) for array, spot in zip((tile, right, lower, corner), spots(1))]
    moves += [(table_f_in, table_f), (table_b_in, table_b), (measured_in, measured)]
    loads = [pltpu.make_async_copy(a, b, sems_in.at[k]) for k, (a, b) in enumerate(moves)]
    for load in loads:
        load.start()

    canvas[...] = jnp.zeros_like(canvas)
    loads[0].wait()
    power = jnp.zeros((pattern, pattern), jnp.float32)
    for mode in range(modes):
        power = power + (probe[mode, 0] * probe[mode, 0] + probe[mode, 1] * probe[mode, 1])
    intensity[...] = power
    for block in range(4):

        @pl.loop(0, boxes[block, 0, 2 * slots])
        def _(slot, block=block):
            at_row = boxes[block, 0, 2 * slot] - row * height + height
            at_col = boxes[block, 0, 2 * slot + 1] - col * width + width
            row_base, col_base, row_shift, col_shift = aligned(at_row, at_col)
            at = (pl.ds(row_base, tall), pl.ds(col_base, wide))
            canvas[at] = canvas[at] + roll_down(pad(intensity[...]), row_shift, col_shift)

    light[...] = canvas[height : 2 * height, width : 2 * width] + 1.0
    light_save = pltpu.make_async_copy(light, light_out, sems_out.at[8])
    light_save.start()

    def bases(slot):
        return aligned(offsets[slot, 0] - row * height, offsets[slot, 1] - col * width)

    def cut(n):
        @pl.loop(0, used[0])
        def _(slot):
            row_base, col_base, row_shift, col_shift = bases(slot)
            row_back = jnp.where(row_shift == 0, 0, tall - row_shift)
            col_back = jnp.where(col_shift == 0, 0, wide - col_shift)
            for part in range(2):
                block = exts[n][part, pl.ds(row_base, tall), pl.ds(col_base, wide)]
                window[slot, n, part] = roll_down(block, row_back, col_back)[:pattern, :pattern]

    def spread(n, slot):
        row_base, col_base, row_shift, col_shift = bases(slot)
        for part in range(2):
            at = (part, pl.ds(row_base, tall), pl.ds(col_base, wide))
            exts[n][at] = exts[n][at] + roll_down(pad(term[slot, part]), row_shift, col_shift)

    def save(n):
        return [
            pltpu.make_async_copy(spot, target.at[n], sems_out.at[4 * n + k])
            for k, (spot, target) in enumerate(zip(spots(n), (grad_tile, grad_right, grad_lower, grad_corner)))
        ]

    for k in range(1, 7):
        loads[k].wait()
    cut(0)
    exts[0][...] = jnp.zeros_like(exts[0])

    @pl.loop(0, used[0])
    def _(slot):
        @each_mode(modes)
        def _(mode):
            wr, wi = probe[mode, 0], probe[mode, 1]
            o_r, o_i = window[slot, 0, 0], window[slot, 0, 1]
            wr, wi = transform(o_r * wr - o_i * wi, o_r * wi + o_i * wr, hop_f[...], hop_b[...])
            waves[slot, mode, 0] = wr
            waves[slot, mode, 1] = wi

    for k in range(7, len(moves)):
        loads[k].wait()
    cut(1)
    exts[1][...] = jnp.zeros_like(exts[1])

    @pl.loop(0, used[0])
    def _(slot):
        intensity[...] = -measured[slot]
        term[slot] = jnp.zeros(term.shape[1:], jnp.float32)

        @each_mode(modes)
        def _(mode):
            wr, wi = waves[slot, mode, 0], waves[slot, mode, 1]
            o_r, o_i = window[slot, 1, 0], window[slot, 1, 1]
            fr, fi = transform(o_r * wr - o_i * wi, o_r * wi + o_i * wr, table_f[...], table_b[...])
            far[mode, 0] = fr
            far[mode, 1] = fi
            intensity[...] += fr * fr + fi * fi

        @each_mode(modes)
        def _(mode):
            gain = intensity[...]
            gr, gi = transform(gain * far[mode, 0], gain * far[mode, 1], table_b[...], table_f[...])
            wr, wi = waves[slot, mode, 0], waves[slot, mode, 1]
            term[slot, 0] += wr * gr + wi * gi
            term[slot, 1] += wr * gi - wi * gr
            o_r, o_i = window[slot, 1, 0], window[slot, 1, 1]
            back[slot, mode, 0] = (o_r * gr + o_i * gi).astype(bf16)
            back[slot, mode, 1] = (o_r * gi - o_i * gr).astype(bf16)

        spread(1, slot)

    saves = save(1)
    for one in saves:
        one.start()
    grad[...] = jnp.zeros_like(grad)

    @pl.loop(0, used[0])
    def _(slot):
        term[slot] = jnp.zeros(term.shape[1:], jnp.float32)

        @each_mode(modes)
        def _(mode):
            gr, gi = transform(back[slot, mode, 0], back[slot, mode, 1], hop_b[...], hop_f[...])
            wr, wi = probe[mode, 0], probe[mode, 1]
            term[slot, 0] += wr * gr + wi * gi
            term[slot, 1] += wr * gi - wi * gr
            o_r, o_i = window[slot, 0, 0], window[slot, 0, 1]
            grad[mode, first] += o_r * gr + o_i * gi
            grad[mode, second] += o_r * gi - o_i * gr

    grad_save = pltpu.make_async_copy(grad, grad_out, sems_out.at[9])
    grad_save.start()

    @pl.loop(0, used[0])
    def _(slot):
        spread(0, slot)

    last = save(0)
    for one in last:
        one.start()
    for one in saves + last + [light_save, grad_save]:
        one.wait()


def run_slots(rows, cols, boxes, offsets, used, tile, right, lower, corner, probe, measured, *matrices):
    layers, _, height, width = tile.shape
    modes, _, pattern, _ = probe.shape
    slots = offsets.shape[0]
    smem = pl.BlockSpec(memory_space=pltpu.SMEM)
    vmem = pl.BlockSpec(memory_space=pltpu.VMEM)
    anyw = pl.BlockSpec(memory_space=pl.ANY)
    f32, bf16 = jnp.float32, jnp.bfloat16
    space, dma = pltpu.VMEM, pltpu.SemaphoreType.DMA
    ext = (2, height + pattern, width + pattern)
    return pl.pallas_call(
        functools.partial(slots_kernel, rows, cols),
        out_shape=(
            jax.ShapeDtypeStruct(tile.shape, f32),
            jax.ShapeDtypeStruct(right.shape, f32),
            jax.ShapeDtypeStruct(lower.shape, f32),
            jax.ShapeDtypeStruct(corner.shape, f32),
            jax.ShapeDtypeStruct((modes, 2 * pattern, pattern), f32),
            jax.ShapeDtypeStruct((height, width), f32),
        ),
        in_specs=[smem, smem, smem] + [anyw] * 10,
        out_specs=(anyw,) * 6,
        scratch_shapes=[
            space((modes, 2 * pattern, pattern), f32), space((height, width), f32),
            space(ext, f32), space(ext, f32),
            space((slots, layers, 2, pattern, pattern), f32),
            space((slots, modes, 2, pattern, pattern), f32),
            space((modes, 2, pattern, pattern), f32),
            space((slots, modes, 2, pattern, pattern), bf16),
            space((slots, 2, pattern, pattern), f32),
            space((2 * height + pattern, 2 * width + pattern), f32),
            space(probe.shape, f32), space(measured.shape, f32),
            *[space((2 * pattern, 2 * pattern), bf16) for _ in range(4)],
            space((pattern, pattern), f32),
            dma((14,)), dma((10,)),
        ],
        compiler_params=pltpu.CompilerParams(vmem_limit_bytes=58 * 1024 * 1024),
        cost_estimate=pl.CostEstimate(flops=20_000_000_000, bytes_accessed=30_000_000, transcendentals=0),
    )(boxes, offsets, used, tile, right, lower, corner, probe, measured, *matrices)


def share_kernel(
    rows, cols, tile, right, lower, corner, grad_tile, grad, light, probe_in, new_object, new_probe,
    fresh, total, side, inner, left_in, above_in, edge, held, landed, core_in, probe, sems_in, sems_out, sent_halo, got_halo, sent, got,
):
    near = neighbours(rows, cols)
    ways = digits(rows, cols)
    partners = list(near.values())
    for digit in ways.values():
        partners += group(digit)
    layers, pattern = right.shape[0], corner.shape[-1]
    height, width = tile.shape[2], tile.shape[3]
    modes = grad.shape[0]
    each = range(layers)
    first, second = pl.ds(0, pattern), pl.ds(pattern, pattern)
    moves = [(right, side), (tile, fresh), (grad_tile, inner), (probe_in, probe)]
    loads = [pltpu.make_async_copy(a, b, sems_in.at[k]) for k, (a, b) in enumerate(moves)]
    for load in loads:
        load.start()
    greet(partners)
    has_up, up = near["up"]
    has_down, down = near["down"]
    has_left, _ = near["left"]
    has_right, far_right = near["right"]

    def copy(source, target, k, device):
        return pltpu.make_async_remote_copy(
            src_ref=source, dst_ref=target, send_sem=sent_halo.at[k], recv_sem=got_halo.at[k],
            device_id=device, device_id_type=MESH,
        )

    top, rest = pl.ds(0, pattern), pl.ds(pattern, height - pattern)
    tops = [[copy(side.at[n, p, top], left_in.at[n, p, top], 6 * n + p, far_right) for p in (0, 1)] for n in each]
    rests = [copy(side.at[n, :, rest], left_in.at[n, :, rest], 6 * n + 2, far_right) for n in each]
    lowers = [[copy(lower.at[n, p], above_in.at[n, p], 6 * n + 3 + p, down) for p in (0, 1)] for n in each]
    corners = [copy(corner.at[n], edge.at[n], 6 * n + 5, down) for n in each]
    leaves = [pltpu.make_async_copy(fresh.at[n], new_object.at[n], sems_out.at[n]) for n in each]
    outs = [pltpu.make_async_copy(total.at[m], new_probe.at[m], sems_out.at[layers + m]) for m in range(modes)]
    reduction = Reduction(rows, cols, grad, total, held, landed, core_in, (sent, got))

    def add_corner(n):
        @pl.when(jnp.logical_and(has_right, has_up))
        def _():
            corners[n].wait_recv()
            side[n, :, :pattern] = side[n, :, :pattern] + edge[n]

    def release(n, part):
        when([has_right], tops[n][part].start)
        when([has_down], lowers[n][part].start)

    def finish(n):
        @pl.when(has_left)
        def _():
            rests[n].wait_recv()
            tops[n][0].wait_recv()
            tops[n][1].wait_recv()

        @pl.when(jnp.logical_not(has_left))
        def _():
            left_in[n] = jnp.zeros(left_in.shape[1:], jnp.float32)

        @pl.when(has_up)
        def _():
            lowers[n][0].wait_recv()
            lowers[n][1].wait_recv()

        @pl.when(jnp.logical_not(has_up))
        def _():
            above_in[n] = jnp.zeros(above_in.shape[1:], jnp.float32)

        inner[n, :, :, :pattern] += left_in[n]
        inner[n, :, :pattern, :] += above_in[n]
        for part in range(2):
            fresh[n, part] = fresh[n, part] - inner[n, part] / light[...]
        leaves[n].start()

    every = range(len(streams))
    for k in range(reduction.share):
        reduction.core_send(k)
    when([has_down, has_right], corners[0].start)
    loads[0].wait()
    when([has_right], rests[0].start)
    for k in range(reduction.share):
        reduction.core_add(k)
        for s in every:
            if streams[s][0] == k:
                reduction.scatter_send(s, 0)
    when([has_down, has_right], corners[1].start)
    when([has_right], rests[1].start)
    for s in every:
        reduction.scatter_add(s, 0)
        reduction.scatter_send(s, 1)
    add_corner(0)
    release(0, 0)
    for s in every:
        reduction.scatter_add(s, 1)
        reduction.scatter_send(s, 2)
    release(0, 1)
    for s in every:
        reduction.scatter_add(s, 2)
        reduction.gather_send(s, 2)
    add_corner(1)
    for s in every:
        reduction.gather_wait(s, 2)
        reduction.gather_send(s, 1)
    release(1, 0)
    loads[1].wait()
    loads[2].wait()
    for s in every:
        reduction.gather_wait(s, 1)
        reduction.gather_send(s, 0)
    release(1, 1)
    finish(0)
    for s in every:
        reduction.gather_wait(s, 0)
        reduction.core_share(s)
    finish(1)
    mine, theirs, _ = member(ways["core"], 1)

    def squares_of(half):
        squares = jnp.zeros((pattern, pattern), jnp.float32)
        for m in range(reduction.share):
            mode = half * reduction.share + m
            squares = squares + (total[mode, first] * total[mode, first] + total[mode, second] * total[mode, second])
        return squares

    squares = squares_of(mine)
    for s in range(len(streams)):
        for made in reduction.waits[s]:
            made.wait_recv()
    squares = squares + squares_of(theirs)
    for made in reduction.pending:
        made.wait_send()
    loads[3].wait()
    count = modes * 2 * pattern * pattern
    scale = jnp.sqrt(jnp.broadcast_to(jnp.sum(squares), (pattern, pattern)) * (1.0 / count) + 1e-06)
    factor = probe_step / scale
    for mode in range(modes):
        total[mode, first] = probe[mode, 0] - factor * total[mode, first]
        total[mode, second] = probe[mode, 1] - factor * total[mode, second]
        outs[mode].start()
    for n in each:
        when([has_right], rests[n].wait_send)
        when([has_down, has_right], corners[n].wait_send)
        for part in (0, 1):
            when([has_right], tops[n][part].wait_send)
            when([has_down], lowers[n][part].wait_send)
    for one in leaves + outs:
        one.wait()


def run_share(rows, cols, tile, right, lower, corner, grad_tile, grad, light, probe):
    layers = right.shape[0]
    pattern = corner.shape[-1]
    modes = grad.shape[0]
    anyw = pl.BlockSpec(memory_space=pl.ANY)
    vmem = pl.BlockSpec(memory_space=pltpu.VMEM)
    f32, space, dma = jnp.float32, pltpu.VMEM, pltpu.SemaphoreType.DMA
    half = (modes // 2, 2 * pattern, pattern)
    count = modes // 2 + len(streams) * (2 * sum(way[2] - 1 for way in digits(rows, cols).values()) - 1)
    new_object, new_probe = pl.pallas_call(
        functools.partial(share_kernel, rows, cols),
        out_shape=(
            jax.ShapeDtypeStruct(tile.shape, f32),
            jax.ShapeDtypeStruct((modes, 2 * pattern, pattern), f32),
        ),
        in_specs=[anyw, anyw, anyw, anyw, anyw, vmem, vmem, anyw],
        out_specs=(anyw, anyw),
        scratch_shapes=[
            space(tile.shape, f32), space((modes, 2 * pattern, pattern), f32),
            space(right.shape, f32), space(tile.shape, f32), space(right.shape, f32), space(lower.shape, f32),
            space(corner.shape, f32), space(half, f32), space(half, f32), space(half, f32), space(probe.shape, f32),
            dma((4,)), dma((layers + modes,)), dma((6 * layers,)), dma((6 * layers,)), dma((count,)), dma((count,)),
        ],
        compiler_params=pltpu.CompilerParams(
            collective_id=1, has_side_effects=True, vmem_limit_bytes=60 * 1024 * 1024
        ),
        cost_estimate=pl.CostEstimate(flops=0, bytes_accessed=30_000_000, transcendentals=0),
    )(tile, right, lower, corner, grad_tile, grad, light, probe)
    return new_object, new_probe.reshape(probe.shape)


def on_device(object_slab, probe_mode_stack, offsets, measured, counts):
    pattern = probe_mode_stack.shape[-1]
    rows, cols = lax.axis_size("obj"), lax.axis_size("scan")
    info = jnp.concatenate([offsets.reshape(-1), counts])
    info = jnp.pad(info[None], ((0, sublanes - 1), (0, lanes - info.shape[0])))
    right, lower, corner, boxes = run_rims(rows, cols, object_slab, info, pattern)
    grad_tile, right, lower, corner, grad, light = run_slots(
        rows, cols, boxes, offsets, counts, object_slab, right, lower, corner, probe_mode_stack, measured, *tables(pattern)
    )
    return run_share(rows, cols, object_slab, right, lower, corner, grad_tile, grad, light, probe_mode_stack)


def solution(mesh):
    in_specs = (
        P(None, None, "obj", "scan"),
        P(),
        P(("obj", "scan"), None),
        P(("obj", "scan"), None, None),
        P(("obj", "scan")),
    )
    out_specs = (P(None, None, "obj", "scan"), P())
    return jax.shard_map(
        on_device, mesh=mesh, in_specs=in_specs, out_specs=out_specs, check_vma=False
    )
```
